32 devices in a mesh: dp: 8 (over y, x, core), ctx: 4 (over z).
Axes of the slice: x: 2, y: 2, z: 4, core: 2. Of those that a mesh axis runs over, the one named last changes fastest.
Arguments:
- tokens: bfloat16 [8, 512, 1024], P('dp', 'ctx'), may hold values from -6 to 6
- ln1_gain: bfloat16 [2, 1024], P(None, ('dp', 'ctx')), may hold values from 0.25 to 1.75
- ln1_bias: bfloat16 [2, 1024], P(None, ('dp', 'ctx')), may hold values from -2.5 to 2.5
- qkv_weight: bfloat16 [2, 1024, 3072], P(None, ('dp', 'ctx')), may hold values from -0.1875 to 0.1875
- out_weight: bfloat16 [2, 1024, 1024], P(None, ('dp', 'ctx')), may hold values from -0.5 to 0.5
- ln2_gain: bfloat16 [2, 1024], P(None, ('dp', 'ctx')), may hold values from 0.25 to 1.75
- ln2_bias: bfloat16 [2, 1024], P(None, ('dp', 'ctx')), may hold values from -2.5 to 2.5
- in_weight: bfloat16 [2, 1024, 4096], P(None, ('dp', 'ctx')), may hold values from -0.1875 to 0.1875
- fc_weight: bfloat16 [2, 4096, 1024], P(None, ('dp', 'ctx')), may hold values from -0.09375 to 0.09375
- final_gain: bfloat16 [1024], P(('dp', 'ctx')), may hold values from 0.25 to 1.75
- final_bias: bfloat16 [1024], P(('dp', 'ctx')), may hold values from -2.5 to 2.5
- datastore: bfloat16 [131072, 1024], P(('dp', 'ctx')), may hold values from -6 to 6
- neighbour_owner: int32 [8, 512, 16], P('dp', 'ctx'), may hold values from 0 to 31, all different within a row; in each aligned block of 128 rows (0 to 127, 128 to 255, ..., all dimensions but the last counted through in order) at most 128 rows name the same one
- neighbour_row: int32 [8, 512, 16], P('dp', 'ctx'), may hold values from 0 to 4095
- neighbour_count: int32 [8, 512], P('dp', 'ctx'), may hold values from 1 to 16, as said below
- cotangent: bfloat16 [8, 512, 1024], P('dp', 'ctx'), may hold values from -6 to 6
Outputs:
- mixed: float32 [8, 512, 1024], P('dp', 'ctx')
- tokens_grad: float32 [8, 512, 1024], P('dp', 'ctx')
- ln1_gain_grad: float32 [2, 1024], P(None, ('dp', 'ctx'))
- ln1_bias_grad: float32 [2, 1024], P(None, ('dp', 'ctx'))
- qkv_weight_grad: float32 [2, 1024, 3072], P(None, ('dp', 'ctx'))
- out_weight_grad: float32 [2, 1024, 1024], P(None, ('dp', 'ctx'))
- ln2_gain_grad: float32 [2, 1024], P(None, ('dp', 'ctx'))
- ln2_bias_grad: float32 [2, 1024], P(None, ('dp', 'ctx'))
- in_weight_grad: float32 [2, 1024, 4096], P(None, ('dp', 'ctx'))
- fc_weight_grad: float32 [2, 4096, 1024], P(None, ('dp', 'ctx'))
- final_gain_grad: float32 [1024], P(('dp', 'ctx'))
- final_bias_grad: float32 [1024], P(('dp', 'ctx'))
The draws below stay inside these ranges and needn't reach their ends.
Inputs may be any that keep to these rules, and one draw needn't show every extreme that they name: `neighbour_owner`: A row names 16 different owners. In each aligned block of 128 positions of a sequence no owner is named by more than 128 rows, and some block has an owner named by exactly 128. `neighbour_count`: in each aligned block of 128 positions of a sequence some position has 16 live slots.
All inputs are finite; a program needn't handle non-finite values.
Results may differ from the reference program's by a relative error of at most 0.014.
Values may be sent and summed in bfloat16 or wider, within the bound.
A program may use at most 256 MiB of HBM per device.

```python
import math
import jax
import jax.numpy as jnp
import numpy as np
from jax import lax

D = 1024
HEADS = 16
HEAD_DIM = 64
FF = 4096
LAYERS = 2
TOK_SEQ = 128
KMAX = 16
DS_DEV = 4096
SEQS = 8
SEQ_LEN = 512
DS_ALL = 131072
CAP = 128
DEVICES = 32


def draw_neighbour_count(key, part):
    key = jax.random.fold_in(key, 7)
    key_one, key_two, key_four = jax.random.split(key, 3)
    grid_shape = (SEQS, SEQ_LEN)
    factor_one = jax.random.randint(key_one, grid_shape, 0, KMAX)
    factor_two = jax.random.randint(key_two, grid_shape, KMAX // 2, 2 * KMAX)
    tailed = jnp.minimum(KMAX, 1 + factor_one * factor_two // KMAX)
    block_count = SEQ_LEN // TOK_SEQ
    chosen = jax.random.randint(key_four, (SEQS, block_count), 0, TOK_SEQ)
    position = jnp.arange(SEQ_LEN)
    marked = (position % TOK_SEQ)[None, :] == jnp.repeat(chosen, TOK_SEQ, axis=1)
    return jnp.where(marked, KMAX, tailed).astype(jnp.int32)


def touch_ends(array, rng, least, top_value):
    dims = array.shape
    index_at = [jax.random.randint(jax.random.fold_in(rng, axis), (), 0, dims[axis]) for axis in range(len(dims))]
    array = array.at[tuple(index_at)].set(least)
    longest = dims.index(max(dims))
    index_at[longest] = (index_at[longest] + 1) % dims[longest]
    return array.at[tuple(index_at)].set(top_value)


def steps_of(rng, shape, cuts, least, high):
    level, own = 1.0, jax.random.fold_in(rng, 6)
    for axis_at, shards_of in cuts:
        heights = jnp.exp(jax.random.uniform(jax.random.fold_in(own, axis_at), (shards_of,), jnp.float32, least / len(cuts), high / len(cuts)))
        level = level * jnp.repeat(heights, shape[axis_at] // shards_of).reshape([-1 if axis == axis_at else 1 for axis in range(len(shape))])
    return level


def shared_out(own_key, own, number, rows, amount, top, limit, lean):
    ranking = jax.random.permutation(own_key, amount)
    heavy_load, usual = portions_of(amount, rows * top, limit, lean, True), portions_of(amount, rows * top, limit, lean, False)
    places = jnp.arange(amount)

    def named(sizes, rotation):
        used = int((sizes > 0).sum())
        fixed = max(1, used // 4)
        shifted = fixed + (places - fixed + rotation * (used - fixed)) % max(1, amount - fixed)
        return jnp.zeros((amount,), jnp.int32).at[ranking[jnp.where(places < fixed, places, shifted)]].set(jnp.asarray(sizes, jnp.int32))

    sizes = jnp.where(number % 4 == 0, named(heavy_load, number // 4), named(usual, number - number // 4 - 1))
    mixed = jax.random.permutation(jax.random.fold_in(own, 3), amount)
    giver, receiver = mixed[0:amount // 2 * 2:2], mixed[1:amount // 2 * 2:2]
    room = jnp.minimum(sizes[giver] - 1, limit - sizes[receiver]) // 2
    room = jnp.where((giver == ranking[0]) | (receiver == ranking[0]) | (sizes[receiver] == 0), 0, jnp.maximum(room, 0))
    shifted = jax.random.randint(jax.random.fold_in(own, 4), (amount // 2,), 0, 1 << 20) % (room + 1)
    sizes = sizes.at[giver].add(-shifted).at[receiver].add(shifted)
    labels = jnp.searchsorted(jnp.cumsum(sizes), jnp.arange(rows * top), side="right").astype(jnp.int32)
    table = labels.reshape(top, rows).T
    table = table[jax.random.permutation(jax.random.fold_in(own, 1), rows)]
    rotation = jax.random.randint(jax.random.fold_in(own, 2), (rows, 1), 0, top)
    return jnp.take_along_axis(table, (jnp.arange(top)[None, :] + rotation) % top, axis=1)


def portions_of(amount, total, most, skew, full):
    portions = [(1 << 20) // math.isqrt(standing ** skew) + 1 for standing in range(1, amount + 1)]
    largest = most if full else min(most, max(-(-total // amount), total * portions[0] // sum(portions)))
    least = 1 if total - largest >= amount - 1 else 0
    holding, surplus = [largest] + [least] * (amount - 1), total - largest - least * (amount - 1)
    while surplus > 0:
        free = [i for i in range(1, amount) if holding[i] < largest] or [i for i in range(1, amount) if holding[i] < most]
        pool, budget = sum([portions[i] for i in free]), surplus
        for i in free:
            addition = min(most - holding[i], max(1, budget * portions[i] // pool), surplus)
            holding[i] = holding[i] + addition
            surplus = surplus - addition
    return np.array(holding)


def scatter_about(stream_key, dims, scale, reach, cuts=(), kind=jnp.bfloat16):
    array = jax.random.normal(stream_key, dims, jnp.float32) * scale
    if len(cuts) > 0:
        array = steps_of(stream_key, dims, cuts, -0.22, 0.18) * array
    return jnp.clip(array, min=-reach, max=reach).astype(kind)


def setup_inputs(seed: int = 0) -> dict:
    key_of = jax.random.split(jax.random.key(seed), 17)
    tokens = scatter_about(key_of[0], (SEQS, SEQ_LEN, D), 1.0, 6.0, ((0, 8), (1, 4)))
    ln1_gain = jnp.clip(1.0 + 0.15 * jax.random.normal(key_of[1], (LAYERS, D), jnp.float32), 0.25, 1.75).astype(jnp.bfloat16)
    ln1_bias = scatter_about(key_of[2], (LAYERS, D), 0.3, 2.5, ((1, 32),))
    qkv_weight = scatter_about(key_of[3], (LAYERS, D, 3 * D), D ** -0.5, 0.1875, ((1, 32),))
    out_weight = scatter_about(key_of[4], (LAYERS, D, D), (D // 8) ** -0.5, 0.5, ((1, 32),))
    ln2_gain = jnp.clip(1.0 + 0.15 * jax.random.normal(key_of[5], (LAYERS, D), jnp.float32), 0.25, 1.75).astype(jnp.bfloat16)
    ln2_bias = scatter_about(key_of[6], (LAYERS, D), 0.3, 2.5, ((1, 32),))
    in_weight = scatter_about(key_of[7], (LAYERS, D, FF), D ** -0.5, 0.1875, ((1, 32),))
    fc_weight = scatter_about(key_of[8], (LAYERS, FF, D), FF ** -0.5, 0.09375, ((1, 32),))
    final_gain = jnp.clip(1.0 + 0.15 * jax.random.normal(key_of[9], (D,), jnp.float32), 0.25, 1.75).astype(jnp.bfloat16)
    final_bias = scatter_about(key_of[10], (D,), 0.3, 2.5, ((0, 32),))
    datastore = scatter_about(key_of[11], (DS_ALL, D), 1.0, 6.0, ((0, 32),))
    neighbour_owner_keys = jax.random.split(jax.random.fold_in(key_of[12], 1), SEQS * SEQ_LEN // TOK_SEQ)
    neighbour_owner_turns = jax.random.permutation(jax.random.fold_in(key_of[12], 3), SEQS * SEQ_LEN // TOK_SEQ)
    neighbour_owner = jax.vmap(lambda own, number: shared_out(jax.random.fold_in(key_of[12], 2), own, number, TOK_SEQ, DEVICES, KMAX, CAP, 2))(neighbour_owner_keys, neighbour_owner_turns).reshape((SEQS, SEQ_LEN, KMAX))
    neighbour_row = touch_ends(jax.random.randint(key_of[13], (SEQS, SEQ_LEN, KMAX), 0, DS_DEV), jax.random.fold_in(key_of[13], 1), 0, DS_DEV - 1).astype(jnp.int32)
    neighbour_count = draw_neighbour_count(jax.random.fold_in(key_of[16], 71), 0)
    cotangent = scatter_about(key_of[15], (SEQS, SEQ_LEN, D), 1.0, 6.0, ((0, 8), (1, 4)))
    return {"tokens": tokens, "ln1_gain": ln1_gain, "ln1_bias": ln1_bias, "qkv_weight": qkv_weight, "out_weight": out_weight, "ln2_gain": ln2_gain, "ln2_bias": ln2_bias, "in_weight": in_weight, "fc_weight": fc_weight, "final_gain": final_gain, "final_bias": final_bias, "datastore": datastore, "neighbour_owner": neighbour_owner, "neighbour_row": neighbour_row, "neighbour_count": neighbour_count, "cotangent": cotangent}


EPSILON = 1e-05
FLOOR = -1e+30
RECALL_SHARE = 0.25
DISTANCE_SCALE = 1.5

@jax.custom_vjp
def low(v):
    return lax.optimization_barrier(v.astype(jnp.bfloat16)).astype(jnp.float32)

@jax.custom_vjp
def low_back(v):
    return v

def low_keep(v):
    return (low(v), None)

def low_pass(kept, grad):
    return (grad,)

def back_keep(v):
    return (v, None)

def back_low(kept, grad):
    return (low(grad),)
low.defvjp(low_keep, low_pass)
low_back.defvjp(back_keep, back_low)

def layer_norm(values, gains, shifts):
    average = lax.optimization_barrier(jnp.mean(values, axis=-1, keepdims=True))
    centered = values - average
    variance = lax.optimization_barrier(jnp.mean(centered * centered, axis=-1, keepdims=True))
    return centered * lax.rsqrt(variance + EPSILON) * gains + shifts

def recall_head(hidden, gains, shifts, neighbours, usable):
    query = layer_norm(hidden, gains, shifts)
    stored = neighbours.astype(jnp.float32)
    offset = query[:, None, :] - stored
    distance = lax.optimization_barrier(jnp.sum(offset * offset, axis=-1))
    scaled = jnp.where(usable, -distance / (DISTANCE_SCALE * math.sqrt(query.shape[-1])), FLOOR)
    highest = lax.optimization_barrier(jnp.max(scaled, axis=-1, keepdims=True))
    raised = jnp.exp(scaled - highest)
    weights = raised / lax.optimization_barrier(jnp.sum(raised, axis=-1, keepdims=True))
    recalled = lax.optimization_barrier(jnp.sum(weights[:, :, None] * stored, axis=1))
    return (1.0 - RECALL_SHARE) * query + RECALL_SHARE * recalled

def matmul(left, right):
    return jnp.dot(left, right, precision=lax.Precision.HIGHEST, preferred_element_type=jnp.float32)

def attention(packed):
    queries = packed[:, :D].reshape(SEQ_LEN, HEADS, HEAD_DIM)
    keys = packed[:, D:2 * D].reshape(SEQ_LEN, HEADS, HEAD_DIM)
    values = packed[:, 2 * D:].reshape(SEQ_LEN, HEADS, HEAD_DIM)
    block_rows = math.gcd(512, SEQ_LEN)
    block_count = SEQ_LEN // block_rows

    def one_block(query_block, start_row):
        scores = jnp.einsum('qhd,khd->hqk', query_block, keys, precision=lax.Precision.HIGHEST) * HEAD_DIM ** (-0.5)
        scores = low_back(scores)
        query_at = start_row + jnp.arange(block_rows, dtype=jnp.int32)
        key_at = jnp.arange(SEQ_LEN, dtype=jnp.int32)
        allowed = query_at[:, None] >= key_at[None, :]
        scores = jnp.where(allowed[None], scores, FLOOR)
        highest = lax.optimization_barrier(jnp.max(scores, axis=-1, keepdims=True))
        raised = jnp.exp(scores - highest)
        probs = low(raised / lax.optimization_barrier(jnp.sum(raised, axis=-1, keepdims=True)))
        return jnp.einsum('hqk,khd->qhd', probs, values, precision=lax.Precision.HIGHEST)
    checked = jax.checkpoint(one_block)
    outputs = lax.map(lambda pair_item: checked(pair_item[0], pair_item[1]), (queries.reshape(block_count, block_rows, HEADS, HEAD_DIM), jnp.arange(block_count, dtype=jnp.int32) * block_rows))
    return outputs.reshape(SEQ_LEN, D)

def block(hidden, gain_one, shift_one, joint, project, gain_two, shift_two, expand, shrink):
    normed = low(layer_norm(hidden, gain_one, shift_one))
    packed = low(low_back(matmul(normed, joint)))
    attended = low(low_back(attention(packed)))
    middle = hidden + low_back(matmul(attended, project))
    normed_two = low(layer_norm(middle, gain_two, shift_two))
    inner = low_back(matmul(normed_two, expand))
    active = low(jax.nn.gelu(inner, approximate=True))
    return middle + low_back(matmul(active, shrink))

def reference(tokens, ln1_gain, ln1_bias, qkv_weight, out_weight, ln2_gain, ln2_bias, in_weight, fc_weight, final_gain, final_bias, datastore, neighbour_owner, neighbour_row, neighbour_count, cotangent):
    floats = [array_in.astype(jnp.float32) for array_in in (tokens, ln1_gain, ln1_bias, qkv_weight, out_weight, ln2_gain, ln2_bias, in_weight, fc_weight, final_gain, final_bias)]

    def forward(token_values, gain_one, shift_one, joint, project, gain_two, shift_two, expand, shrink, head_gain, head_shift):

        def one_sequence(sequence_item):
            values_in, owners, rows_in, counts = sequence_item
            hidden = values_in
            for layer_index in range(LAYERS):
                hidden = block(hidden, gain_one[layer_index], shift_one[layer_index], joint[layer_index], project[layer_index], gain_two[layer_index], shift_two[layer_index], expand[layer_index], shrink[layer_index])
            flat_index = (owners * DS_DEV + rows_in).reshape(-1).astype(jnp.int32)
            picked = jnp.take(datastore, flat_index, axis=0).reshape(SEQ_LEN, KMAX, D)
            usable = jnp.arange(KMAX, dtype=jnp.int32)[None, :] < counts[:, None]
            return recall_head(hidden, head_gain, head_shift, picked, usable)
        return lax.map(jax.checkpoint(one_sequence), (token_values, neighbour_owner, neighbour_row, neighbour_count))
    mixed, pullback = jax.vjp(forward, *floats)
    grads = pullback(cotangent.astype(jnp.float32))
    return (mixed, grads[0], grads[1], grads[2], grads[3], grads[4], grads[5], grads[6], grads[7], grads[8], grads[9], grads[10])
```

```python
import functools
import math

import jax
import jax.numpy as jnp
from jax import lax
from jax.experimental import pallas as pl
from jax.experimental.pallas import tpu as pltpu
from jax.sharding import PartitionSpec as P

HEADS = 16
LAYERS = 2

EPSILON = 1e-05
FLOOR = -1e30
RECALL_SHARE = 0.25
DISTANCE_SCALE = 1.5

MESH = pl.DeviceIdType.MESH
VMEM = pltpu.VMEM
BF16 = jnp.bfloat16
F32 = jnp.float32


def norm_parts(values):
    average = jnp.mean(values, axis=-1, keepdims=True)
    centered = values - average
    variance = jnp.mean(centered * centered, axis=-1, keepdims=True)
    inverse = lax.rsqrt(variance + EPSILON)
    return centered * inverse, inverse


def norm_backward(grad, unit, inverse, gains):
    scaled = grad * gains
    return inverse * (
        scaled
        - jnp.mean(scaled, axis=-1, keepdims=True)
        - unit * jnp.mean(scaled * unit, axis=-1, keepdims=True)
    )


def plane_kernel(count, reduce, mode, gather, *refs):
    refs = list(refs)
    half = count // 2
    partial_ref = refs.pop(0) if reduce else None
    base_ref = refs.pop(0)
    if mode in ("norm", "back"):
        gain_ref = refs.pop(0)
    if mode == "norm":
        shift_ref = refs.pop(0)
    if mode == "back":
        saved_ref = refs.pop(0)
    full_ref = refs.pop(0) if gather else None
    new_ref = refs.pop(0) if reduce else None
    stat_ref = refs.pop(0) if mode == "back" else None
    if reduce:
        side_ref, out_ref, in_ref = refs.pop(0), refs.pop(0), refs.pop(0)
        side_send, side_recv, far_send, far_recv = (refs.pop(0) for _ in range(4))
    if gather:
        gather_send, gather_recv, pass_send, pass_recv = (refs.pop(0) for _ in range(4))

    me = lax.axis_index("dp")
    plane = lax.axis_index("ctx")
    chip, core = me // 2, me % 2
    sibling = 2 * chip + (1 - core)
    others = [(2 * ((chip + j) % half) + core, (chip + j) % half) for j in range(1, half)]
    sources = [2 * ((chip + half - j) % half) + core for j in range(1, half)]

    barrier = pltpu.get_barrier_semaphore()
    for target in [sibling] + [other for other, _ in others]:
        pl.semaphore_signal(barrier, inc=1, device_id=(target, plane), device_id_type=MESH)
    pl.semaphore_wait(barrier, half)

    if reduce:
        side = []
        for j in range(half):
            where = (chip + j + 1) % half
            copy = pltpu.make_async_remote_copy(
                src_ref=partial_ref.at[2 * where + (1 - core)],
                dst_ref=side_ref.at[j],
                send_sem=side_send.at[j],
                recv_sem=side_recv.at[j],
                device_id=(sibling, plane),
                device_id_type=MESH,
            )
            copy.start()
            side.append(copy)
        far = []
        for j in range(1, half):
            target, where = others[j - 1]
            side[j - 1].wait_recv()
            out_ref[j - 1] = (
                partial_ref[2 * where + core].astype(F32) + side_ref[j - 1].astype(F32)
            ).astype(BF16)
            copy = pltpu.make_async_remote_copy(
                src_ref=out_ref.at[j - 1],
                dst_ref=in_ref.at[j - 1],
                send_sem=far_send.at[j - 1],
                recv_sem=far_recv.at[j - 1],
                device_id=(target, plane),
                device_id_type=MESH,
            )
            copy.start()
            far.append(copy)
        side[half - 1].wait_recv()
        total = partial_ref[me].astype(F32) + side_ref[half - 1].astype(F32)
        for j in range(1, half):
            far[j - 1].wait_recv()
            total = total + in_ref[j - 1].astype(F32)
    if mode == "norm":
        value = base_ref[...].astype(F32)
        if reduce:
            value = value + total
            new_ref[...] = value
        unit, _ = norm_parts(value)
        result = unit * gain_ref[...] + shift_ref[...]
    elif mode == "back":
        unit, inverse = norm_parts(saved_ref[...].astype(F32))
        stat_ref[0:1, :] = jnp.sum(total * unit, axis=0, keepdims=True)
        stat_ref[1:2, :] = jnp.sum(total, axis=0, keepdims=True)
        result = base_ref[...] + norm_backward(total, unit, inverse, gain_ref[...])
        new_ref[...] = result
    else:
        result = base_ref[...].astype(F32)
        if reduce:
            result = result + total
            new_ref[...] = result

    if gather:
        full_ref[me] = result.astype(BF16)
        sends = []
        for j, target in enumerate([sibling] + [other for other, _ in others]):
            copy = pltpu.make_async_remote_copy(
                src_ref=full_ref.at[me],
                dst_ref=full_ref.at[me],
                send_sem=gather_send.at[j],
                recv_sem=gather_recv.at[j],
                device_id=(target, plane),
                device_id_type=MESH,
            )
            copy.start()
            sends.append(copy)
        passes = []
        for j in range(1, half):
            sends[j].wait_recv()
            copy = pltpu.make_async_remote_copy(
                src_ref=full_ref.at[sources[j - 1]],
                dst_ref=full_ref.at[sources[j - 1]],
                send_sem=pass_send.at[j - 1],
                recv_sem=pass_recv.at[j - 1],
                device_id=(sibling, plane),
                device_id_type=MESH,
            )
            copy.start()
            passes.append(copy)
        sends[0].wait_recv()
        for copy in passes:
            copy.wait_recv()
        for copy in sends + passes:
            copy.wait_send()
    if reduce:
        for copy in side + far:
            copy.wait_send()


def plane_exchange(count, call_id, partial, base, gains=None, shifts=None, saved=None, gather=True):
    reduce = partial is not None
    mode = "plain" if gains is None else ("back" if saved is not None else "norm")
    rows, width = base.shape
    half = count // 2
    operands = [partial] if reduce else []
    operands.append(base)
    if gains is not None:
        operands.append(gains.reshape(1, width))
    if mode == "norm":
        operands.append(shifts.reshape(1, width))
    if mode == "back":
        operands.append(saved)
    outs, scratch = [], []
    if gather:
        outs.append(jax.ShapeDtypeStruct((count, rows, width), BF16))
    if reduce:
        outs.append(jax.ShapeDtypeStruct((rows, width), F32))
    if mode == "back":
        outs.append(jax.ShapeDtypeStruct((8, width), F32))
    dma = pltpu.SemaphoreType.DMA
    if reduce:
        scratch += [
            VMEM((half, rows, width), BF16),
            VMEM((half - 1, rows, width), BF16),
            VMEM((half - 1, rows, width), BF16),
            dma((half,)),
            dma((half,)),
            dma((half - 1,)),
            dma((half - 1,)),
        ]
    if gather:
        scratch += [dma((half,)), dma((half,)), dma((half - 1,)), dma((half - 1,))]
    spec = pl.BlockSpec(memory_space=VMEM)
    return pl.pallas_call(
        functools.partial(plane_kernel, count, reduce, mode, gather),
        out_shape=tuple(outs),
        in_specs=[spec] * len(operands),
        out_specs=tuple([spec] * len(outs)),
        scratch_shapes=scratch,
        compiler_params=pltpu.CompilerParams(
            collective_id=call_id, has_side_effects=True, vmem_limit_bytes=40 * 1024 * 1024
        ),
    )(*operands)


def swap_kernel(devices, ring, x_ref, o_ref, own_sem, send_sem, recv_sem):
    me = lax.axis_index("dp") * ring + lax.axis_index("ctx")
    barrier = pltpu.get_barrier_semaphore()

    def greet(j, carry):
        target = (me + j) % devices
        pl.semaphore_signal(
            barrier, inc=1, device_id=(target // ring, target % ring), device_id_type=MESH
        )
        return carry

    lax.fori_loop(1, devices, greet, 0)
    pl.semaphore_wait(barrier, devices - 1)
    own = pltpu.make_async_copy(x_ref.at[me], o_ref.at[me], own_sem)
    own.start()

    def copy_of(j):
        target = (me + j) % devices
        return pltpu.make_async_remote_copy(
            src_ref=x_ref.at[target],
            dst_ref=o_ref.at[me],
            send_sem=send_sem.at[j],
            recv_sem=recv_sem.at[j],
            device_id=(target // ring, target % ring),
            device_id_type=MESH,
        )

    def begin(j, carry):
        copy_of(j).start()
        return carry

    def finish(j, carry):
        copy_of(j).wait()
        return carry

    lax.fori_loop(1, devices, begin, 0)
    lax.fori_loop(1, devices, finish, 0)
    own.wait()


def swap_all(x, ring, call_id):
    devices = x.shape[0]
    dma = pltpu.SemaphoreType.DMA
    spec = pl.BlockSpec(memory_space=VMEM)
    return pl.pallas_call(
        functools.partial(swap_kernel, devices, ring),
        out_shape=jax.ShapeDtypeStruct(x.shape, x.dtype),
        in_specs=[spec],
        out_specs=spec,
        scratch_shapes=[dma, dma((devices,)), dma((devices,))],
        compiler_params=pltpu.CompilerParams(collective_id=call_id, has_side_effects=True),
    )(x)


def dot(left, right):
    return jnp.dot(left, right, preferred_element_type=F32)


def contract_rows(left, right):
    return lax.dot_general(left, right, (((0,), (0,)), ((), ())), preferred_element_type=F32)


def contract_cols(left, right):
    return lax.dot_general(left, right, (((1,), (1,)), ((), ())), preferred_element_type=F32)


def split_heads(flat, seqs, heads):
    return flat.reshape(seqs, flat.shape[0] // seqs, heads, -1)


def attend(packed, seqs, heads):
    width = packed.shape[1] // 3
    queries, keys, values = (
        split_heads(packed[:, i * width : (i + 1) * width], seqs, heads) for i in range(3)
    )
    scale = queries.shape[-1] ** (-0.5)
    scores = jnp.einsum("sqhd,skhd->shqk", queries, keys, preferred_element_type=F32) * scale
    at = jnp.arange(queries.shape[1])
    allowed = at[:, None] >= at[None, :]
    scores = jnp.where(allowed, scores, FLOOR)
    highest = jnp.max(scores, axis=-1, keepdims=True)
    raised = jnp.exp(scores - highest)
    probs = raised / jnp.sum(raised, axis=-1, keepdims=True)
    output = jnp.einsum("shqk,skhd->sqhd", probs.astype(BF16), values, preferred_element_type=F32)
    return probs, output.reshape(packed.shape[0], width).astype(BF16)


def attend_backward(packed, probs, grad_flat, seqs, heads):
    width = packed.shape[1] // 3
    queries, keys, values = (
        split_heads(packed[:, i * width : (i + 1) * width], seqs, heads) for i in range(3)
    )
    grad = split_heads(grad_flat, seqs, heads)
    scale = queries.shape[-1] ** (-0.5)
    grad_probs = jnp.einsum("sqhd,skhd->shqk", grad, values, preferred_element_type=F32)
    delta = jnp.sum(probs * grad_probs, axis=-1, keepdims=True)
    grad_scores = (probs * (grad_probs - delta)).astype(BF16)
    parts = (
        jnp.einsum("shqk,skhd->sqhd", grad_scores, keys, preferred_element_type=F32) * scale,
        jnp.einsum("shqk,sqhd->skhd", grad_scores, queries, preferred_element_type=F32) * scale,
        jnp.einsum("shqk,sqhd->skhd", probs.astype(BF16), grad, preferred_element_type=F32),
    )
    return jnp.concatenate(
        [part.reshape(packed.shape[0], width).astype(BF16) for part in parts], axis=1
    )


def smooth_gate(values):
    return jax.nn.gelu(values, approximate=True)


def recall(hidden, gains, shifts, stored, usable, cotangent):
    unit, inverse = norm_parts(hidden)
    query = unit * gains + shifts
    scale = DISTANCE_SCALE * math.sqrt(query.shape[-1])
    rows = stored.astype(F32)
    offset = query[None] - rows
    distance = jnp.sum(offset * offset, axis=-1)
    pull = RECALL_SHARE * jnp.sum(cotangent[None] * rows, axis=-1)
    scaled = jnp.where(usable, -distance / scale, FLOOR)
    raised = jnp.where(usable, jnp.exp(scaled - jnp.max(scaled, axis=0, keepdims=True)), 0.0)
    weights = raised / jnp.sum(raised, axis=0, keepdims=True)
    recalled = jnp.sum(jnp.where(usable[..., None], weights[..., None] * rows, 0.0), axis=0)
    mixed = (1.0 - RECALL_SHARE) * query + RECALL_SHARE * recalled
    grad_scaled = weights * (pull - jnp.sum(weights * pull, axis=0, keepdims=True))
    moved = jnp.sum(jnp.where(usable[..., None], grad_scaled[..., None] * rows, 0.0), axis=0)
    moved = moved - jnp.sum(grad_scaled, axis=0)[:, None] * query
    grad_query = (1.0 - RECALL_SHARE) * cotangent + moved * (2.0 / scale)
    sums = jnp.stack([jnp.sum(grad_query * unit, axis=0), jnp.sum(grad_query, axis=0)])
    return mixed, norm_backward(grad_query, unit, inverse, gains), sums


def shards(
    tokens,
    ln1_gain,
    ln1_bias,
    qkv_weight,
    out_weight,
    ln2_gain,
    ln2_bias,
    in_weight,
    fc_weight,
    final_gain,
    final_bias,
    datastore,
    neighbour_owner,
    neighbour_row,
    neighbour_count,
    cotangent,
):
    local_seqs, local_rows, width = tokens.shape
    rows = local_seqs * local_rows
    count, ring = lax.axis_size("dp"), lax.axis_size("ctx")
    devices = count * ring
    both = ("dp", "ctx")
    seqs = count * local_seqs // ring
    heads = HEADS // count
    slots = neighbour_owner.shape[2]
    part = width // devices
    head_width = width // count
    inner_width = in_weight.shape[2] // count

    forth = []
    for s in range(count):
        for p in range(ring):
            forth.append((s * ring + p, ((s % seqs) * ring + p) * ring + s // seqs))
    back = [(there, here) for here, there in forth]
    my_tokens = lax.ppermute(tokens.reshape(rows, width), both, forth)
    my_cotangent = lax.ppermute(cotangent.reshape(rows, width), both, forth)
    wanted = jnp.concatenate(
        [
            neighbour_owner.reshape(rows, slots),
            neighbour_row.reshape(rows, slots),
            neighbour_count.reshape(rows, 1),
        ],
        axis=1,
    )
    wanted = lax.ppermute(wanted, both, forth)
    owners, picks, live = wanted[:, :slots], wanted[:, slots : 2 * slots], wanted[:, 2 * slots :]

    small = jnp.stack(
        [ln1_gain[0], ln1_gain[1], ln1_bias[0], ln1_bias[1], ln2_gain[0], ln2_gain[1]]
        + [ln2_bias[0], ln2_bias[1], final_gain, final_bias]
    ).astype(F32)
    small = jnp.pad(small, ((0, 6), (0, 128 - part)))
    everyone = swap_all(jnp.broadcast_to(small[None], (devices, 16, 128)), ring, 0)
    vectors = jnp.transpose(everyone[:, :10, :part], (1, 0, 2)).reshape(10, width)
    gain_one, shift_one = vectors[0:2], vectors[2:4]
    gain_two, shift_two = vectors[4:6], vectors[6:8]
    head_gain, head_shift = vectors[8], vectors[9]

    columns = jnp.concatenate(
        [
            qkv_weight.reshape(LAYERS, part, 3, count, head_width)
            .transpose(3, 0, 1, 2, 4)
            .reshape(count, LAYERS, part, 3 * head_width),
            in_weight.reshape(LAYERS, part, count, inner_width).transpose(2, 0, 1, 3),
        ],
        axis=-1,
    )
    columns = lax.all_to_all(columns, "dp", split_axis=0, concat_axis=0, tiled=True)
    joint, project, expand, shrink = [], [], [], []
    for layer in range(LAYERS):
        wide = lax.all_gather(columns[:, layer], "ctx", axis=0, tiled=False)
        wide = wide.transpose(1, 0, 2, 3).reshape(width, -1)
        joint.append(wide[:, : 3 * head_width])
        expand.append(wide[:, 3 * head_width :])
        tall = lax.all_gather(
            jnp.concatenate([out_weight[layer], fc_weight[layer]], axis=0),
            "ctx",
            axis=0,
            tiled=False,
        )
        project.append(tall[:, :part].reshape(-1, width))
        shrink.append(tall[:, part:].reshape(-1, width))

    hits = (owners[:, :, None] == jnp.arange(devices)[None, None, :]) & (
        jnp.arange(slots)[None, :, None] < live[:, :, None]
    )
    asked = jnp.sum(jnp.where(hits, picks[:, :, None], 0), axis=1).T
    usable = jnp.any(hits, axis=1).T
    asked = lax.all_to_all(asked, both, split_axis=0, concat_axis=0, tiled=True)
    served = jnp.take(datastore, asked.reshape(-1), axis=0).reshape(devices, rows, width)
    stored = lax.all_to_all(served, both, split_axis=0, concat_axis=0, tiled=True)

    exchange = functools.partial(plane_exchange, count)
    (normed,) = exchange(1, None, my_tokens, gain_one[0], shift_one[0])
    hidden = my_tokens.astype(F32)
    saved = []
    for layer in range(LAYERS):
        normed = normed.reshape(count * rows, width)
        packed = dot(normed, joint[layer]).astype(BF16)
        probs, attended = attend(packed, seqs, heads)
        partial = dot(attended, project[layer]).astype(BF16).reshape(count, rows, width)
        normed_two, middle = exchange(2, partial, hidden, gain_two[layer], shift_two[layer])
        normed_two = normed_two.reshape(count * rows, width)
        inner = dot(normed_two, expand[layer])
        active = smooth_gate(inner).astype(BF16)
        partial = dot(active, shrink[layer]).astype(BF16).reshape(count, rows, width)
        saved.append((hidden, normed, packed, probs, attended, middle, normed_two, inner, active))
        if layer + 1 < LAYERS:
            normed, hidden = exchange(
                2, partial, middle, gain_one[layer + 1], shift_one[layer + 1]
            )
        else:
            (hidden,) = exchange(3, partial, middle, gather=False)

    mixed, grad_hidden, head_sums = recall(
        hidden, head_gain, head_shift, stored, usable, my_cotangent.astype(F32)
    )
    mixed = lax.ppermute(mixed, both, back)

    (branch,) = exchange(4, None, grad_hidden)
    sums_one, sums_two = [None] * LAYERS, [None] * LAYERS
    grad_wide, grad_tall = [None] * LAYERS, [None] * LAYERS
    for layer in reversed(range(LAYERS)):
        start, normed, packed, probs, attended, middle, normed_two, inner, active = saved[layer]
        branch = branch.reshape(count * rows, width)
        grad_shrink = contract_rows(active, branch).astype(BF16)
        grad_active = contract_cols(branch, shrink[layer])
        _, gate_back = jax.vjp(smooth_gate, inner)
        grad_inner = gate_back(grad_active)[0].astype(BF16)
        grad_expand = contract_rows(normed_two, grad_inner).astype(BF16)
        partial = contract_cols(grad_inner, expand[layer]).astype(BF16)
        grad_out, grad_middle, sums_two[layer] = exchange(
            5, partial.reshape(count, rows, width), grad_hidden, gain_two[layer], saved=middle
        )
        grad_out = grad_out.reshape(count * rows, width)
        grad_project = contract_rows(attended, grad_out).astype(BF16)
        grad_attended = contract_cols(grad_out, project[layer]).astype(BF16)
        grad_packed = attend_backward(packed, probs, grad_attended, seqs, heads)
        grad_joint = contract_rows(normed, grad_packed).astype(BF16)
        partial = contract_cols(grad_packed, joint[layer]).astype(BF16)
        partial = partial.reshape(count, rows, width)
        if layer > 0:
            branch, grad_hidden, sums_one[layer] = exchange(
                5, partial, grad_middle, gain_one[layer], saved=start
            )
        else:
            grad_hidden, sums_one[layer] = exchange(
                6, partial, grad_middle, gain_one[layer], saved=start, gather=False
            )
        wide = jnp.concatenate([grad_joint, grad_expand], axis=1)
        wide = wide.reshape(count, ring, part, -1).transpose(1, 0, 2, 3)
        grad_wide[layer] = lax.psum_scatter(wide, "ctx", scatter_dimension=0, tiled=False)
        tall = jnp.concatenate(
            [grad_project.reshape(ring, part, width), grad_shrink.reshape(ring, -1, width)], axis=1
        )
        grad_tall[layer] = lax.psum_scatter(tall, "ctx", scatter_dimension=0, tiled=False)

    tokens_grad = lax.ppermute(grad_hidden, both, back)
    wide = lax.all_to_all(
        jnp.stack(grad_wide, axis=1), "dp", split_axis=0, concat_axis=0, tiled=True
    ).astype(F32)
    qkv_grad = (
        wide[..., : 3 * head_width]
        .reshape(count, LAYERS, part, 3, head_width)
        .transpose(1, 2, 3, 0, 4)
        .reshape(LAYERS, part, 3 * width)
    )
    in_grad = wide[..., 3 * head_width :].transpose(1, 2, 0, 3).reshape(LAYERS, part, -1)
    tall = jnp.stack(grad_tall).astype(F32)

    sums = jnp.concatenate(
        [sums_one[0][:2], sums_one[1][:2], sums_two[0][:2], sums_two[1][:2], head_sums]
    )
    sums = jnp.pad(sums, ((0, 6), (0, 0))).reshape(16, devices, part).transpose(1, 0, 2)
    sums = jnp.pad(sums, ((0, 0), (0, 0), (0, 128 - part)))
    sums = jnp.sum(swap_all(sums, ring, 7), axis=0)[:, :part]

    return (
        mixed.reshape(local_seqs, local_rows, width),
        tokens_grad.reshape(local_seqs, local_rows, width),
        jnp.stack([sums[0], sums[2]]),
        jnp.stack([sums[1], sums[3]]),
        qkv_grad,
        tall[:, :part],
        jnp.stack([sums[4], sums[6]]),
        jnp.stack([sums[5], sums[7]]),
        in_grad,
        tall[:, part:],
        sums[8],
        sums[9],
    )


def solution(mesh):
    both = ("dp", "ctx")
    return jax.shard_map(
        shards,
        mesh=mesh,
        in_specs=(
            P("dp", "ctx", None),
            P(None, both),
            P(None, both),
            P(None, both, None),
            P(None, both, None),
            P(None, both),
            P(None, both),
            P(None, both, None),
            P(None, both, None),
            P(both),
            P(both),
            P(both, None),
            P("dp", "ctx", None),
            P("dp", "ctx", None),
            P("dp", "ctx"),
            P("dp", "ctx", None),
        ),
        out_specs=(
            P("dp", "ctx", None),
            P("dp", "ctx", None),
            P(None, both),
            P(None, both),
            P(None, both, None),
            P(None, both, None),
            P(None, both),
            P(None, both),
            P(None, both, None),
            P(None, both, None),
            P(both),
            P(both),
        ),
        check_vma=False,
    )
```

```python
import functools
import math

import jax
import jax.numpy as jnp
from jax import lax
from jax.experimental import pallas as pl
from jax.experimental.pallas import tpu as pltpu
from jax.sharding import PartitionSpec as P

HEADS = 16
LAYERS = 2

EPSILON = 1e-05
FLOOR = -1e30
RECALL_SHARE = 0.25
DISTANCE_SCALE = 1.5

MESH = pl.DeviceIdType.MESH
VMEM = pltpu.VMEM
BF16 = jnp.bfloat16
F32 = jnp.float32


def norm_parts(values):
    average = jnp.mean(values, axis=-1, keepdims=True)
    centered = values - average
    variance = jnp.mean(centered * centered, axis=-1, keepdims=True)
    inverse = lax.rsqrt(variance + EPSILON)
    return centered * inverse, inverse


def norm_backward(grad, unit, inverse, gains):
    scaled = grad * gains
    return inverse * (
        scaled
        - jnp.mean(scaled, axis=-1, keepdims=True)
        - unit * jnp.mean(scaled * unit, axis=-1, keepdims=True)
    )


def send(source, target, send_sem, recv_sem, where):
    copy = pltpu.make_async_remote_copy(
        src_ref=source,
        dst_ref=target,
        send_sem=send_sem,
        recv_sem=recv_sem,
        device_id=where,
        device_id_type=MESH,
    )
    copy.start()
    return copy


def greet_all(targets):
    barrier = pltpu.get_barrier_semaphore()
    for target in targets:
        pl.semaphore_signal(barrier, inc=1, device_id=target, device_id_type=MESH)
    pl.semaphore_wait(barrier, len(targets))


def gather_begin(count, me, plane, full_ref, send_sem, recv_sem):
    half = count // 2
    chip, core = me // 2, me % 2
    targets = [2 * chip + (1 - core)]
    targets += [2 * ((chip + j) % half) + core for j in range(1, half)]
    return [
        send(full_ref.at[me], full_ref.at[me], send_sem.at[j], recv_sem.at[j], (target, plane))
        for j, target in enumerate(targets)
    ]


def gather_end(count, me, plane, full_ref, sends, send_sem, recv_sem):
    half = count // 2
    chip, core = me // 2, me % 2
    sibling = 2 * chip + (1 - core)
    passes = []
    for j in range(1, half):
        block = full_ref.at[2 * ((chip + half - j) % half) + core]
        sends[j].wait_recv()
        passes.append(
            send(block, block, send_sem.at[j - 1], recv_sem.at[j - 1], (sibling, plane))
        )
    sends[0].wait_recv()
    for copy in passes:
        copy.wait_recv()
    return sends + passes


def plane_kernel(count, ring, reduce, mode, gather, kinds, *refs):
    refs = list(refs)
    half = count // 2
    partial_ref = refs.pop(0) if reduce else None
    base_ref = refs.pop(0) if mode != "none" else None
    gain_ref = refs.pop(0) if mode in ("norm", "back") else None
    shift_ref = refs.pop(0) if mode == "norm" else None
    saved_ref = refs.pop(0) if mode == "back" else None
    ride_refs = [refs.pop(0) for _ in kinds]
    full_ref = refs.pop(0) if gather else None
    new_ref = refs.pop(0) if reduce else None
    stat_ref = refs.pop(0) if mode == "back" else None
    ride_outs = [refs.pop(0) for _ in kinds]
    if reduce:
        side_ref, out_ref, in_ref = refs.pop(0), refs.pop(0), refs.pop(0)
        side_send, side_recv, far_send, far_recv = (refs.pop(0) for _ in range(4))
    if gather:
        gather_send, gather_recv, pass_send, pass_recv = (refs.pop(0) for _ in range(4))
    land_refs = [refs.pop(0) if kind in ("sum0", "sum1") else None for kind in kinds]
    if kinds:
        ride_send, ride_recv, ride_own = refs.pop(0), refs.pop(0), refs.pop(0)

    me = lax.axis_index("dp")
    plane = lax.axis_index("ctx")
    chip, core = me // 2, me % 2
    sibling = 2 * chip + (1 - core)
    others = [(2 * ((chip + j) % half) + core, (chip + j) % half) for j in range(1, half)]

    greet = []
    if "mix" in kinds:
        greet += [((me + k) % count, plane) for k in range(1, count)]
    elif reduce or gather:
        greet += [(sibling, plane)] + [(other, plane) for other, _ in others]
    if kinds:
        greet += [(me, (plane + j) % ring) for j in range(1, ring)]
    greet_all(greet)
    pending = []
    rides, stays = [], []
    for i, kind in enumerate(kinds):
        for k in range(1, count) if kind == "mix" else ():
            there = (me + k) % count
            rides.append(
                send(
                    ride_refs[i].at[there],
                    ride_outs[i].at[me],
                    ride_send.at[i, k - 1],
                    ride_recv.at[i, k - 1],
                    (there, plane),
                )
            )
        for j in range(1, ring) if kind != "mix" else ():
            there = (plane + j) % ring
            if kind == "sum0":
                source, target = ride_refs[i].at[there], land_refs[i].at[j - 1]
            elif kind == "sum1":
                source, target = ride_refs[i].at[:, there], land_refs[i].at[j - 1]
            elif kind == "get0":
                source, target = ride_refs[i], ride_outs[i].at[plane]
            elif kind == "hop":
                source, target = ride_refs[i].at[there], ride_outs[i].at[plane]
            else:
                source, target = ride_refs[i], ride_outs[i].at[:, plane]
            rides.append(
                send(source, target, ride_send.at[i, j - 1], ride_recv.at[i, j - 1], (me, there))
            )
        if kind not in ("sum0", "sum1"):
            if kind == "mix":
                source, target = ride_refs[i].at[me], ride_outs[i].at[me]
            elif kind == "hop":
                source, target = ride_refs[i].at[plane], ride_outs[i].at[plane]
            elif kind == "get0":
                source, target = ride_refs[i], ride_outs[i].at[plane]
            else:
                source, target = ride_refs[i], ride_outs[i].at[:, plane]
            stay = pltpu.make_async_copy(source, target, ride_own.at[i])
            stay.start()
            stays.append(stay)
    pending += rides

    if reduce:
        side = []
        for j in range(half):
            where = (chip + j + 1) % half
            side.append(
                send(
                    partial_ref.at[2 * where + (1 - core)],
                    side_ref.at[j],
                    side_send.at[j],
                    side_recv.at[j],
                    (sibling, plane),
                )
            )
        far = []
        for j in range(1, half):
            target, where = others[j - 1]
            side[j - 1].wait_recv()
            out_ref[j - 1] = (
                partial_ref[2 * where + core].astype(F32) + side_ref[j - 1].astype(F32)
            ).astype(BF16)
            far.append(
                send(
                    out_ref.at[j - 1],
                    in_ref.at[j - 1],
                    far_send.at[j - 1],
                    far_recv.at[j - 1],
                    (target, plane),
                )
            )
        side[half - 1].wait_recv()
        total = partial_ref[me].astype(F32) + side_ref[half - 1].astype(F32)
        for j in range(1, half):
            far[j - 1].wait_recv()
            total = total + in_ref[j - 1].astype(F32)
        pending += side + far
    if mode == "norm":
        value = base_ref[...] + total
        new_ref[...] = value
        unit, _ = norm_parts(value)
        result = unit * gain_ref[...] + shift_ref[...]
    elif mode == "back":
        unit, inverse = norm_parts(saved_ref[...].astype(F32))
        stat_ref[0:1, :] = jnp.sum(total * unit, axis=0, keepdims=True)
        stat_ref[1:2, :] = jnp.sum(total, axis=0, keepdims=True)
        result = base_ref[...] + norm_backward(total, unit, inverse, gain_ref[...])
        new_ref[...] = result
    elif mode == "plain":
        result = base_ref[...]
        if reduce:
            result = result + total
            new_ref[...] = result

    if gather:
        full_ref[me] = result.astype(BF16)
        sends = gather_begin(count, me, plane, full_ref, gather_send, gather_recv)
        pending += gather_end(count, me, plane, full_ref, sends, pass_send, pass_recv)
    for copy in rides:
        copy.wait_recv()
    for copy in stays:
        copy.wait()
    for i, kind in enumerate(kinds):
        if kind not in ("sum0", "sum1"):
            continue
        steps = ride_outs[i].shape[0]
        chunk = 1 if kind == "sum1" else min(steps, 32)

        def add(step, carry, i=i, kind=kind, chunk=chunk):
            at = pl.ds(pl.multiple_of(step * chunk, chunk), chunk)
            own = ride_refs[i][plane, at] if kind == "sum0" else ride_refs[i][at, plane]
            total = own.astype(F32)
            for j in range(1, ring):
                total = total + land_refs[i][j - 1, at].astype(F32)
            ride_outs[i][at] = total.astype(ride_outs[i].dtype)
            return carry

        lax.fori_loop(0, steps // chunk, add, 0)
    for copy in pending:
        copy.wait_send()


def plane_exchange(
    count,
    ring,
    call_id,
    partial=None,
    base=None,
    gains=None,
    shifts=None,
    saved=None,
    gather=True,
    sums=(),
    gets=(),
    mixes=(),
    hops=(),
):
    reduce = partial is not None
    mode = "none" if base is None else "plain"
    if gains is not None:
        mode = "norm" if saved is None else "back"
    half = count // 2
    operands = [partial] if reduce else []
    if base is not None:
        operands.append(base)
        rows, width = base.shape
    if gains is not None:
        operands.append(gains.reshape(1, width))
    if mode == "norm":
        operands.append(shifts.reshape(1, width))
    if mode == "back":
        operands.append(saved)
    operands += sums
    specs = [pl.BlockSpec(memory_space=VMEM)] * len(operands)
    operands += list(gets) + list(mixes) + list(hops)
    specs += [pl.BlockSpec(memory_space=pl.ANY)] * (len(operands) - len(specs))
    kinds = tuple("sum" + str(x.ndim - 3) for x in sums)
    kinds += tuple("get" + str(x.ndim - 2) for x in gets)
    kinds += ("mix",) * len(mixes) + ("hop",) * len(hops)
    outs, scratch = [], []
    if gather:
        outs.append(jax.ShapeDtypeStruct((count, rows, width), BF16))
    if reduce:
        outs.append(jax.ShapeDtypeStruct((rows, width), F32))
    if mode == "back":
        outs.append(jax.ShapeDtypeStruct((8, width), F32))
    lands = [x.shape[1:] if x.ndim == 3 else x.shape[:1] + x.shape[2:] for x in sums]
    outs += [
        jax.ShapeDtypeStruct(land, F32 if x.ndim == 3 else BF16) for land, x in zip(lands, sums)
    ]
    out_specs = [pl.BlockSpec(memory_space=VMEM)] * len(outs)
    outs += [
        jax.ShapeDtypeStruct((ring,) + x.shape if x.ndim == 2 else (count, ring) + x.shape[1:], BF16)
        for x in gets
    ]
    outs += [jax.ShapeDtypeStruct(x.shape, x.dtype) for x in list(mixes) + list(hops)]
    out_specs += [pl.BlockSpec(memory_space=pl.ANY)] * (len(outs) - len(out_specs))
    dma = pltpu.SemaphoreType.DMA
    if reduce:
        scratch += [
            VMEM((half, rows, width), BF16),
            VMEM((half - 1, rows, width), BF16),
            VMEM((half - 1, rows, width), BF16),
            dma((half,)),
            dma((half,)),
            dma((half - 1,)),
            dma((half - 1,)),
        ]
    if gather:
        scratch += [dma((half,)), dma((half,)), dma((half - 1,)), dma((half - 1,))]
    scratch += [VMEM((ring - 1,) + land, BF16) for land in lands]
    if kinds:
        most = max(ring, count if mixes else 0) - 1
        scratch += [dma((len(kinds), most)), dma((len(kinds), most)), dma((len(kinds),))]
    return pl.pallas_call(
        functools.partial(plane_kernel, count, ring, reduce, mode, gather, kinds),
        out_shape=tuple(outs),
        in_specs=specs,
        out_specs=tuple(out_specs),
        scratch_shapes=scratch,
        compiler_params=pltpu.CompilerParams(
            collective_id=call_id, has_side_effects=True, vmem_limit_bytes=40 * 1024 * 1024
        ),
        cost_estimate=pl.CostEstimate(
            flops=0, bytes_accessed=(60 if reduce else 30) << 20, transcendentals=0
        ),
    )(*operands)


def first_kernel(count, ring, layers, talls, *refs):
    refs = list(refs)
    token_ref, small_ref, served_ref, flag_ref = (refs.pop(0) for _ in range(4))
    column_refs = [refs.pop(0) for _ in range(2)]
    tall_refs = [refs.pop(0) for _ in range(talls)]
    full_ref, vector_ref, rows_ref, flags_ref = (refs.pop(0) for _ in range(4))
    wide_refs = [[refs.pop(0) for _ in range(layers)] for _ in range(2)]
    whole_refs = [refs.pop(0) for _ in range(talls)]
    small_all = refs.pop(0)
    column_all = [refs.pop(0) for _ in range(2)]
    own_sem = refs.pop(0)
    (
        gather_send,
        gather_recv,
        pass_send,
        pass_recv,
        small_send,
        small_recv,
        across_send,
        across_recv,
        column_send,
        column_recv,
        tall_send,
        tall_recv,
        wide_send,
        wide_recv,
        flag_send,
        flag_recv,
        rows_send,
        rows_recv,
    ) = refs
    me = lax.axis_index("dp")
    plane = lax.axis_index("ctx")
    mates = [(me + k) % count for k in range(1, count)]
    planes = [(plane + j) % ring for j in range(1, ring)]
    greet_all([(mate, plane) for mate in mates] + [(me, there) for there in planes])

    stays = []

    def stay(source, target):
        copy = pltpu.make_async_copy(source, target, own_sem.at[len(stays)])
        copy.start()
        stays.append(copy)

    small_all[me, plane] = small_ref[...]
    smalls = [
        send(small_ref, small_all.at[me, plane], small_send.at[k], small_recv.at[k], (mate, plane))
        for k, mate in enumerate(mates)
    ]
    columns = []
    for i in range(2):
        stay(column_refs[i].at[me], column_all[i].at[me])
        for k, mate in enumerate(mates):
            columns.append(
                send(
                    column_refs[i].at[mate],
                    column_all[i].at[me],
                    column_send.at[i, k],
                    column_recv.at[i, k],
                    (mate, plane),
                )
            )
    pending = smalls + columns
    late = []
    for j, there in enumerate(planes):
        late.append(
            send(
                flag_ref.at[there],
                flags_ref.at[plane],
                flag_send.at[j],
                flag_recv.at[j],
                (me, there),
            )
        )
    flags_ref[plane] = flag_ref[plane]
    for copy in smalls:
        copy.wait_recv()
    across = [
        send(
            small_all.at[:, plane],
            small_all.at[:, plane],
            across_send.at[j],
            across_recv.at[j],
            (me, there),
        )
        for j, there in enumerate(planes)
    ]

    def spread_tall(i):
        stay(tall_refs[i], whole_refs[i].at[plane])
        for j, there in enumerate(planes):
            late.append(
                send(
                    tall_refs[i],
                    whole_refs[i].at[plane],
                    tall_send.at[i, j],
                    tall_recv.at[i, j],
                    (me, there),
                )
            )

    for i in range(2):
        spread_tall(i)
    for copy in across:
        copy.wait_recv()
    groups = vector_ref.shape[1] // 128
    members = count * ring // groups
    for group in range(groups):
        total = small_all[group * members // ring, group * members % ring]
        for n in range(group * members + 1, (group + 1) * members):
            total = total + small_all[n // ring, n % ring]
        vector_ref[:, group * 128 : (group + 1) * 128] = total
    unit, _ = norm_parts(token_ref[...].astype(F32))
    full_ref[me] = (unit * vector_ref[0:1, :] + vector_ref[1:2, :]).astype(BF16)
    sends = gather_begin(count, me, plane, full_ref, gather_send, gather_recv)
    for copy in columns:
        copy.wait_recv()
    for copy in stays[:2]:
        copy.wait()
    for layer in range(layers):
        for i in range(2):
            stay(column_all[i].at[:, layer], wide_refs[i][layer].at[:, plane])
            for j, there in enumerate(planes):
                late.append(
                    send(
                        column_all[i].at[:, layer],
                        wide_refs[i][layer].at[:, plane],
                        wide_send.at[layer, i, j],
                        wide_recv.at[layer, i, j],
                        (me, there),
                    )
                )
    for i in range(2, talls):
        spread_tall(i)
    for k, mate in enumerate(mates):
        late.append(
            send(
                served_ref.at[mate],
                rows_ref.at[me],
                rows_send.at[k],
                rows_recv.at[k],
                (mate, plane),
            )
        )
    stay(served_ref.at[me], rows_ref.at[me])
    pending += gather_end(count, me, plane, full_ref, sends, pass_send, pass_recv)
    for copy in late:
        copy.wait_recv()
    for copy in stays[2:]:
        copy.wait()
    for copy in pending + across + late:
        copy.wait_send()


def first_exchange(count, ring, call_id, tokens, small, served, flags, joint, expand, talls):
    rows, width = tokens.shape
    layers, half = joint.shape[1], count // 2
    dma = pltpu.SemaphoreType.DMA
    near, far = pl.BlockSpec(memory_space=VMEM), pl.BlockSpec(memory_space=pl.ANY)
    outs = [
        jax.ShapeDtypeStruct((count, rows, width), BF16),
        jax.ShapeDtypeStruct((16, width), F32),
        jax.ShapeDtypeStruct(served.shape, BF16),
        jax.ShapeDtypeStruct(flags.shape, flags.dtype),
    ]
    for x in (joint, expand):
        outs += [jax.ShapeDtypeStruct((count, ring) + x.shape[2:], BF16)] * layers
    outs += [jax.ShapeDtypeStruct((ring,) + x.shape, BF16) for x in talls]

    def pair(*shape):
        return [dma(shape), dma(shape)]

    return pl.pallas_call(
        functools.partial(first_kernel, count, ring, layers, len(talls)),
        out_shape=tuple(outs),
        in_specs=[near, near, far, near, near, near] + [far] * len(talls),
        out_specs=tuple([near, near, far, near] + [far] * (2 * layers + len(talls))),
        scratch_shapes=[
            VMEM((count, ring, 16, 128), F32),
            VMEM(joint.shape, BF16),
            VMEM(expand.shape, BF16),
            dma((3 + 2 * layers + len(talls),)),
        ]
        + pair(half)
        + pair(half - 1)
        + pair(count - 1)
        + pair(ring - 1)
        + pair(2, count - 1)
        + pair(len(talls), ring - 1)
        + pair(layers, 2, ring - 1)
        + pair(ring - 1)
        + pair(count - 1),
        compiler_params=pltpu.CompilerParams(
            collective_id=call_id, has_side_effects=True, vmem_limit_bytes=40 * 1024 * 1024
        ),
        cost_estimate=pl.CostEstimate(flops=0, bytes_accessed=200 << 20, transcendentals=0),
    )(tokens, small, served, flags, joint, expand, *talls)


def last_kernel(
    count,
    ring,
    seqs,
    sums_ref,
    wide_ref,
    rows_ref,
    total_ref,
    mixed_ref,
    home_ref,
    sums_in,
    across_ref,
    own_sem,
    home_send,
    home_recv,
    sums_send,
    sums_recv,
    wide_send,
    wide_recv,
    across_send,
    across_recv,
):
    me = lax.axis_index("dp")
    plane = lax.axis_index("ctx")
    home = (plane * seqs + me // ring, me % ring)
    guest = ((me % seqs) * ring + plane, me // seqs)
    away = jnp.logical_or(home[0] != me, home[1] != plane)
    barrier = pltpu.get_barrier_semaphore()
    greet = [((me + k) % count, plane) for k in range(1, count)]
    greet += [(me, (plane + j) % ring) for j in range(1, ring)]
    for target in greet:
        pl.semaphore_signal(barrier, inc=1, device_id=target, device_id_type=MESH)

    @pl.when(away)
    def _():
        pl.semaphore_signal(barrier, inc=1, device_id=guest, device_id_type=MESH)

    pl.semaphore_wait(barrier, len(greet) + away.astype(jnp.int32))

    pending, sums = [], []
    for k in range(1, count):
        there = (me + k) % count
        sums.append(
            send(
                sums_ref.at[there],
                sums_in.at[me],
                sums_send.at[k - 1],
                sums_recv.at[k - 1],
                (there, plane),
            )
        )
    for k in range(1, count):
        there = (me + k) % count
        pending.append(
            send(
                wide_ref.at[there],
                mixed_ref.at[me],
                wide_send.at[k - 1],
                wide_recv.at[k - 1],
                (there, plane),
            )
        )
    home_copy = pltpu.make_async_remote_copy(
        src_ref=rows_ref,
        dst_ref=home_ref,
        send_sem=home_send,
        recv_sem=home_recv,
        device_id=home,
        device_id_type=MESH,
    )

    @pl.when(away)
    def _():
        home_copy.start()

    @pl.when(jnp.logical_not(away))
    def _():
        home_ref[...] = rows_ref[...]

    sums_in[me] = sums_ref[me]
    stay = pltpu.make_async_copy(wide_ref.at[me], mixed_ref.at[me], own_sem)
    stay.start()
    for copy in sums:
        copy.wait_recv()
    total = sums_in[0]
    for k in range(1, count):
        total = total + sums_in[k]
    across_ref[plane] = total
    across = [
        send(
            across_ref.at[plane],
            across_ref.at[plane],
            across_send.at[j - 1],
            across_recv.at[j - 1],
            (me, (plane + j) % ring),
        )
        for j in range(1, ring)
    ]
    for copy in across:
        copy.wait_recv()
    total = across_ref[0]
    for j in range(1, ring):
        total = total + across_ref[j]
    total_ref[...] = total
    for copy in pending:
        copy.wait_recv()
    stay.wait()
    for copy in pending + sums + across:
        copy.wait_send()

    @pl.when(away)
    def _():
        home_copy.wait_recv()
        home_copy.wait_send()


def last_exchange(count, ring, seqs, call_id, sums, wide, rows):
    dma = pltpu.SemaphoreType.DMA
    spec = pl.BlockSpec(memory_space=VMEM)
    return pl.pallas_call(
        functools.partial(last_kernel, count, ring, seqs),
        out_shape=(
            jax.ShapeDtypeStruct(sums.shape[1:], F32),
            jax.ShapeDtypeStruct(wide.shape, BF16),
            jax.ShapeDtypeStruct(rows.shape, BF16),
        ),
        in_specs=[spec] * 3,
        out_specs=(spec,) * 3,
        scratch_shapes=[
            VMEM(sums.shape, F32),
            VMEM((ring,) + sums.shape[1:], F32),
            dma,
            dma,
            dma,
            dma((count - 1,)),
            dma((count - 1,)),
            dma((count - 1,)),
            dma((count - 1,)),
            dma((ring - 1,)),
            dma((ring - 1,)),
        ],
        compiler_params=pltpu.CompilerParams(collective_id=call_id, has_side_effects=True),
    )(sums, wide, rows)


def after(*arrays):
    return lax.optimization_barrier(arrays)


def dot(left, right):
    return jnp.dot(left, right, preferred_element_type=F32)


def contract_rows(left, right):
    return lax.dot_general(left, right, (((0,), (0,)), ((), ())), preferred_element_type=F32)


def contract_cols(left, right):
    return lax.dot_general(left, right, (((1,), (1,)), ((), ())), preferred_element_type=F32)


def split_heads(flat, seqs, heads):
    return flat.reshape(seqs, flat.shape[0] // seqs, heads, -1)


def attend(packed, seqs, heads):
    width = packed.shape[1] // 3
    queries, keys, values = (
        split_heads(packed[:, i * width : (i + 1) * width], seqs, heads) for i in range(3)
    )
    scale = queries.shape[-1] ** (-0.5)
    scores = jnp.einsum("sqhd,skhd->shqk", queries, keys, preferred_element_type=F32) * scale
    at = jnp.arange(queries.shape[1])
    allowed = at[:, None] >= at[None, :]
    scores = jnp.where(allowed, scores, FLOOR)
    highest = jnp.max(scores, axis=-1, keepdims=True)
    raised = jnp.exp(scores - highest)
    probs = raised / jnp.sum(raised, axis=-1, keepdims=True)
    output = jnp.einsum("shqk,skhd->sqhd", probs.astype(BF16), values, preferred_element_type=F32)
    return probs, output.reshape(packed.shape[0], width).astype(BF16)


def attend_backward(packed, probs, grad_flat, seqs, heads):
    width = packed.shape[1] // 3
    queries, keys, values = (
        split_heads(packed[:, i * width : (i + 1) * width], seqs, heads) for i in range(3)
    )
    grad = split_heads(grad_flat, seqs, heads)
    scale = queries.shape[-1] ** (-0.5)
    grad_probs = jnp.einsum("sqhd,skhd->shqk", grad, values, preferred_element_type=F32)
    delta = jnp.sum(probs * grad_probs, axis=-1, keepdims=True)
    grad_scores = (probs * (grad_probs - delta)).astype(BF16)
    parts = (
        jnp.einsum("shqk,skhd->sqhd", grad_scores, keys, preferred_element_type=F32) * scale,
        jnp.einsum("shqk,sqhd->skhd", grad_scores, queries, preferred_element_type=F32) * scale,
        jnp.einsum("shqk,sqhd->skhd", probs.astype(BF16), grad, preferred_element_type=F32),
    )
    return jnp.concatenate(
        [part.reshape(packed.shape[0], width).astype(BF16) for part in parts], axis=1
    )


def smooth_gate(values):
    return jax.nn.gelu(values, approximate=True)


def ranks_of(flags):
    planes, groups, rows = flags.shape
    upto = jnp.arange(rows)[:, None] <= jnp.arange(rows)[None, :]
    inside = dot(flags.astype(BF16), upto.astype(BF16))
    before = jnp.where(
        jnp.arange(groups)[None, :, None] < jnp.arange(groups)[None, None, :],
        inside[:, :, -1:],
        0.0,
    )
    rank = inside + jnp.sum(before, axis=1)[:, :, None]
    return rank.reshape(planes, groups * rows), rank[:, -1, -1]


def pieces_of(values, terms):
    pieces = []
    for _ in range(terms):
        pieces.append(values.astype(BF16))
        values = values - pieces[-1].astype(F32)
    return jnp.concatenate(pieces, axis=0)


def recall(hidden, gains, shifts, stored, token_of, cotangent):
    rows = hidden.shape[0]
    unit, inverse = norm_parts(hidden)
    query = unit * gains + shifts
    scale = DISTANCE_SCALE * math.sqrt(query.shape[-1])
    usable = token_of[None, :] == jnp.arange(rows)[:, None]
    lengths = jnp.sum(jnp.square(stored.astype(F32)), axis=-1)
    near = contract_cols(pieces_of(query, 3), stored).reshape(3, rows, -1)
    near = near[0] + (near[1] + near[2])
    pull = RECALL_SHARE * contract_cols(cotangent, stored)
    scaled = jnp.where(usable, (2.0 * near - lengths[None, :]) / scale, FLOOR)
    raised = jnp.where(usable, jnp.exp(scaled - jnp.max(scaled, axis=1, keepdims=True)), 0.0)
    weights = raised / jnp.sum(raised, axis=1, keepdims=True)
    grad_scaled = weights * (pull - jnp.sum(weights * pull, axis=1, keepdims=True))
    both = jnp.concatenate([pieces_of(weights, 2), pieces_of(grad_scaled, 2)], axis=0)
    both = dot(both, stored).reshape(4, rows, -1)
    recalled, moved = both[0] + both[1], both[2] + both[3]
    mixed = (1.0 - RECALL_SHARE) * query + RECALL_SHARE * recalled
    moved = moved - jnp.sum(grad_scaled, axis=1, keepdims=True) * query
    grad_query = (1.0 - RECALL_SHARE) * cotangent.astype(F32) + moved * (2.0 / scale)
    sums = jnp.stack([jnp.sum(grad_query * unit, axis=0), jnp.sum(grad_query, axis=0)])
    return mixed, norm_backward(grad_query, unit, inverse, gains), sums


def shards(
    tokens,
    ln1_gain,
    ln1_bias,
    qkv_weight,
    out_weight,
    ln2_gain,
    ln2_bias,
    in_weight,
    fc_weight,
    final_gain,
    final_bias,
    datastore,
    neighbour_owner,
    neighbour_row,
    neighbour_count,
    cotangent,
):
    local_seqs, local_rows, width = tokens.shape
    rows = local_seqs * local_rows
    count, ring = lax.axis_size("dp"), lax.axis_size("ctx")
    devices = count * ring
    both = ("dp", "ctx")
    seqs = count * local_seqs // ring
    heads = HEADS // count
    slots = neighbour_owner.shape[2]
    part = width // devices
    head_width = width // count
    inner_width = in_weight.shape[2] // count

    forth = []
    for s in range(count):
        for p in range(ring):
            forth.append((s * ring + p, ((s % seqs) * ring + p) * ring + s // seqs))
    back = [(there, here) for here, there in forth]
    order = [here for here, there in sorted(forth, key=lambda pair: pair[1])]

    room = rows * slots // ring
    owners = neighbour_owner.reshape(rows, slots)
    live = neighbour_count.reshape(rows, 1)
    hits = (owners[:, :, None] == jnp.arange(devices)[None, None, :]) & (
        jnp.arange(slots)[None, :, None] < live[:, :, None]
    )
    asked = jnp.sum(jnp.where(hits, neighbour_row.reshape(rows, slots, 1), 0), axis=1).T
    asked = lax.all_to_all(asked, both, split_axis=0, concat_axis=0, tiled=True)
    asked = jnp.stack([asked[here] for here in order])
    usable = jnp.any(hits, axis=1).T.reshape(count, ring, rows).transpose(1, 0, 2)
    crowded = jnp.max(jnp.sum(usable, axis=(1, 2))) > room

    small = jnp.stack(
        [ln1_gain[0], ln1_bias[0], ln1_gain[1], ln1_bias[1], ln2_gain[0], ln2_bias[0]]
        + [ln2_gain[1], ln2_bias[1], final_gain, final_bias]
    ).astype(F32)
    small = jnp.concatenate([small, jnp.broadcast_to(crowded.astype(F32), (1, part))])
    here = lax.axis_index("dp") * ring + lax.axis_index("ctx")
    places = 128 // part
    small = jnp.tile(jnp.pad(small, ((0, 5), (0, 0))), (1, places))
    small = jnp.where(jnp.arange(128)[None, :] // part == here % places, small, 0.0)

    joint_own = qkv_weight.reshape(LAYERS, part, 3, count, head_width).transpose(3, 0, 1, 2, 4)
    joint_own = joint_own.reshape(count, LAYERS, part, 3 * head_width)
    expand_own = in_weight.reshape(LAYERS, part, count, inner_width).transpose(2, 0, 1, 3)

    my_tokens, usable, asked = after(tokens.reshape(rows, width), usable.astype(jnp.int32), asked)
    served = datastore.at[asked.reshape(-1)].get(mode="promise_in_bounds")
    my_tokens = lax.ppermute(my_tokens, both, forth)
    usable = lax.ppermute(usable, both, forth)
    exchange = functools.partial(plane_exchange, count, ring)
    first = first_exchange(
        count,
        ring,
        0,
        my_tokens,
        small,
        served.reshape(count, ring * rows, width),
        usable,
        joint_own,
        expand_own,
        (out_weight[0], fc_weight[0], out_weight[1]),
    )
    normed, vectors, served, flags = first[:4]
    joint, expand = list(first[4 : 4 + LAYERS]), list(first[4 + LAYERS : 4 + 2 * LAYERS])
    project, shrink = [first[-3], first[-1]], [first[-2], None]
    gain_one, shift_one = [vectors[0], vectors[2]], [vectors[1], vectors[3]]
    gain_two, shift_two = [vectors[4], vectors[6]], [vectors[5], vectors[7]]
    head_gain, head_shift = vectors[8], vectors[9]
    crowded = jnp.max(vectors[10]) > 0.5
    cotangent, normed = after(cotangent, normed)
    my_cotangent = lax.ppermute(cotangent.reshape(rows, width), both, forth)
    rank, _ = ranks_of(flags)
    served = served.reshape(count, ring, rows, width)

    def sent(begin, end):
        begin, end = begin * room // 16, end * room // 16
        chosen = flags.reshape(ring, 1, count * rows) * (
            rank[:, None, :] == jnp.arange(begin + 1, end + 1, dtype=F32)[None, :, None]
        )
        return jnp.einsum(
            "cpdt,dctw->cpw",
            chosen.astype(BF16).reshape(ring, end - begin, count, rows),
            served,
            preferred_element_type=F32,
        ).astype(BF16)

    hidden = my_tokens.astype(F32)
    saved = []
    for layer in range(LAYERS):
        normed = normed.reshape(count * rows, width)
        joint[layer] = joint[layer].reshape(width, 3 * head_width)
        project[layer] = project[layer].reshape(-1, width)
        packed = dot(normed, joint[layer]).astype(BF16)
        probs, attended = attend(packed, seqs, heads)
        partial = dot(attended, project[layer]).astype(BF16).reshape(count, rows, width)
        gains = (gain_two[layer], shift_two[layer])
        if layer == 0:
            normed_two, middle, stored0 = exchange(
                2, partial, hidden, *gains, hops=(sent(0, 6),)
            )
        else:
            normed_two, middle, stored2 = exchange(
                3, partial, hidden, *gains, hops=(sent(9, 16),)
            )
        normed_two = normed_two.reshape(count * rows, width)
        expand[layer] = expand[layer].reshape(width, inner_width)
        shrink[layer] = shrink[layer].reshape(-1, width)
        inner = dot(normed_two, expand[layer])
        active = smooth_gate(inner).astype(BF16)
        partial = dot(active, shrink[layer]).astype(BF16).reshape(count, rows, width)
        saved.append((hidden, normed, packed, probs, attended, middle, normed_two, inner, active))
        if layer + 1 < LAYERS:
            normed, hidden, shrink[1], stored1 = exchange(
                4,
                partial,
                middle,
                gain_one[layer + 1],
                shift_one[layer + 1],
                gets=(fc_weight[1],),
                hops=(sent(6, 9),),
            )
        else:
            (hidden,) = exchange(5, partial, middle, gather=False)

    def few(served):
        rank, total = ranks_of(usable)
        at = jnp.arange(room, dtype=F32)
        kept = jnp.sum((rank[:, None, :] <= at[None, :, None]).astype(jnp.int32), axis=-1)
        stored = jnp.concatenate([stored0, stored1, stored2], axis=1).reshape(ring * room, width)
        token_of = jnp.where(at[None, :] < total[:, None], kept % rows, -1).reshape(-1)
        return recall(hidden, head_gain, head_shift, stored, token_of, my_cotangent)

    def many(served):
        stored = lax.all_to_all(served, "ctx", split_axis=1, concat_axis=0, tiled=True)
        token_of = jnp.where(usable > 0, jnp.arange(rows)[None, None, :], -1).reshape(-1)
        stored = stored.reshape(devices * rows, width)
        return recall(hidden, head_gain, head_shift, stored, token_of, my_cotangent)

    mixed, grad_hidden, head_sums = lax.cond(crowded, many, few, served)
    mixed = lax.ppermute(mixed, both, back)

    (branch,) = exchange(6, base=grad_hidden)
    sums_one, sums_two = [None] * LAYERS, [None] * LAYERS
    grad_wide, grad_tall = [None] * LAYERS, [None] * LAYERS
    for layer in reversed(range(LAYERS)):
        start, normed, packed, probs, attended, middle, normed_two, inner, active = saved[layer]
        branch = branch.reshape(count * rows, width)
        grad_shrink = contract_rows(active, branch).astype(BF16).reshape(ring, -1, width)
        grad_active = contract_cols(branch, shrink[layer])
        _, gate_back = jax.vjp(smooth_gate, inner)
        grad_inner = gate_back(grad_active)[0].astype(BF16)
        grad_expand = contract_rows(normed_two, grad_inner).astype(BF16)
        grad_expand = grad_expand.reshape(count, ring, part, inner_width)
        partial = contract_cols(grad_inner, expand[layer]).astype(BF16)
        grad_out, grad_middle, sums_two[layer], shrink_sum, expand_sum = exchange(
            7,
            partial.reshape(count, rows, width),
            grad_hidden,
            gain_two[layer],
            saved=middle,
            sums=(grad_shrink, grad_expand),
        )
        grad_out = grad_out.reshape(count * rows, width)
        grad_project = contract_rows(attended, grad_out).astype(BF16).reshape(ring, part, width)
        grad_attended = contract_cols(grad_out, project[layer]).astype(BF16)
        grad_packed = attend_backward(packed, probs, grad_attended, seqs, heads)
        grad_joint = contract_rows(normed, grad_packed).astype(BF16)
        grad_joint = grad_joint.reshape(count, ring, part, 3 * head_width)
        partial = contract_cols(grad_packed, joint[layer]).astype(BF16)
        partial = partial.reshape(count, rows, width)
        rides = (grad_project, grad_joint)
        if layer > 0:
            branch, grad_hidden, sums_one[layer], project_sum, joint_sum = exchange(
                8, partial, grad_middle, gain_one[layer], saved=start, sums=rides
            )
        else:
            grad_hidden, sums_one[layer], project_sum, joint_sum = exchange(
                9, partial, grad_middle, gain_one[layer], saved=start, gather=False, sums=rides
            )
        grad_wide[layer] = jnp.concatenate([joint_sum, expand_sum], axis=-1)
        grad_tall[layer] = (project_sum, shrink_sum)

    sums = jnp.concatenate(
        [sums_one[0][:2], sums_one[1][:2], sums_two[0][:2], sums_two[1][:2], head_sums]
    )
    sums = jnp.pad(sums, ((0, 6), (0, 0))).reshape(16, count, head_width).transpose(1, 0, 2)
    sums, wide, tokens_grad = last_exchange(
        count, ring, seqs, 10, sums, jnp.stack(grad_wide, axis=1), grad_hidden.astype(BF16)
    )
    sums = lax.dynamic_slice_in_dim(sums, lax.axis_index("ctx") * part, part, axis=1)
    wide = wide.astype(F32)
    qkv_grad = (
        wide[..., : 3 * head_width]
        .reshape(count, LAYERS, part, 3, head_width)
        .transpose(1, 2, 3, 0, 4)
        .reshape(LAYERS, part, 3 * width)
    )
    in_grad = wide[..., 3 * head_width :].transpose(1, 2, 0, 3).reshape(LAYERS, part, -1)

    return (
        mixed.reshape(local_seqs, local_rows, width),
        tokens_grad.astype(F32).reshape(local_seqs, local_rows, width),
        jnp.stack([sums[0], sums[2]]),
        jnp.stack([sums[1], sums[3]]),
        qkv_grad,
        jnp.stack([pair[0] for pair in grad_tall]),
        jnp.stack([sums[4], sums[6]]),
        jnp.stack([sums[5], sums[7]]),
        in_grad,
        jnp.stack([pair[1] for pair in grad_tall]),
        sums[8],
        sums[9],
    )


def solution(mesh):
    both = ("dp", "ctx")
    return jax.shard_map(
        shards,
        mesh=mesh,
        in_specs=(
            P("dp", "ctx", None),
            P(None, both),
            P(None, both),
            P(None, both, None),
            P(None, both, None),
            P(None, both),
            P(None, both),
            P(None, both, None),
            P(None, both, None),
            P(both),
            P(both),
            P(both, None),
            P("dp", "ctx", None),
            P("dp", "ctx", None),
            P("dp", "ctx"),
            P("dp", "ctx", None),
        ),
        out_specs=(
            P("dp", "ctx", None),
            P("dp", "ctx", None),
            P(None, both),
            P(None, both),
            P(None, both, None),
            P(None, both, None),
            P(None, both),
            P(None, both),
            P(None, both, None),
            P(None, both, None),
            P(both),
            P(both),
        ),
        check_vma=False,
    )
```

```python
import functools
import math

import jax
import jax.numpy as jnp
from jax import lax
from jax.experimental import pallas as pl
from jax.experimental.pallas import tpu as pltpu
from jax.sharding import PartitionSpec as P

HEADS = 16
LAYERS = 2

EPSILON = 1e-05
FLOOR = -1e30
RECALL_SHARE = 0.25
DISTANCE_SCALE = 1.5

MESH = pl.DeviceIdType.MESH
VMEM = pltpu.VMEM
BF16 = jnp.bfloat16
F32 = jnp.float32


def norm_parts(values):
    average = jnp.mean(values, axis=-1, keepdims=True)
    centered = values - average
    variance = jnp.mean(centered * centered, axis=-1, keepdims=True)
    inverse = lax.rsqrt(variance + EPSILON)
    return centered * inverse, inverse


def norm_backward(grad, unit, inverse, gains):
    scaled = grad * gains
    return inverse * (
        scaled
        - jnp.mean(scaled, axis=-1, keepdims=True)
        - unit * jnp.mean(scaled * unit, axis=-1, keepdims=True)
    )


def send(source, target, send_sem, recv_sem, where):
    copy = pltpu.make_async_remote_copy(
        src_ref=source,
        dst_ref=target,
        send_sem=send_sem,
        recv_sem=recv_sem,
        device_id=where,
        device_id_type=MESH,
    )
    copy.start()
    return copy


def partner_of(me, plane, ring):
    return ((me // ring) * ring + plane, me % ring), me % ring != plane


def greet_all(targets, partner=None, away=None):
    barrier = pltpu.get_barrier_semaphore()
    for target in targets:
        pl.semaphore_signal(barrier, inc=1, device_id=target, device_id_type=MESH)
    if partner is None:
        pl.semaphore_wait(barrier, len(targets))
        return

    @pl.when(away)
    def _():
        pl.semaphore_signal(barrier, inc=1, device_id=partner, device_id_type=MESH)

    pl.semaphore_wait(barrier, len(targets) + away.astype(jnp.int32))


def swap_begin(source, target, send_sem, recv_sem, partner, away):
    copy = pltpu.make_async_remote_copy(
        src_ref=source,
        dst_ref=target,
        send_sem=send_sem,
        recv_sem=recv_sem,
        device_id=partner,
        device_id_type=MESH,
    )
    stay = pltpu.make_async_copy(source, target, recv_sem)

    @pl.when(away)
    def _():
        copy.start()

    @pl.when(jnp.logical_not(away))
    def _():
        stay.start()

    return copy, stay, away


def swap_end(swap):
    copy, stay, away = swap

    @pl.when(away)
    def _():
        copy.wait()

    @pl.when(jnp.logical_not(away))
    def _():
        stay.wait()


def gather_begin(count, me, plane, full_ref, send_sem, recv_sem):
    half = count // 2
    chip, core = me // 2, me % 2
    targets = [2 * chip + (1 - core)]
    targets += [2 * ((chip + j) % half) + core for j in range(1, half)]
    return [
        send(full_ref.at[me], full_ref.at[me], send_sem.at[j], recv_sem.at[j], (target, plane))
        for j, target in enumerate(targets)
    ]


def gather_end(count, me, plane, full_ref, sends, send_sem, recv_sem):
    half = count // 2
    chip, core = me // 2, me % 2
    sibling = 2 * chip + (1 - core)
    passes = []
    for j in range(1, half):
        block = full_ref.at[2 * ((chip + half - j) % half) + core]
        sends[j].wait_recv()
        passes.append(
            send(block, block, send_sem.at[j - 1], recv_sem.at[j - 1], (sibling, plane))
        )
    sends[0].wait_recv()
    for copy in passes:
        copy.wait_recv()
    return sends + passes


def plane_kernel(count, ring, reduce, mode, gather, kinds, *refs):
    refs = list(refs)
    half = count // 2
    partial_ref = refs.pop(0) if reduce else None
    base_ref = refs.pop(0) if mode != "none" else None
    gain_ref = refs.pop(0) if mode in ("norm", "back") else None
    shift_ref = refs.pop(0) if mode == "norm" else None
    saved_ref = refs.pop(0) if mode == "back" else None
    ride_refs = [refs.pop(0) for _ in kinds]
    full_ref = refs.pop(0) if gather else None
    new_ref = refs.pop(0) if reduce else None
    stat_ref = refs.pop(0) if mode == "back" else None
    ride_outs = [refs.pop(0) for _ in kinds]
    if reduce:
        side_ref, out_ref, in_ref = refs.pop(0), refs.pop(0), refs.pop(0)
        side_send, side_recv, far_send, far_recv = (refs.pop(0) for _ in range(4))
    if gather:
        gather_send, gather_recv, pass_send, pass_recv = (refs.pop(0) for _ in range(4))
    land_refs = [refs.pop(0) if kind in ("sum0", "sum1") else None for kind in kinds]
    if kinds:
        ride_send, ride_recv, ride_own = refs.pop(0), refs.pop(0), refs.pop(0)

    me = lax.axis_index("dp")
    plane = lax.axis_index("ctx")
    chip, core = me // 2, me % 2
    sibling = 2 * chip + (1 - core)
    others = [(2 * ((chip + j) % half) + core, (chip + j) % half) for j in range(1, half)]

    greet = []
    if "mix" in kinds:
        greet += [((me + k) % count, plane) for k in range(1, count)]
    elif reduce or gather:
        greet += [(sibling, plane)] + [(other, plane) for other, _ in others]
    if any(kind not in ("mix", "swap") for kind in kinds):
        greet += [(me, (plane + j) % ring) for j in range(1, ring)]
    partner, away = partner_of(me, plane, ring)
    if "swap" in kinds:
        greet_all(greet, partner, away)
    else:
        greet_all(greet)
    pending = []
    rides, stays, swaps = [], [], []
    for i, kind in enumerate(kinds):
        for k in range(1, count) if kind == "mix" else ():
            there = (me + k) % count
            rides.append(
                send(
                    ride_refs[i].at[there],
                    ride_outs[i].at[me],
                    ride_send.at[i, k - 1],
                    ride_recv.at[i, k - 1],
                    (there, plane),
                )
            )
        if kind == "swap":
            swaps.append(
                swap_begin(
                    ride_refs[i],
                    ride_outs[i],
                    ride_send.at[i, 0],
                    ride_recv.at[i, 0],
                    partner,
                    away,
                )
            )
        for j in range(1, ring) if kind not in ("mix", "swap") else ():
            there = (plane + j) % ring
            if kind == "sum0":
                source, target = ride_refs[i].at[there], land_refs[i].at[j - 1]
            elif kind == "sum1":
                source, target = ride_refs[i].at[:, there], land_refs[i].at[j - 1]
            elif kind == "get0":
                source, target = ride_refs[i], ride_outs[i].at[plane]
            elif kind == "hop":
                source, target = ride_refs[i].at[there], ride_outs[i].at[plane]
            else:
                source, target = ride_refs[i], ride_outs[i].at[:, plane]
            rides.append(
                send(source, target, ride_send.at[i, j - 1], ride_recv.at[i, j - 1], (me, there))
            )
        if kind not in ("sum0", "sum1", "swap"):
            if kind == "mix":
                source, target = ride_refs[i].at[me], ride_outs[i].at[me]
            elif kind == "hop":
                source, target = ride_refs[i].at[plane], ride_outs[i].at[plane]
            elif kind == "get0":
                source, target = ride_refs[i], ride_outs[i].at[plane]
            else:
                source, target = ride_refs[i], ride_outs[i].at[:, plane]
            stay = pltpu.make_async_copy(source, target, ride_own.at[i])
            stay.start()
            stays.append(stay)
    pending += rides

    if reduce:
        side = []
        for j in range(half):
            where = (chip + j + 1) % half
            side.append(
                send(
                    partial_ref.at[2 * where + (1 - core)],
                    side_ref.at[j],
                    side_send.at[j],
                    side_recv.at[j],
                    (sibling, plane),
                )
            )
        far = []
        for j in range(1, half):
            target, where = others[j - 1]
            side[j - 1].wait_recv()
            out_ref[j - 1] = (
                partial_ref[2 * where + core].astype(F32) + side_ref[j - 1].astype(F32)
            ).astype(BF16)
            far.append(
                send(
                    out_ref.at[j - 1],
                    in_ref.at[j - 1],
                    far_send.at[j - 1],
                    far_recv.at[j - 1],
                    (target, plane),
                )
            )
        side[half - 1].wait_recv()
        total = partial_ref[me].astype(F32) + side_ref[half - 1].astype(F32)
        for j in range(1, half):
            far[j - 1].wait_recv()
            total = total + in_ref[j - 1].astype(F32)
        pending += side + far
    if mode == "norm":
        value = base_ref[...] + total
        new_ref[...] = value
        unit, _ = norm_parts(value)
        result = unit * gain_ref[...] + shift_ref[...]
    elif mode == "back":
        unit, inverse = norm_parts(saved_ref[...].astype(F32))
        stat_ref[0:1, :] = jnp.sum(total * unit, axis=0, keepdims=True)
        stat_ref[1:2, :] = jnp.sum(total, axis=0, keepdims=True)
        result = base_ref[...] + norm_backward(total, unit, inverse, gain_ref[...])
        new_ref[...] = result
    elif mode == "plain":
        result = base_ref[...]
        if reduce:
            result = result + total
            new_ref[...] = result

    if gather:
        full_ref[me] = result.astype(BF16)
        sends = gather_begin(count, me, plane, full_ref, gather_send, gather_recv)
        pending += gather_end(count, me, plane, full_ref, sends, pass_send, pass_recv)
    for copy in rides:
        copy.wait_recv()
    for copy in stays:
        copy.wait()
    for swap in swaps:
        swap_end(swap)
    for i, kind in enumerate(kinds):
        if kind not in ("sum0", "sum1"):
            continue
        steps = ride_outs[i].shape[0]
        chunk = 1 if kind == "sum1" else min(steps, 32)

        def add(step, carry, i=i, kind=kind, chunk=chunk):
            at = pl.ds(pl.multiple_of(step * chunk, chunk), chunk)
            own = ride_refs[i][plane, at] if kind == "sum0" else ride_refs[i][at, plane]
            total = own.astype(F32)
            for j in range(1, ring):
                total = total + land_refs[i][j - 1, at].astype(F32)
            ride_outs[i][at] = total.astype(ride_outs[i].dtype)
            return carry

        lax.fori_loop(0, steps // chunk, add, 0)
    for copy in pending:
        copy.wait_send()


def plane_exchange(
    count,
    ring,
    call_id,
    partial=None,
    base=None,
    gains=None,
    shifts=None,
    saved=None,
    gather=True,
    sums=(),
    gets=(),
    mixes=(),
    hops=(),
    swaps=(),
):
    reduce = partial is not None
    mode = "none" if base is None else "plain"
    if gains is not None:
        mode = "norm" if saved is None else "back"
    half = count // 2
    operands = [partial] if reduce else []
    if base is not None:
        operands.append(base)
        rows, width = base.shape
    if gains is not None:
        operands.append(gains.reshape(1, width))
    if mode == "norm":
        operands.append(shifts.reshape(1, width))
    if mode == "back":
        operands.append(saved)
    operands += sums
    specs = [pl.BlockSpec(memory_space=VMEM)] * len(operands)
    operands += list(gets) + list(mixes) + list(hops) + list(swaps)
    specs += [pl.BlockSpec(memory_space=pl.ANY)] * (len(operands) - len(specs))
    kinds = tuple("sum" + str(x.ndim - 3) for x in sums)
    kinds += tuple("get" + str(x.ndim - 2) for x in gets)
    kinds += ("mix",) * len(mixes) + ("hop",) * len(hops) + ("swap",) * len(swaps)
    outs, scratch = [], []
    if gather:
        outs.append(jax.ShapeDtypeStruct((count, rows, width), BF16))
    if reduce:
        outs.append(jax.ShapeDtypeStruct((rows, width), F32))
    if mode == "back":
        outs.append(jax.ShapeDtypeStruct((8, width), F32))
    lands = [x.shape[1:] if x.ndim == 3 else x.shape[:1] + x.shape[2:] for x in sums]
    outs += [
        jax.ShapeDtypeStruct(land, F32 if x.ndim == 3 else BF16) for land, x in zip(lands, sums)
    ]
    out_specs = [pl.BlockSpec(memory_space=VMEM)] * len(outs)
    outs += [
        jax.ShapeDtypeStruct((ring,) + x.shape if x.ndim == 2 else (count, ring) + x.shape[1:], BF16)
        for x in gets
    ]
    outs += [jax.ShapeDtypeStruct(x.shape, x.dtype) for x in list(mixes) + list(hops) + list(swaps)]
    out_specs += [pl.BlockSpec(memory_space=pl.ANY)] * (len(outs) - len(out_specs))
    dma = pltpu.SemaphoreType.DMA
    if reduce:
        scratch += [
            VMEM((half, rows, width), BF16),
            VMEM((half - 1, rows, width), BF16),
            VMEM((half - 1, rows, width), BF16),
            dma((half,)),
            dma((half,)),
            dma((half - 1,)),
            dma((half - 1,)),
        ]
    if gather:
        scratch += [dma((half,)), dma((half,)), dma((half - 1,)), dma((half - 1,))]
    scratch += [VMEM((ring - 1,) + land, BF16) for land in lands]
    if kinds:
        most = max(ring, count if mixes else 0) - 1
        scratch += [dma((len(kinds), most)), dma((len(kinds), most)), dma((len(kinds),))]
    return pl.pallas_call(
        functools.partial(plane_kernel, count, ring, reduce, mode, gather, kinds),
        out_shape=tuple(outs),
        in_specs=specs,
        out_specs=tuple(out_specs),
        scratch_shapes=scratch,
        compiler_params=pltpu.CompilerParams(
            collective_id=call_id, has_side_effects=True, vmem_limit_bytes=40 * 1024 * 1024
        ),
        cost_estimate=pl.CostEstimate(
            flops=0, bytes_accessed=(60 if reduce else 30) << 20, transcendentals=0
        ),
    )(*operands)


def relay(source, target, sems, where, begin):
    copy = pltpu.make_async_remote_copy(
        src_ref=source,
        dst_ref=target,
        send_sem=sems[0],
        recv_sem=sems[1],
        device_id=where,
        device_id_type=MESH,
    )
    if begin:
        copy.start()
    return copy


def relay_begin(ring, me, plane, own, place, send_sem, recv_sem):
    for side, shift in ((0, 1), (1, -1)):
        there = (me, (plane + ring + shift) % ring)
        sems = (send_sem.at[side, 0], recv_sem.at[side, 0])

        @pl.when(plane < ring - 1 if side == 0 else plane > 0)
        def _(there=there, sems=sems):
            relay(own, place(plane), sems, there, True)


def relay_step(ring, me, plane, step, place, send_sem, recv_sem):
    for side, shift in ((0, 1), (1, -1)):
        there = (me, (plane + ring + shift) % ring)
        origin = (plane + ring - shift * step) % ring
        came = plane >= step if side == 0 else plane < ring - step
        more = plane < ring - 1 if side == 0 else plane > 0

        @pl.when(came)
        def _(side=side, there=there, origin=origin):
            block = place(origin)
            sems = (send_sem.at[side, step - 1], recv_sem.at[side, step - 1])
            relay(block, block, sems, there, False).wait_recv()

        if step < ring - 1:

            @pl.when(jnp.logical_and(came, more))
            def _(side=side, there=there, origin=origin):
                block = place(origin)
                sems = (send_sem.at[side, step], recv_sem.at[side, step])
                relay(block, block, sems, there, True)


def relay_end(ring, me, plane, place, send_sem, recv_sem):
    for step in range(ring - 1):
        for side, shift in ((0, 1), (1, -1)):
            there = (me, (plane + ring + shift) % ring)
            came = plane >= step if side == 0 else plane < ring - step
            more = plane < ring - 1 if side == 0 else plane > 0

            @pl.when(jnp.logical_and(came, more))
            def _(side=side, there=there):
                block = place(plane)
                sems = (send_sem.at[side, step], recv_sem.at[side, step])
                relay(block, block, sems, there, False).wait_send()


def first_kernel(count, ring, layers, talls, *refs):
    refs = list(refs)
    token_ref, small_ref, served_ref, flag_ref = (refs.pop(0) for _ in range(4))
    column_refs = [refs.pop(0) for _ in range(2)]
    tall_refs = [refs.pop(0) for _ in range(talls)]
    full_ref, vector_ref, rows_ref, flags_ref = (refs.pop(0) for _ in range(4))
    wide_refs = [[refs.pop(0) for _ in range(layers)] for _ in range(2)]
    whole_refs = [refs.pop(0) for _ in range(talls)]
    small_all = refs.pop(0)
    column_all = [refs.pop(0) for _ in range(2)]
    own_sem = refs.pop(0)
    (
        gather_send,
        gather_recv,
        pass_send,
        pass_recv,
        small_send,
        small_recv,
        across_send,
        across_recv,
        column_send,
        column_recv,
        relay_send,
        relay_recv,
        flag_send,
        flag_recv,
        rows_send,
        rows_recv,
    ) = refs
    me = lax.axis_index("dp")
    plane = lax.axis_index("ctx")
    mates = [(me + k) % count for k in range(1, count)]
    planes = [(plane + j) % ring for j in range(1, ring)]
    greet_all([(mate, plane) for mate in mates] + [(me, there) for there in planes])

    stays = []

    def stay(source, target):
        copy = pltpu.make_async_copy(source, target, own_sem.at[len(stays)])
        copy.start()
        stays.append(copy)

    small_all[me, plane] = small_ref[...]
    smalls = [
        send(small_ref, small_all.at[me, plane], small_send.at[k], small_recv.at[k], (mate, plane))
        for k, mate in enumerate(mates)
    ]
    columns = []
    for i in range(2):
        stay(column_refs[i].at[me], column_all[i].at[me])
        for k, mate in enumerate(mates):
            columns.append(
                send(
                    column_refs[i].at[mate],
                    column_all[i].at[me],
                    column_send.at[i, k],
                    column_recv.at[i, k],
                    (mate, plane),
                )
            )
    column_stays = stays[:]
    pending = smalls + columns
    late = []
    for j, there in enumerate(planes):
        late.append(
            send(
                flag_ref.at[there],
                flags_ref.at[plane],
                flag_send.at[j],
                flag_recv.at[j],
                (me, there),
            )
        )
    flags_ref[plane] = flag_ref[plane]
    for copy in smalls:
        copy.wait_recv()
    across = [
        send(
            small_all.at[:, plane],
            small_all.at[:, plane],
            across_send.at[j],
            across_recv.at[j],
            (me, there),
        )
        for j, there in enumerate(planes)
    ]

    relays = []

    def spread(own, place):
        n = len(relays)
        relays.append((place, relay_send.at[n], relay_recv.at[n]))
        stay(own, place(plane))
        relay_begin(ring, me, plane, own, *relays[-1])

    def spread_tall(i):
        spread(tall_refs[i], lambda p: whole_refs[i].at[p])

    for i in range(2):
        spread_tall(i)
    for copy in across:
        copy.wait_recv()
    groups = vector_ref.shape[1] // 128
    members = count * ring // groups
    for group in range(groups):
        total = small_all[group * members // ring, group * members % ring]
        for n in range(group * members + 1, (group + 1) * members):
            total = total + small_all[n // ring, n % ring]
        vector_ref[:, group * 128 : (group + 1) * 128] = total
    unit, _ = norm_parts(token_ref[...].astype(F32))
    full_ref[me] = (unit * vector_ref[0:1, :] + vector_ref[1:2, :]).astype(BF16)
    sends = gather_begin(count, me, plane, full_ref, gather_send, gather_recv)
    for copy in columns:
        copy.wait_recv()
    for copy in column_stays:
        copy.wait()
    for layer in range(layers):
        for i in range(2):
            spread(
                column_all[i].at[:, layer],
                lambda p, layer=layer, i=i: wide_refs[i][layer].at[:, p],
            )
    for i in range(2, talls):
        spread_tall(i)
    for k, mate in enumerate(mates):
        late.append(
            send(
                served_ref.at[mate],
                rows_ref.at[me],
                rows_send.at[k],
                rows_recv.at[k],
                (mate, plane),
            )
        )
    stay(served_ref.at[me], rows_ref.at[me])
    pending += gather_end(count, me, plane, full_ref, sends, pass_send, pass_recv)
    for step in range(1, ring):
        for one in relays:
            relay_step(ring, me, plane, step, *one)
    for copy in late:
        copy.wait_recv()
    for copy in stays[len(column_stays) :]:
        copy.wait()
    for copy in pending + across + late:
        copy.wait_send()
    for one in relays:
        relay_end(ring, me, plane, *one)


def first_exchange(count, ring, call_id, tokens, small, served, flags, joint, expand, talls):
    rows, width = tokens.shape
    layers, half = joint.shape[1], count // 2
    dma = pltpu.SemaphoreType.DMA
    near, far = pl.BlockSpec(memory_space=VMEM), pl.BlockSpec(memory_space=pl.ANY)
    outs = [
        jax.ShapeDtypeStruct((count, rows, width), BF16),
        jax.ShapeDtypeStruct((16, width), F32),
        jax.ShapeDtypeStruct(served.shape, BF16),
        jax.ShapeDtypeStruct(flags.shape, flags.dtype),
    ]
    for x in (joint, expand):
        outs += [jax.ShapeDtypeStruct((count, ring) + x.shape[2:], BF16)] * layers
    outs += [jax.ShapeDtypeStruct((ring,) + x.shape, BF16) for x in talls]

    def pair(*shape):
        return [dma(shape), dma(shape)]

    return pl.pallas_call(
        functools.partial(first_kernel, count, ring, layers, len(talls)),
        out_shape=tuple(outs),
        in_specs=[near, near, far, near, near, near] + [far] * len(talls),
        out_specs=tuple([near, near, far, near] + [far] * (2 * layers + len(talls))),
        scratch_shapes=[
            VMEM((count, ring, 16, 128), F32),
            VMEM(joint.shape, BF16),
            VMEM(expand.shape, BF16),
            dma((3 + 2 * layers + len(talls),)),
        ]
        + pair(half)
        + pair(half - 1)
        + pair(count - 1)
        + pair(ring - 1)
        + pair(2, count - 1)
        + pair(2 * layers + len(talls), 2, ring - 1)
        + pair(ring - 1)
        + pair(count - 1),
        compiler_params=pltpu.CompilerParams(
            collective_id=call_id, has_side_effects=True, vmem_limit_bytes=40 * 1024 * 1024
        ),
        cost_estimate=pl.CostEstimate(flops=0, bytes_accessed=200 << 20, transcendentals=0),
    )(tokens, small, served, flags, joint, expand, *talls)


def last_kernel(
    count,
    ring,
    layers,
    sums_ref,
    wide_ref,
    rows_ref,
    *refs,
):
    refs = list(refs)
    joint_refs = [refs.pop(0) for _ in range(layers - 1)]
    expand_refs = [refs.pop(0) for _ in range(layers)]
    total_ref, joint_grad_ref, expand_grad_ref, home_ref = (refs.pop(0) for _ in range(4))
    sums_in, across_ref, mixed_ref, rows_in = (refs.pop(0) for _ in range(4))
    (
        own_sem,
        swap_send,
        swap_recv,
        sums_send,
        sums_recv,
        wide_send,
        wide_recv,
        across_send,
        across_recv,
    ) = refs
    me = lax.axis_index("dp")
    plane = lax.axis_index("ctx")
    partner, away = partner_of(me, plane, ring)
    greet = [((me + k) % count, plane) for k in range(1, count)]
    greet += [(me, (plane + j) % ring) for j in range(1, ring)]
    greet_all(greet, partner, away)

    pending, sums = [], []
    for k in range(1, count):
        there = (me + k) % count
        sums.append(
            send(
                sums_ref.at[there],
                sums_in.at[me],
                sums_send.at[k - 1],
                sums_recv.at[k - 1],
                (there, plane),
            )
        )
    swap = swap_begin(rows_ref, rows_in, swap_send, swap_recv, partner, away)
    for k in range(1, count):
        there = (me + k) % count
        pending.append(
            send(
                wide_ref.at[there],
                mixed_ref.at[me],
                wide_send.at[k - 1],
                wide_recv.at[k - 1],
                (there, plane),
            )
        )
    sums_in[me] = sums_ref[me]
    stay = pltpu.make_async_copy(wide_ref.at[me], mixed_ref.at[me], own_sem)
    stay.start()
    for copy in sums:
        copy.wait_recv()
    total = sums_in[0]
    for k in range(1, count):
        total = total + sums_in[k]
    across_ref[plane] = total
    across = [
        send(
            across_ref.at[plane],
            across_ref.at[plane],
            across_send.at[j - 1],
            across_recv.at[j - 1],
            (me, (plane + j) % ring),
        )
        for j in range(1, ring)
    ]
    inner = expand_refs[0].shape[2]
    size = wide_ref.shape[2] // 3
    for layer in range(layers):
        for k in range(count):
            expand_grad_ref[layer, :, k * inner : (k + 1) * inner] = expand_refs[layer][k].astype(F32)

    def spread(layer, ref):
        for k in range(count):
            for i in range(3):
                at = (i * count + k) * size
                joint_grad_ref[layer, :, at : at + size] = ref[
                    k, :, i * size : (i + 1) * size
                ].astype(F32)

    for layer in range(1, layers):
        spread(layer, joint_refs[layer - 1])
    for copy in across:
        copy.wait_recv()
    total = across_ref[0]
    for j in range(1, ring):
        total = total + across_ref[j]
    total_ref[...] = total
    for copy in pending:
        copy.wait_recv()
    stay.wait()
    spread(0, mixed_ref)
    swap_end(swap)
    home_ref[...] = rows_in[...].astype(F32)
    for copy in pending + sums + across:
        copy.wait_send()


def last_exchange(count, ring, call_id, sums, wide, rows, joints, expands):
    dma = pltpu.SemaphoreType.DMA
    layers = len(expands)
    part = wide.shape[1]
    operands = (sums, wide, rows, *joints, *expands)
    outs = (
        jax.ShapeDtypeStruct(sums.shape[1:], F32),
        jax.ShapeDtypeStruct((layers, part, count * wide.shape[2]), F32),
        jax.ShapeDtypeStruct((layers, part, count * expands[0].shape[2]), F32),
        jax.ShapeDtypeStruct(rows.shape, F32),
    )
    spec = pl.BlockSpec(memory_space=VMEM)
    return pl.pallas_call(
        functools.partial(last_kernel, count, ring, layers),
        out_shape=outs,
        in_specs=[spec] * len(operands),
        out_specs=(spec,) * len(outs),
        scratch_shapes=[
            VMEM(sums.shape, F32),
            VMEM((ring,) + sums.shape[1:], F32),
            VMEM(wide.shape, BF16),
            VMEM(rows.shape, BF16),
            dma,
            dma,
            dma,
            dma((count - 1,)),
            dma((count - 1,)),
            dma((count - 1,)),
            dma((count - 1,)),
            dma((ring - 1,)),
            dma((ring - 1,)),
        ],
        compiler_params=pltpu.CompilerParams(
            collective_id=call_id, has_side_effects=True, vmem_limit_bytes=40 * 1024 * 1024
        ),
    )(*operands)


GATE_SCALE = math.sqrt(2.0 / math.pi)
GATE_CUBE = 0.044715


def after(*arrays):
    return lax.optimization_barrier(arrays)


def dot(left, right):
    return jnp.dot(left, right, preferred_element_type=F32)


def contract_rows(left, right):
    return lax.dot_general(left, right, (((0,), (0,)), ((), ())), preferred_element_type=F32)


def contract_cols(left, right):
    return lax.dot_general(left, right, (((1,), (1,)), ((), ())), preferred_element_type=F32)


def local_call(body, outs, operands, grid, in_specs, out_specs, scratch=(), flops=0):
    moved = sum(math.prod(x.shape) * x.dtype.itemsize for x in list(operands) + list(outs))
    return pl.pallas_call(
        body,
        out_shape=tuple(outs),
        grid=grid,
        in_specs=in_specs,
        out_specs=tuple(out_specs),
        scratch_shapes=list(scratch),
        compiler_params=pltpu.CompilerParams(vmem_limit_bytes=48 * 1024 * 1024),
        cost_estimate=pl.CostEstimate(flops=flops, bytes_accessed=moved, transcendentals=0),
    )(*operands)


def whole(x):
    return pl.BlockSpec(x.shape, lambda *_, n=len(x.shape): (0,) * n)


def stripe(shape):
    return pl.BlockSpec(shape, lambda i: (i,) + (0,) * (len(shape) - 1))


def probabilities(queries, keys, begin):
    scores = contract_cols(queries, keys) * (queries.shape[-1] ** (-0.5))
    row = begin + lax.broadcasted_iota(jnp.int32, scores.shape, 0)
    allowed = row >= lax.broadcasted_iota(jnp.int32, scores.shape, 1)
    scores = jnp.where(allowed, scores, FLOOR)
    raised = jnp.exp(scores - jnp.max(scores, axis=-1, keepdims=True))
    return raised / jnp.sum(raised, axis=-1, keepdims=True)


def attend_kernel(heads, block, x_ref, joint_ref, project_ref, packed_ref, attended_ref, partial_ref):
    packed_ref[...] = dot(x_ref[...], joint_ref[...]).astype(BF16)
    length, width = attended_ref.shape
    size = width // heads
    for head in range(heads):
        at = head * size
        for begin in range(0, length, block):
            end = begin + block
            probs = probabilities(
                packed_ref[begin:end, at : at + size], packed_ref[:end, width + at : width + at + size], begin
            )
            values = packed_ref[:end, 2 * width + at : 2 * width + at + size]
            attended_ref[begin:end, at : at + size] = dot(probs.astype(BF16), values).astype(BF16)
    partial_ref[...] = dot(attended_ref[...], project_ref[...]).astype(BF16)


def attend(normed, joint, project, seqs, heads):
    rows, width = normed.shape
    length, inner = rows // seqs, project.shape[0]
    outs = [
        jax.ShapeDtypeStruct((rows, 3 * inner), BF16),
        jax.ShapeDtypeStruct((rows, inner), BF16),
        jax.ShapeDtypeStruct((rows, width), BF16),
    ]
    return local_call(
        functools.partial(attend_kernel, heads, min(256, length)),
        outs,
        (normed, joint, project),
        (seqs,),
        [stripe((length, width)), whole(joint), whole(project)],
        [stripe((length, 3 * inner)), stripe((length, inner)), stripe((length, width))],
        flops=8 * rows * width * inner,
    )


def attend_backward_kernel(
    heads,
    block,
    grad_ref,
    x_ref,
    packed_ref,
    attended_ref,
    joint_ref,
    project_ref,
    joint_grad_ref,
    project_grad_ref,
    partial_ref,
    joint_sum,
    project_sum,
    key_sum,
    value_sum,
    low_ref,
):
    step = pl.program_id(0)
    length, width = attended_ref.shape
    size = width // heads
    scale = size ** (-0.5)
    grad = contract_cols(grad_ref[...], project_ref[...]).astype(BF16)
    key_sum[...] = jnp.zeros_like(key_sum)
    value_sum[...] = jnp.zeros_like(value_sum)
    for head in range(heads):
        at = head * size
        for begin in range(0, length, block):
            end = begin + block
            queries = packed_ref[begin:end, at : at + size]
            keys = packed_ref[:end, width + at : width + at + size]
            values = packed_ref[:end, 2 * width + at : 2 * width + at + size]
            here = grad[begin:end, at : at + size]
            probs = probabilities(queries, keys, begin)
            grad_probs = contract_cols(here, values)
            delta = jnp.sum(probs * grad_probs, axis=-1, keepdims=True)
            grad_scores = (probs * (grad_probs - delta)).astype(BF16)
            low_ref[begin:end, at : at + size] = (dot(grad_scores, keys) * scale).astype(BF16)
            key_sum[:end, at : at + size] += contract_rows(grad_scores, queries) * scale
            value_sum[:end, at : at + size] += contract_rows(probs.astype(BF16), here)
    low_ref[:, width : 2 * width] = key_sum[...].astype(BF16)
    low_ref[:, 2 * width :] = value_sum[...].astype(BF16)
    partial_ref[...] = contract_cols(low_ref[...], joint_ref[...]).astype(BF16)
    joint_part = contract_rows(x_ref[...], low_ref[...])
    project_part = contract_rows(attended_ref[...], grad_ref[...])

    @pl.when(step == 0)
    def _():
        joint_sum[...] = joint_part
        project_sum[...] = project_part

    @pl.when(step > 0)
    def _():
        joint_sum[...] += joint_part
        project_sum[...] += project_part

    @pl.when(step == pl.num_programs(0) - 1)
    def _():
        joint_grad_ref[...] = joint_sum[...].astype(BF16)
        project_grad_ref[...] = project_sum[...].astype(BF16)


def attend_backward(grad_out, normed, packed, attended, joint, project, seqs, heads):
    rows, width = normed.shape
    length, inner = rows // seqs, project.shape[0]
    outs = [
        jax.ShapeDtypeStruct(joint.shape, BF16),
        jax.ShapeDtypeStruct(project.shape, BF16),
        jax.ShapeDtypeStruct((rows, width), BF16),
    ]
    return local_call(
        functools.partial(attend_backward_kernel, heads, min(256, length)),
        outs,
        (grad_out, normed, packed, attended, joint, project),
        (seqs,),
        [
            stripe((length, width)),
            stripe((length, width)),
            stripe((length, 3 * inner)),
            stripe((length, inner)),
            whole(joint),
            whole(project),
        ],
        [whole(outs[0]), whole(outs[1]), stripe((length, width))],
        [
            VMEM(joint.shape, F32),
            VMEM(project.shape, F32),
            VMEM((length, inner), F32),
            VMEM((length, inner), F32),
            VMEM((length, 3 * inner), BF16),
        ],
        flops=16 * rows * width * inner,
    )


def forward_kernel(x_ref, expand_ref, shrink_ref, inner_ref, partial_ref):
    inner = dot(x_ref[...], expand_ref[...])
    inner_ref[...] = inner
    turn = jnp.tanh(GATE_SCALE * (inner + GATE_CUBE * (inner * inner * inner)))
    active = (0.5 * inner * (1.0 + turn)).astype(BF16)
    partial_ref[...] = dot(active, shrink_ref[...]).astype(BF16)


def forward(normed, expand, shrink):
    rows, width = normed.shape
    inner, block = expand.shape[1], 256
    outs = [jax.ShapeDtypeStruct((rows, inner), F32), jax.ShapeDtypeStruct((rows, width), BF16)]
    return local_call(
        forward_kernel,
        outs,
        (normed, expand, shrink),
        (rows // block,),
        [stripe((block, width)), whole(expand), whole(shrink)],
        [stripe((block, inner)), stripe((block, width))],
        flops=4 * rows * width * inner,
    )


def backward_kernel(
    branch_ref,
    x_ref,
    inner_ref,
    expand_ref,
    shrink_ref,
    expand_grad_ref,
    shrink_grad_ref,
    partial_ref,
    expand_sum,
    shrink_sum,
):
    step = pl.program_id(0)
    branch, inner = branch_ref[...], inner_ref[...]
    square = inner * inner
    turn = jnp.tanh(GATE_SCALE * (inner + GATE_CUBE * (square * inner)))
    active = (0.5 * inner * (1.0 + turn)).astype(BF16)
    slope = GATE_SCALE * (1.0 + (3.0 * GATE_CUBE) * square)
    slope = 0.5 * (1.0 + turn) + 0.5 * inner * (1.0 - turn * turn) * slope
    grad_inner = (contract_cols(branch, shrink_ref[...]) * slope).astype(BF16)
    partial_ref[...] = contract_cols(grad_inner, expand_ref[...]).astype(BF16)
    expand_part = contract_rows(x_ref[...], grad_inner)
    shrink_part = contract_rows(active, branch)

    @pl.when(step == 0)
    def _():
        expand_sum[...] = expand_part
        shrink_sum[...] = shrink_part

    @pl.when(step > 0)
    def _():
        expand_sum[...] += expand_part
        shrink_sum[...] += shrink_part

    @pl.when(step == pl.num_programs(0) - 1)
    def _():
        expand_grad_ref[...] = expand_sum[...].astype(BF16)
        shrink_grad_ref[...] = shrink_sum[...].astype(BF16)


def backward(branch, normed, inner, expand, shrink):
    rows, width = normed.shape
    block = 256
    outs = [
        jax.ShapeDtypeStruct(expand.shape, BF16),
        jax.ShapeDtypeStruct(shrink.shape, BF16),
        jax.ShapeDtypeStruct((rows, width), BF16),
    ]
    return local_call(
        backward_kernel,
        outs,
        (branch, normed, inner, expand, shrink),
        (rows // block,),
        [
            stripe((block, width)),
            stripe((block, width)),
            stripe((block, inner.shape[1])),
            whole(expand),
            whole(shrink),
        ],
        [whole(outs[0]), whole(outs[1]), stripe((block, width))],
        [VMEM(expand.shape, F32), VMEM(shrink.shape, F32)],
        flops=8 * rows * width * inner.shape[1],
    )


def ranks_of(flags):
    planes, groups, rows = flags.shape
    upto = jnp.arange(rows)[:, None] <= jnp.arange(rows)[None, :]
    inside = dot(flags.astype(BF16), upto.astype(BF16))
    before = jnp.where(
        jnp.arange(groups)[None, :, None] < jnp.arange(groups)[None, None, :],
        inside[:, :, -1:],
        0.0,
    )
    rank = inside + jnp.sum(before, axis=1)[:, :, None]
    return rank.reshape(planes, groups * rows), rank[:, -1, -1]


def pieces_of(values, terms):
    pieces = []
    for _ in range(terms):
        pieces.append(values.astype(BF16))
        values = values - pieces[-1].astype(F32)
    return jnp.concatenate(pieces, axis=0)


def recall_kernel(
    tile,
    hidden_ref,
    vector_ref,
    cotangent_ref,
    token_ref,
    stored_ref,
    mixed_ref,
    grad_ref,
    sums_ref,
    scaled_ref,
    pull_ref,
):
    rows, width = hidden_ref.shape
    tiles = stored_ref.shape[0] // tile
    unit, inverse = norm_parts(hidden_ref[...])
    gains = vector_ref[8:9, :]
    query = unit * gains + vector_ref[9:10, :]
    scale = DISTANCE_SCALE * math.sqrt(width)
    terms = jnp.concatenate([pieces_of(query, 3), cotangent_ref[...]], axis=0)
    ones = jnp.ones((8, width), BF16)

    def look(n, carry):
        at = pl.ds(pl.multiple_of(n * tile, tile), tile)
        stored = stored_ref[at, :]
        near = contract_cols(terms, stored)
        squares = jnp.square(stored.astype(F32))
        high = squares.astype(BF16)
        low = (squares - high.astype(F32)).astype(BF16)
        lengths = (contract_cols(ones, high) + contract_cols(ones, low))[0:1, :]
        scaled_ref[:, at] = (
            2.0 * (near[:rows] + (near[rows : 2 * rows] + near[2 * rows : 3 * rows])) - lengths
        ) / scale
        pull_ref[:, at] = RECALL_SHARE * near[3 * rows :]
        return carry

    lax.fori_loop(0, tiles, look, 0)
    usable = token_ref[...] == lax.broadcasted_iota(jnp.int32, scaled_ref.shape, 0)
    scaled = jnp.where(usable, scaled_ref[...], FLOOR)
    raised = jnp.where(usable, jnp.exp(scaled - jnp.max(scaled, axis=1, keepdims=True)), 0.0)
    weights = raised / jnp.sum(raised, axis=1, keepdims=True)
    pull = pull_ref[...]
    grad_scaled = weights * (pull - jnp.sum(weights * pull, axis=1, keepdims=True))
    scaled_ref[...] = weights
    pull_ref[...] = grad_scaled
    rest = jnp.sum(grad_scaled, axis=1, keepdims=True)

    def gather(n, total):
        at = pl.ds(pl.multiple_of(n * tile, tile), tile)
        both = jnp.concatenate(
            [pieces_of(scaled_ref[:, at], 2), pieces_of(pull_ref[:, at], 2)], axis=0
        )
        return total + dot(both, stored_ref[at, :])

    total = lax.fori_loop(0, tiles, gather, jnp.zeros((4 * rows, width), F32))
    recalled = total[:rows] + total[rows : 2 * rows]
    moved = total[2 * rows : 3 * rows] + total[3 * rows :] - rest * query
    mixed_ref[...] = (1.0 - RECALL_SHARE) * query + RECALL_SHARE * recalled
    grad_query = (1.0 - RECALL_SHARE) * cotangent_ref[...].astype(F32) + moved * (2.0 / scale)
    sums_ref[0:1, :] = jnp.sum(grad_query * unit, axis=0, keepdims=True)
    sums_ref[1:2, :] = jnp.sum(grad_query, axis=0, keepdims=True)
    grad_ref[...] = norm_backward(grad_query, unit, inverse, gains)


def recall_padded(hidden, vectors, stored, usable, cotangent):
    unit, inverse = norm_parts(hidden)
    query = unit * vectors[8] + vectors[9]
    scale = DISTANCE_SCALE * math.sqrt(query.shape[-1])
    stored, cotangent = stored.astype(F32), cotangent.astype(F32)
    distance = jnp.sum(jnp.square(query[None] - stored), axis=-1)
    pull = RECALL_SHARE * jnp.sum(cotangent[None] * stored, axis=-1)
    scaled = jnp.where(usable, -distance / scale, FLOOR)
    raised = jnp.where(usable, jnp.exp(scaled - jnp.max(scaled, axis=0, keepdims=True)), 0.0)
    weights = raised / jnp.sum(raised, axis=0, keepdims=True)
    grad_scaled = weights * (pull - jnp.sum(weights * pull, axis=0, keepdims=True))
    recalled = jnp.sum(weights[..., None] * stored, axis=0)
    moved = jnp.sum(grad_scaled[..., None] * stored, axis=0)
    moved = moved - jnp.sum(grad_scaled, axis=0)[:, None] * query
    mixed = (1.0 - RECALL_SHARE) * query + RECALL_SHARE * recalled
    grad_query = (1.0 - RECALL_SHARE) * cotangent + moved * (2.0 / scale)
    sums = jnp.stack([jnp.sum(grad_query * unit, axis=0), jnp.sum(grad_query, axis=0)])
    grad = norm_backward(grad_query, unit, inverse, vectors[8])
    return mixed, grad, jnp.pad(sums, ((0, 6), (0, 0)))


def recall(hidden, vectors, stored, token_of, cotangent):
    rows, width = hidden.shape
    entries = stored.shape[0]
    operands = (hidden, vectors, cotangent, token_of.reshape(1, entries), stored)
    outs = [
        jax.ShapeDtypeStruct((rows, width), F32),
        jax.ShapeDtypeStruct((rows, width), F32),
        jax.ShapeDtypeStruct((8, width), F32),
    ]
    return local_call(
        functools.partial(recall_kernel, min(512, entries)),
        outs,
        operands,
        (1,),
        [whole(x) for x in operands],
        [whole(x) for x in outs],
        [VMEM((rows, entries), F32), VMEM((rows, entries), F32)],
        flops=16 * rows * width * entries,
    )


def shards(
    tokens,
    ln1_gain,
    ln1_bias,
    qkv_weight,
    out_weight,
    ln2_gain,
    ln2_bias,
    in_weight,
    fc_weight,
    final_gain,
    final_bias,
    datastore,
    neighbour_owner,
    neighbour_row,
    neighbour_count,
    cotangent,
):
    local_seqs, local_rows, width = tokens.shape
    rows = local_seqs * local_rows
    count, ring = lax.axis_size("dp"), lax.axis_size("ctx")
    devices = count * ring
    both = ("dp", "ctx")
    seqs = count * local_seqs // ring
    heads = HEADS // count
    slots = neighbour_owner.shape[2]
    part = width // devices
    head_width = width // count
    inner_width = in_weight.shape[2] // count

    forth = []
    for s in range(count):
        for p in range(ring):
            forth.append((s * ring + p, ((s // ring) * ring + p) * ring + s % ring))

    pair_room = -(-(3 * rows * slots) // (2 * devices * 16)) * 16
    room = rows * slots // ring
    owners = neighbour_owner.reshape(rows, slots)
    live = neighbour_count.reshape(rows, 1)
    hits = (owners[:, :, None] == jnp.arange(devices)[None, None, :]) & (
        jnp.arange(slots)[None, :, None] < live[:, :, None]
    )
    asked_all = jnp.sum(jnp.where(hits, neighbour_row.reshape(rows, slots, 1), 0), axis=1).T
    usable_all = jnp.any(hits, axis=1).T
    upto = jnp.arange(rows)[:, None] <= jnp.arange(rows)[None, :]
    order = dot(usable_all.astype(BF16), upto.astype(BF16))
    taken = usable_all[:, None, :] & (
        order[:, None, :] == jnp.arange(1, pair_room + 1, dtype=F32)[None, :, None]
    )
    asked = jnp.sum(jnp.where(taken, asked_all[:, None, :], 0), axis=-1)
    asked = lax.all_to_all(asked, both, split_axis=0, concat_axis=0, tiled=True)
    asked = asked.reshape(count // ring, ring, ring, pair_room).swapaxes(1, 2)

    def by_plane(x):
        return x.reshape((count, ring) + x.shape[1:]).swapaxes(0, 1)

    token_at = by_plane(jnp.sum(jnp.where(taken, jnp.arange(rows)[None, None, :], 0), axis=-1))
    amounts = order[:, -1]
    usable = by_plane(jnp.arange(pair_room, dtype=F32)[None, :] < amounts[:, None])
    crowded = (jnp.max(amounts) > pair_room) | (jnp.max(jnp.sum(by_plane(amounts), axis=1)) > room)

    small = jnp.stack(
        [ln1_gain[0], ln1_bias[0], ln1_gain[1], ln1_bias[1], ln2_gain[0], ln2_bias[0]]
        + [ln2_gain[1], ln2_bias[1], final_gain, final_bias]
    ).astype(F32)
    small = jnp.concatenate([small, jnp.broadcast_to(crowded.astype(F32), (1, part))])
    here = lax.axis_index("dp") * ring + lax.axis_index("ctx")
    places = 128 // part
    small = jnp.tile(jnp.pad(small, ((0, 5), (0, 0))), (1, places))
    small = jnp.where(jnp.arange(128)[None, :] // part == here % places, small, 0.0)

    joint_own = qkv_weight.reshape(LAYERS, part, 3, count, head_width).transpose(3, 0, 1, 2, 4)
    joint_own = joint_own.reshape(count, LAYERS, part, 3 * head_width)
    expand_own = in_weight.reshape(LAYERS, part, count, inner_width).transpose(2, 0, 1, 3)

    notes = jnp.concatenate([usable.astype(jnp.int32), token_at], axis=-1)
    my_tokens, notes, asked = after(tokens.reshape(rows, width), notes, asked)
    served = datastore.at[asked.reshape(-1)].get(mode="promise_in_bounds")
    my_tokens = lax.ppermute(my_tokens, both, forth)
    notes = lax.ppermute(notes, both, forth)
    usable, token_at = notes[..., :pair_room], notes[..., pair_room:]
    exchange = functools.partial(plane_exchange, count, ring)
    first = first_exchange(
        count,
        ring,
        0,
        my_tokens,
        small,
        served.reshape(count, ring * pair_room, width),
        usable,
        joint_own,
        expand_own,
        (out_weight[0], fc_weight[0], out_weight[1], fc_weight[1]),
    )
    normed, vectors, served, flags = first[:4]
    joint, expand = list(first[4 : 4 + LAYERS]), list(first[4 + LAYERS : 4 + 2 * LAYERS])
    project, shrink = [first[-4], first[-2]], [first[-3], first[-1]]
    gain_one, shift_one = [vectors[0], vectors[2]], [vectors[1], vectors[3]]
    gain_two, shift_two = [vectors[4], vectors[6]], [vectors[5], vectors[7]]
    crowded = jnp.max(vectors[10]) > 0.5
    rank, _ = ranks_of(flags)
    served = served.reshape(count, ring, pair_room, width)

    def sent(begin, end):
        begin, end = begin * room // 16, end * room // 16
        chosen = flags.reshape(ring, 1, count * pair_room) * (
            rank[:, None, :] == jnp.arange(begin + 1, end + 1, dtype=F32)[None, :, None]
        )
        return jnp.einsum(
            "cpdt,dctw->cpw",
            chosen.astype(BF16).reshape(ring, end - begin, count, pair_room),
            served,
            preferred_element_type=F32,
        ).astype(BF16)

    hidden = my_tokens.astype(F32)
    saved = []
    for layer in range(LAYERS):
        normed = normed.reshape(count * rows, width)
        joint[layer] = joint[layer].reshape(width, 3 * head_width)
        project[layer] = project[layer].reshape(-1, width)
        packed, attended, partial = attend(normed, joint[layer], project[layer], seqs, heads)
        partial = partial.reshape(count, rows, width)
        gains = (gain_two[layer], shift_two[layer])
        if layer == 0:
            normed_two, middle, stored0 = exchange(
                2, partial, hidden, *gains, hops=(sent(0, 5),)
            )
        else:
            normed_two, middle, stored2 = exchange(
                3, partial, hidden, *gains, hops=(sent(11, 16),)
            )
        normed_two = normed_two.reshape(count * rows, width)
        expand[layer] = expand[layer].reshape(width, inner_width)
        shrink[layer] = shrink[layer].reshape(-1, width)
        inner, partial = forward(normed_two, expand[layer], shrink[layer])
        partial = partial.reshape(count, rows, width)
        saved.append((hidden, normed, packed, attended, middle, normed_two, inner))
        if layer + 1 < LAYERS:
            normed, hidden, stored1 = exchange(
                4,
                partial,
                middle,
                gain_one[layer + 1],
                shift_one[layer + 1],
                hops=(sent(5, 11),),
            )
        else:
            hidden, my_cotangent = exchange(
                5, partial, middle, gather=False, swaps=(cotangent.reshape(rows, width),)
            )

    def few():
        rank, _ = ranks_of(usable)
        chosen = (usable.reshape(ring, 1, -1) > 0) & (
            rank[:, None, :] == jnp.arange(1, room + 1, dtype=F32)[None, :, None]
        )
        token_of = jnp.sum(jnp.where(chosen, token_at.reshape(ring, 1, -1) + 1, 0), axis=-1) - 1
        stored = jnp.concatenate([stored0, stored1, stored2], axis=1).reshape(ring * room, width)
        return recall(hidden, vectors, stored, token_of.reshape(-1), my_cotangent)

    def many():
        asked = lax.all_to_all(asked_all, both, split_axis=0, concat_axis=0, tiled=True)
        stored = datastore.at[asked.reshape(-1)].get(mode="promise_in_bounds")
        stored = stored.reshape(devices, rows, width)
        stored = lax.all_to_all(stored, both, split_axis=0, concat_axis=0, tiled=True)
        stored = lax.ppermute(stored, both, forth)
        marks = lax.ppermute(usable_all.astype(jnp.int32), both, forth)
        return recall_padded(hidden, vectors, stored, marks > 0, my_cotangent)

    mixed, grad_hidden, head_sums = lax.cond(crowded, many, few)
    branch, mixed = exchange(6, base=grad_hidden, swaps=(mixed.astype(BF16),))
    sums_one, sums_two = [None] * LAYERS, [None] * LAYERS
    joint_sums, expand_sums = [None] * LAYERS, [None] * LAYERS
    grad_tall = [None] * LAYERS
    for layer in reversed(range(LAYERS)):
        start, normed, packed, attended, middle, normed_two, inner = saved[layer]
        grad_expand, grad_shrink, partial = backward(
            branch.reshape(count * rows, width), normed_two, inner, expand[layer], shrink[layer]
        )
        grad_expand = grad_expand.reshape(count, ring, part, inner_width)
        grad_shrink = grad_shrink.reshape(ring, -1, width)
        cut = grad_shrink.shape[1] // 2
        grad_out, grad_middle, sums_two[layer], upper_sum, expand_sum = exchange(
            7,
            partial.reshape(count, rows, width),
            grad_hidden,
            gain_two[layer],
            saved=middle,
            sums=(grad_shrink[:, :cut], grad_expand),
        )
        expand_sums[layer] = expand_sum
        grad_joint, grad_project, partial = attend_backward(
            grad_out.reshape(count * rows, width),
            normed,
            packed,
            attended,
            joint[layer],
            project[layer],
            seqs,
            heads,
        )
        rides = (
            grad_project.reshape(ring, part, width),
            grad_shrink[:, cut:],
            grad_joint.reshape(count, ring, part, 3 * head_width),
        )
        partial = partial.reshape(count, rows, width)
        if layer > 0:
            branch, grad_hidden, sums_one[layer], project_sum, lower_sum, joint_sum = exchange(
                8, partial, grad_middle, gain_one[layer], saved=start, sums=rides
            )
        else:
            grad_hidden, sums_one[layer], project_sum, lower_sum, joint_sum, *mixes = exchange(
                9,
                partial,
                grad_middle,
                gain_one[layer],
                saved=start,
                gather=False,
                sums=rides,
                mixes=tuple(joint_sums[1:]) + tuple(expand_sums),
            )
        shrink_sum = jnp.concatenate([upper_sum, lower_sum], axis=0)
        joint_sums[layer] = joint_sum
        grad_tall[layer] = (project_sum, shrink_sum)

    sums = jnp.concatenate(
        [sums_one[0][:2], sums_one[1][:2], sums_two[0][:2], sums_two[1][:2], head_sums[:2]]
    )
    sums = jnp.pad(sums, ((0, 6), (0, 0))).reshape(16, count, head_width).transpose(1, 0, 2)
    sums, qkv_grad, in_grad, tokens_grad = last_exchange(
        count,
        ring,
        10,
        sums,
        joint_sums[0],
        grad_hidden.astype(BF16),
        mixes[: LAYERS - 1],
        mixes[LAYERS - 1 :],
    )
    sums = lax.dynamic_slice_in_dim(sums, lax.axis_index("ctx") * part, part, axis=1)

    return (
        mixed.astype(F32).reshape(local_seqs, local_rows, width),
        tokens_grad.reshape(local_seqs, local_rows, width),
        jnp.stack([sums[0], sums[2]]),
        jnp.stack([sums[1], sums[3]]),
        qkv_grad,
        jnp.stack([pair[0] for pair in grad_tall]),
        jnp.stack([sums[4], sums[6]]),
        jnp.stack([sums[5], sums[7]]),
        in_grad,
        jnp.stack([pair[1] for pair in grad_tall]),
        sums[8],
        sums[9],
    )


def solution(mesh):
    both = ("dp", "ctx")
    return jax.shard_map(
        shards,
        mesh=mesh,
        in_specs=(
            P("dp", "ctx", None),
            P(None, both),
            P(None, both),
            P(None, both, None),
            P(None, both, None),
            P(None, both),
            P(None, both),
            P(None, both, None),
            P(None, both, None),
            P(both),
            P(both),
            P(both, None),
            P("dp", "ctx", None),
            P("dp", "ctx", None),
            P("dp", "ctx"),
            P("dp", "ctx", None),
        ),
        out_specs=(
            P("dp", "ctx", None),
            P("dp", "ctx", None),
            P(None, both),
            P(None, both),
            P(None, both, None),
            P(None, both, None),
            P(None, both),
            P(None, both),
            P(None, both, None),
            P(None, both, None),
            P(both),
            P(both),
        ),
        check_vma=False,
    )
```

```python
import functools
import math

import jax
import jax.numpy as jnp
from jax import lax
from jax.experimental import pallas as pl
from jax.experimental.pallas import tpu as pltpu
from jax.sharding import PartitionSpec as P

HEADS = 16
LAYERS = 2

EPSILON = 1e-05
FLOOR = -1e30
RECALL_SHARE = 0.25
DISTANCE_SCALE = 1.5

MESH = pl.DeviceIdType.MESH
VMEM = pltpu.VMEM
BF16 = jnp.bfloat16
F32 = jnp.float32


def norm_parts(values):
    average = jnp.mean(values, axis=-1, keepdims=True)
    centered = values - average
    variance = jnp.mean(centered * centered, axis=-1, keepdims=True)
    inverse = lax.rsqrt(variance + EPSILON)
    return centered * inverse, inverse


def norm_backward(grad, unit, inverse, gains):
    scaled = grad * gains
    return inverse * (
        scaled
        - jnp.mean(scaled, axis=-1, keepdims=True)
        - unit * jnp.mean(scaled * unit, axis=-1, keepdims=True)
    )


def send(source, target, send_sem, recv_sem, where):
    copy = pltpu.make_async_remote_copy(
        src_ref=source,
        dst_ref=target,
        send_sem=send_sem,
        recv_sem=recv_sem,
        device_id=where,
        device_id_type=MESH,
    )
    copy.start()
    return copy


def partner_of(me, plane, ring):
    return ((me // ring) * ring + plane, me % ring), me % ring != plane


def greet_all(targets, partner=None, away=None):
    barrier = pltpu.get_barrier_semaphore()
    for target in targets:
        pl.semaphore_signal(barrier, inc=1, device_id=target, device_id_type=MESH)
    if partner is None:
        pl.semaphore_wait(barrier, len(targets))
        return

    @pl.when(away)
    def _():
        pl.semaphore_signal(barrier, inc=1, device_id=partner, device_id_type=MESH)

    pl.semaphore_wait(barrier, len(targets) + away.astype(jnp.int32))


def swap_begin(source, target, send_sem, recv_sem, partner, away):
    copy = pltpu.make_async_remote_copy(
        src_ref=source,
        dst_ref=target,
        send_sem=send_sem,
        recv_sem=recv_sem,
        device_id=partner,
        device_id_type=MESH,
    )
    stay = pltpu.make_async_copy(source, target, recv_sem)

    @pl.when(away)
    def _():
        copy.start()

    @pl.when(jnp.logical_not(away))
    def _():
        stay.start()

    return copy, stay, away


def swap_end(swap):
    copy, stay, away = swap

    @pl.when(away)
    def _():
        copy.wait()

    @pl.when(jnp.logical_not(away))
    def _():
        stay.wait()


def square_of(me):
    core, x, y = me % 2, (me // 2) % 2, me // 4
    return (
        4 * y + 2 * (1 - x) + core,
        4 * (1 - y) + 2 * x + core,
        4 * (1 - y) + 2 * (1 - x) + core,
    )


def gather_sems(count):
    half = count // 2
    dma = pltpu.SemaphoreType.DMA
    if count == 8:
        return [dma((7,)), dma((7,)), dma((6,)), dma((6,))]
    return [dma((half,)), dma((half,)), dma((half - 1,)), dma((half - 1,))]


def gather_begin(count, me, plane, own_ref, full_ref, send_sem, recv_sem):
    half = count // 2
    chip, core = me // 2, me % 2
    sibling = 2 * chip + (1 - core)
    if count == 8:
        beside, beyond, _ = square_of(me)
        cut = own_ref.shape[0] // 2
        sends = {}
        for n, target, begin in ((1, beside, 0), (3, beyond, 1), (2, beside, 1), (4, beyond, 0)):
            at = pl.ds(begin * cut, cut)
            sends[n] = send(
                own_ref.at[at],
                full_ref.at[me, at],
                send_sem.at[n],
                recv_sem.at[n],
                (target, plane),
            )
        sends[0] = send(
            own_ref, full_ref.at[me], send_sem.at[0], recv_sem.at[0], (sibling, plane)
        )
        return sends
    targets = [sibling] + [2 * ((chip + j) % half) + core for j in range(1, half)]
    return {
        j: send(own_ref, full_ref.at[me], send_sem.at[j], recv_sem.at[j], (target, plane))
        for j, target in enumerate(targets)
    }


def gather_end(count, me, plane, full_ref, sends, send_sem, recv_sem, pass_send, pass_recv):
    half = count // 2
    chip, core = me // 2, me % 2
    sibling = 2 * chip + (1 - core)
    passes = []

    def hand_on(block):
        n = len(passes)
        passes.append(send(block, block, pass_send.at[n], pass_recv.at[n], (sibling, plane)))

    if count == 8:
        beside, beyond, across = square_of(me)
        cut = full_ref.shape[1] // 2

        def part(device, begin):
            return full_ref.at[device, pl.ds(begin * cut, cut)]

        sends[1].wait_recv()
        block = part(beside, 0)
        sends[5] = send(block, block, send_sem.at[5], recv_sem.at[5], (beyond, plane))
        hand_on(block)
        sends[3].wait_recv()
        block = part(beyond, 1)
        sends[6] = send(block, block, send_sem.at[6], recv_sem.at[6], (beside, plane))
        hand_on(block)
        for n, device, begin in ((2, beside, 1), (4, beyond, 0), (5, across, 0), (6, across, 1)):
            sends[n].wait_recv()
            hand_on(part(device, begin))
    else:
        for j in range(1, half):
            sends[j].wait_recv()
            hand_on(full_ref.at[2 * ((chip + half - j) % half) + core])
    sends[0].wait_recv()
    for copy in passes:
        copy.wait_recv()
    return list(sends.values()) + passes


def plane_kernel(count, ring, reduce, mode, gather, kinds, *refs):
    refs = list(refs)
    half = count // 2
    partial_ref = refs.pop(0) if reduce else None
    base_ref = refs.pop(0) if mode != "none" else None
    gain_ref = refs.pop(0) if mode in ("norm", "back") else None
    shift_ref = refs.pop(0) if mode == "norm" else None
    saved_ref = refs.pop(0) if mode == "back" else None
    ride_refs = [refs.pop(0) for _ in kinds]
    full_ref = refs.pop(0) if gather else None
    new_ref = refs.pop(0) if reduce else None
    stat_ref = refs.pop(0) if mode == "back" else None
    ride_outs = [refs.pop(0) for _ in kinds]
    square, paired = count == 8, ring == 4
    if reduce:
        mine_ref, side_ref, out_ref, in_ref = (refs.pop(0) for _ in range(4))
        mine_sem, side_send, side_recv, far_send, far_recv = (refs.pop(0) for _ in range(5))
    if gather:
        own_ref, own_sem = refs.pop(0), refs.pop(0)
        gather_send, gather_recv, pass_send, pass_recv = (refs.pop(0) for _ in range(4))
    land_refs = [refs.pop(0) if kind in ("sum0", "sum1") else None for kind in kinds]
    if kinds:
        ride_send, ride_recv, ride_own = refs.pop(0), refs.pop(0), refs.pop(0)

    me = lax.axis_index("dp")
    plane = lax.axis_index("ctx")
    chip, core = me // 2, me % 2
    sibling = 2 * chip + (1 - core)
    if square:
        peers = list(square_of(me))
    else:
        peers = [2 * ((chip + j) % half) + core for j in range(1, half)]

    greet = []
    if "mix" in kinds:
        greet += [((me + k) % count, plane) for k in range(1, count)]
    elif reduce or gather:
        greet += [(sibling, plane)] + [(peer, plane) for peer in peers]
    mate, twin = 2 * (plane // 2) + (1 - plane % 2), (plane + 2) % ring
    if any(kind in ("get0", "get1", "hop") for kind in kinds) or (kinds and not paired):
        greet += [(me, (plane + j) % ring) for j in range(1, ring)]
    elif "sum0" in kinds or "sum1" in kinds:
        greet += [(me, mate), (me, twin)]
    partner, away = partner_of(me, plane, ring)
    if "swap" in kinds:
        greet_all(greet, partner, away)
    else:
        greet_all(greet)
    pending = []
    rides, stays, swaps, mixes = [], [], [], []

    def to_mate(i, n, t):
        return send(
            ride_refs[i].at[t] if kinds[i] == "sum0" else ride_refs[i].at[:, t],
            land_refs[i].at[n],
            ride_send.at[i, n],
            ride_recv.at[i, n],
            (me, mate),
        )

    for i, kind in enumerate(kinds):
        if kind == "swap":
            swaps.append(
                swap_begin(
                    ride_refs[i],
                    ride_outs[i],
                    ride_send.at[i, 0],
                    ride_recv.at[i, 0],
                    partner,
                    away,
                )
            )
        if kind in ("sum0", "sum1") and paired:
            rides.append(to_mate(i, 0, 2 * (1 - plane // 2) + (1 - plane % 2)))
            continue
        for j in range(1, ring) if kind not in ("mix", "swap") else ():
            there = (plane + j) % ring
            if kind == "sum0":
                source, target = ride_refs[i].at[there], land_refs[i].at[j - 1]
            elif kind == "sum1":
                source, target = ride_refs[i].at[:, there], land_refs[i].at[j - 1]
            elif kind == "get0":
                source, target = ride_refs[i], ride_outs[i].at[plane]
            elif kind == "hop":
                source, target = ride_refs[i].at[there], ride_outs[i].at[plane]
            else:
                source, target = ride_refs[i], ride_outs[i].at[:, plane]
            rides.append(
                send(source, target, ride_send.at[i, j - 1], ride_recv.at[i, j - 1], (me, there))
            )
        if kind not in ("sum0", "sum1", "swap"):
            if kind == "mix":
                source, target = ride_refs[i].at[me], ride_outs[i].at[me]
            elif kind == "hop":
                source, target = ride_refs[i].at[plane], ride_outs[i].at[plane]
            elif kind == "get0":
                source, target = ride_refs[i], ride_outs[i].at[plane]
            else:
                source, target = ride_refs[i], ride_outs[i].at[:, plane]
            stay = pltpu.make_async_copy(source, target, ride_own.at[i])
            stay.start()
            stays.append(stay)
    pending += rides

    def chunks_of(i):
        steps = ride_outs[i].shape[0]
        chunk = 1 if kinds[i] == "sum1" else min(steps, 32)
        return steps // chunk, chunk

    def own_part(i, at, t):
        return (ride_refs[i][t, at] if kinds[i] == "sum0" else ride_refs[i][at, t]).astype(F32)

    pairs = [i for i, kind in enumerate(kinds) if kind in ("sum0", "sum1") and paired]

    def add_pairs(most):
        for i in pairs[len(crossing) : len(crossing) + most]:
            rides[i].wait_recv()
            steps, chunk = chunks_of(i)

            def add(step, carry, i=i, chunk=chunk):
                at = pl.ds(pl.multiple_of(step * chunk, chunk), chunk)
                total = own_part(i, at, twin) + land_refs[i][0, at].astype(F32)
                land_refs[i][3, at] = total.astype(BF16)
                return carry

            lax.fori_loop(0, steps, add, 0)
            crossing.append(
                send(
                    land_refs[i].at[3],
                    land_refs[i].at[2],
                    ride_send.at[i, 2],
                    ride_recv.at[i, 2],
                    (me, twin),
                )
            )
        if len(crossing) == len(pairs) and not staying:
            staying.extend(to_mate(i, 1, mate) for i in pairs)

    def begin_mixes():
        for i, kind in enumerate(kinds):
            for k in range(1, count) if kind == "mix" else ():
                there = (me + k) % count
                mixes.append(
                    send(
                        ride_refs[i].at[there],
                        ride_outs[i].at[me],
                        ride_send.at[i, k - 1],
                        ride_recv.at[i, k - 1],
                        (there, plane),
                    )
                )

    staying = []
    crossing = []
    if reduce:
        if square:
            beside, beyond, across = peers
            order = [across // 2, beside // 2, beyond // 2, chip]
        else:
            order = [(chip + j + 1) % half for j in range(half)]
        side, mine = [], []
        for j, where in enumerate(order):
            side.append(
                send(
                    partial_ref.at[2 * where + (1 - core)],
                    side_ref.at[j],
                    side_send.at[j],
                    side_recv.at[j],
                    (sibling, plane),
                )
            )
            mine.append(
                pltpu.make_async_copy(
                    partial_ref.at[2 * where + core], mine_ref.at[j], mine_sem.at[j]
                )
            )
            mine[-1].start()

        def pair_sum(j):
            mine[j].wait()
            side[j].wait_recv()
            return mine_ref[j].astype(F32) + side_ref[j].astype(F32)

        far = []
        if square:
            cut = out_ref.shape[1] // 2
            upper, lower = pl.ds(0, cut), pl.ds(cut, cut)

            def give(source, slot, target):
                far.append(
                    send(
                        source,
                        in_ref.at[slot],
                        far_send.at[slot],
                        far_recv.at[slot],
                        (target, plane),
                    )
                )

            out_ref[0] = pair_sum(0).astype(BF16)
            give(out_ref.at[0, upper], 0, beside)
            give(out_ref.at[0, lower], 3, beyond)
            out_ref[1] = pair_sum(1).astype(BF16)
            give(out_ref.at[1, upper], 1, beside)
            out_ref[2] = pair_sum(2).astype(BF16)
            give(out_ref.at[2, lower], 4, beyond)
            total = pair_sum(3)
            add_pairs(1)
            far[0].wait_recv()
            out_ref[3, upper] = (out_ref[2, upper].astype(F32) + in_ref[0].astype(F32)).astype(BF16)
            give(out_ref.at[3, upper], 5, beyond)
            far[1].wait_recv()
            out_ref[3, lower] = (out_ref[1, lower].astype(F32) + in_ref[3].astype(F32)).astype(BF16)
            give(out_ref.at[3, lower], 2, beside)
            begin_mixes()
            add_pairs(1)
            far[2].wait_recv()
            far[3].wait_recv()
            far[4].wait_recv()
            far[5].wait_recv()
            total = total + jnp.concatenate(
                [
                    in_ref[1].astype(F32) + in_ref[5].astype(F32),
                    in_ref[4].astype(F32) + in_ref[2].astype(F32),
                ],
                axis=0,
            )
        else:
            for j in range(1, half):
                out_ref[j - 1] = pair_sum(j - 1).astype(BF16)
                far.append(
                    send(
                        out_ref.at[j - 1],
                        in_ref.at[j - 1],
                        far_send.at[j - 1],
                        far_recv.at[j - 1],
                        (peers[j - 1], plane),
                    )
                )
            total = pair_sum(half - 1)
            for j in range(1, half):
                far[j - 1].wait_recv()
                total = total + in_ref[j - 1].astype(F32)
        pending += side + far
    if mode == "norm":
        value = base_ref[...] + total
        new_ref[...] = value
        unit, _ = norm_parts(value)
        result = unit * gain_ref[...] + shift_ref[...]
    elif mode == "back":
        unit, inverse = norm_parts(saved_ref[...].astype(F32))
        stat_ref[0:1, :] = jnp.sum(total * unit, axis=0, keepdims=True)
        stat_ref[1:2, :] = jnp.sum(total, axis=0, keepdims=True)
        result = base_ref[...] + norm_backward(total, unit, inverse, gain_ref[...])
        new_ref[...] = result
    elif mode == "plain":
        result = base_ref[...]
        if reduce:
            result = result + total
            new_ref[...] = result

    if gather:
        own_ref[...] = result.astype(BF16)
        sends = gather_begin(count, me, plane, own_ref, full_ref, gather_send, gather_recv)
        stay = pltpu.make_async_copy(own_ref, full_ref.at[me], own_sem)
        stay.start()
        stays.append(stay)
    if not (reduce and square):
        begin_mixes()
    add_pairs(len(pairs))
    if gather:
        pending += gather_end(
            count, me, plane, full_ref, sends, gather_send, gather_recv, pass_send, pass_recv
        )
    n = len(pairs)
    for copy in rides[n:] + mixes + staying + crossing:
        copy.wait_recv()
    pending += mixes + staying + crossing
    for copy in stays:
        copy.wait()
    for swap in swaps:
        swap_end(swap)
    for i, kind in enumerate(kinds):
        if kind not in ("sum0", "sum1"):
            continue
        steps, chunk = chunks_of(i)

        def add(step, carry, i=i, chunk=chunk):
            at = pl.ds(pl.multiple_of(step * chunk, chunk), chunk)
            total = own_part(i, at, plane)
            for j in (1, 2) if paired else range(ring - 1):
                total = total + land_refs[i][j, at].astype(F32)
            ride_outs[i][at] = total.astype(ride_outs[i].dtype)
            return carry

        lax.fori_loop(0, steps, add, 0)
    for copy in pending:
        copy.wait_send()


def plane_exchange(
    count,
    ring,
    call_id,
    partial=None,
    base=None,
    gains=None,
    shifts=None,
    saved=None,
    gather=True,
    sums=(),
    gets=(),
    mixes=(),
    hops=(),
    swaps=(),
):
    reduce = partial is not None
    mode = "none" if base is None else "plain"
    if gains is not None:
        mode = "norm" if saved is None else "back"
    half = count // 2
    operands = [partial] if reduce else []
    if base is not None:
        operands.append(base)
        rows, width = base.shape
    if gains is not None:
        operands.append(gains.reshape(1, width))
    if mode == "norm":
        operands.append(shifts.reshape(1, width))
    if mode == "back":
        operands.append(saved)
    operands += sums
    specs = [pl.BlockSpec(memory_space=VMEM)] * len(operands)
    if reduce:
        specs[0] = pl.BlockSpec(memory_space=pltpu.HBM)
    operands += list(gets) + list(mixes) + list(hops) + list(swaps)
    specs += [pl.BlockSpec(memory_space=pltpu.HBM)] * (len(operands) - len(specs))
    kinds = tuple("sum" + str(x.ndim - 3) for x in sums)
    kinds += tuple("get" + str(x.ndim - 2) for x in gets)
    kinds += ("mix",) * len(mixes) + ("hop",) * len(hops) + ("swap",) * len(swaps)
    outs, scratch = [], []
    if gather:
        outs.append(jax.ShapeDtypeStruct((count, rows, width), BF16))
    if reduce:
        outs.append(jax.ShapeDtypeStruct((rows, width), F32))
    if mode == "back":
        outs.append(jax.ShapeDtypeStruct((8, width), F32))
    lands = [x.shape[1:] if x.ndim == 3 else x.shape[:1] + x.shape[2:] for x in sums]
    outs += [
        jax.ShapeDtypeStruct(land, F32 if x.ndim == 3 else BF16) for land, x in zip(lands, sums)
    ]
    out_specs = [pl.BlockSpec(memory_space=VMEM)] * len(outs)
    if gather:
        out_specs[0] = pl.BlockSpec(memory_space=pltpu.HBM)
    outs += [
        jax.ShapeDtypeStruct((ring,) + x.shape if x.ndim == 2 else (count, ring) + x.shape[1:], BF16)
        for x in gets
    ]
    outs += [jax.ShapeDtypeStruct(x.shape, x.dtype) for x in list(mixes) + list(hops) + list(swaps)]
    out_specs += [pl.BlockSpec(memory_space=pltpu.HBM)] * (len(outs) - len(out_specs))
    dma = pltpu.SemaphoreType.DMA
    if reduce:
        taken = (6, rows // 2, width) if count == 8 else (half - 1, rows, width)
        scratch += [
            VMEM((half, rows, width), BF16),
            VMEM((half, rows, width), BF16),
            VMEM((half, rows, width), BF16),
            VMEM(taken, BF16),
            dma((half,)),
            dma((half,)),
            dma((half,)),
            dma(taken[:1]),
            dma(taken[:1]),
        ]
    if gather:
        scratch += [VMEM((rows, width), BF16), dma] + gather_sems(count)
    scratch += [VMEM((4 if ring == 4 else ring - 1,) + land, BF16) for land in lands]
    if kinds:
        most = max(ring, count if mixes else 0) - 1
        scratch += [dma((len(kinds), most)), dma((len(kinds), most)), dma((len(kinds),))]
    return pl.pallas_call(
        functools.partial(plane_kernel, count, ring, reduce, mode, gather, kinds),
        out_shape=tuple(outs),
        in_specs=specs,
        out_specs=tuple(out_specs),
        scratch_shapes=scratch,
        compiler_params=pltpu.CompilerParams(
            collective_id=call_id, has_side_effects=True, vmem_limit_bytes=16 * 1024 * 1024
        ),
        cost_estimate=pl.CostEstimate(
            flops=0, bytes_accessed=(60 if reduce else 30) << 20, transcendentals=0
        ),
    )(*operands)


def relay(source, target, sems, where, begin):
    copy = pltpu.make_async_remote_copy(
        src_ref=source,
        dst_ref=target,
        send_sem=sems[0],
        recv_sem=sems[1],
        device_id=where,
        device_id_type=MESH,
    )
    if begin:
        copy.start()
    return copy


def relay_begin(ring, me, plane, own, place, send_sem, recv_sem):
    for side, shift in ((0, 1), (1, -1)):
        there = (me, (plane + ring + shift) % ring)
        sems = (send_sem.at[side, 0], recv_sem.at[side, 0])

        @pl.when(plane < ring - 1 if side == 0 else plane > 0)
        def _(there=there, sems=sems):
            relay(own, place(plane), sems, there, True)


def relay_step(ring, me, plane, step, place, send_sem, recv_sem):
    for side, shift in ((0, 1), (1, -1)):
        there = (me, (plane + ring + shift) % ring)
        origin = (plane + ring - shift * step) % ring
        came = plane >= step if side == 0 else plane < ring - step
        more = plane < ring - 1 if side == 0 else plane > 0

        @pl.when(came)
        def _(side=side, there=there, origin=origin):
            block = place(origin)
            sems = (send_sem.at[side, step - 1], recv_sem.at[side, step - 1])
            relay(block, block, sems, there, False).wait_recv()

        if step < ring - 1:

            @pl.when(jnp.logical_and(came, more))
            def _(side=side, there=there, origin=origin):
                block = place(origin)
                sems = (send_sem.at[side, step], recv_sem.at[side, step])
                relay(block, block, sems, there, True)


def relay_end(ring, me, plane, place, send_sem, recv_sem):
    for step in range(ring - 1):
        for side, shift in ((0, 1), (1, -1)):
            there = (me, (plane + ring + shift) % ring)
            came = plane >= step if side == 0 else plane < ring - step
            more = plane < ring - 1 if side == 0 else plane > 0

            @pl.when(jnp.logical_and(came, more))
            def _(side=side, there=there):
                block = place(plane)
                sems = (send_sem.at[side, step], recv_sem.at[side, step])
                relay(block, block, sems, there, False).wait_send()


def first_kernel(count, ring, layers, talls, *refs):
    refs = list(refs)
    token_ref, small_ref, served_ref, flag_ref = (refs.pop(0) for _ in range(4))
    column_refs = [refs.pop(0) for _ in range(2)]
    tall_refs = [refs.pop(0) for _ in range(talls)]
    full_ref, vector_ref, rows_ref, flags_ref = (refs.pop(0) for _ in range(4))
    wide_refs = [[refs.pop(0) for _ in range(layers)] for _ in range(2)]
    whole_refs = [refs.pop(0) for _ in range(talls)]
    small_all = refs.pop(0)
    column_all = [refs.pop(0) for _ in range(2)]
    own_sem, own_ref = refs.pop(0), refs.pop(0)
    (
        gather_send,
        gather_recv,
        pass_send,
        pass_recv,
        small_send,
        small_recv,
        across_send,
        across_recv,
        column_send,
        column_recv,
        relay_send,
        relay_recv,
        flag_send,
        flag_recv,
        rows_send,
        rows_recv,
    ) = refs
    me = lax.axis_index("dp")
    plane = lax.axis_index("ctx")
    mates = [(me + k) % count for k in range(1, count)]
    planes = [(plane + j) % ring for j in range(1, ring)]
    greet_all([(mate, plane) for mate in mates] + [(me, there) for there in planes])

    stays = []

    def stay(source, target):
        copy = pltpu.make_async_copy(source, target, own_sem.at[len(stays)])
        copy.start()
        stays.append(copy)

    small_all[me, plane] = small_ref[...]
    smalls = [
        send(small_ref, small_all.at[me, plane], small_send.at[k], small_recv.at[k], (mate, plane))
        for k, mate in enumerate(mates)
    ]
    columns = []
    for i in range(2):
        stay(column_refs[i].at[me], column_all[i].at[me])
        for k, mate in enumerate(mates):
            columns.append(
                send(
                    column_refs[i].at[mate],
                    column_all[i].at[me],
                    column_send.at[i, k],
                    column_recv.at[i, k],
                    (mate, plane),
                )
            )
    column_stays = stays[:]
    pending = smalls + columns
    late = []
    for j, there in enumerate(planes):
        late.append(
            send(
                flag_ref.at[there],
                flags_ref.at[plane],
                flag_send.at[j],
                flag_recv.at[j],
                (me, there),
            )
        )
    flags_ref[plane] = flag_ref[plane]
    for copy in smalls:
        copy.wait_recv()
    across = [
        send(
            small_all.at[:, plane],
            small_all.at[:, plane],
            across_send.at[j],
            across_recv.at[j],
            (me, there),
        )
        for j, there in enumerate(planes)
    ]

    relays = []

    def spread(own, place):
        n = len(relays)
        relays.append((place, relay_send.at[n], relay_recv.at[n]))
        stay(own, place(plane))
        relay_begin(ring, me, plane, own, *relays[-1])

    def spread_tall(i):
        spread(tall_refs[i], lambda p: whole_refs[i].at[p])

    for i in range(2):
        spread_tall(i)
    for copy in across:
        copy.wait_recv()
    groups = vector_ref.shape[1] // 128
    members = count * ring // groups
    for group in range(groups):
        total = small_all[group * members // ring, group * members % ring]
        for n in range(group * members + 1, (group + 1) * members):
            total = total + small_all[n // ring, n % ring]
        vector_ref[:, group * 128 : (group + 1) * 128] = total
    unit, _ = norm_parts(token_ref[...].astype(F32))
    own_ref[...] = (unit * vector_ref[0:1, :] + vector_ref[1:2, :]).astype(BF16)
    stay(own_ref, full_ref.at[me])
    sends = gather_begin(count, me, plane, own_ref, full_ref, gather_send, gather_recv)
    for copy in columns:
        copy.wait_recv()
    for copy in column_stays:
        copy.wait()
    for layer in range(layers):
        for i in range(2):
            spread(
                column_all[i].at[:, layer],
                lambda p, layer=layer, i=i: wide_refs[i][layer].at[:, p],
            )
    for i in range(2, talls):
        spread_tall(i)
    pending += gather_end(
        count, me, plane, full_ref, sends, gather_send, gather_recv, pass_send, pass_recv
    )
    for k, mate in enumerate(mates):
        late.append(
            send(
                served_ref.at[mate],
                rows_ref.at[me],
                rows_send.at[k],
                rows_recv.at[k],
                (mate, plane),
            )
        )
    stay(served_ref.at[me], rows_ref.at[me])
    for step in range(1, ring):
        for one in relays:
            relay_step(ring, me, plane, step, *one)
    for copy in late:
        copy.wait_recv()
    for copy in stays[len(column_stays) :]:
        copy.wait()
    for copy in pending + across + late:
        copy.wait_send()
    for one in relays:
        relay_end(ring, me, plane, *one)


def first_exchange(count, ring, call_id, tokens, small, served, flags, joint, expand, talls):
    rows, width = tokens.shape
    layers = joint.shape[1]
    dma = pltpu.SemaphoreType.DMA
    near, far = pl.BlockSpec(memory_space=VMEM), pl.BlockSpec(memory_space=pltpu.HBM)
    outs = [
        jax.ShapeDtypeStruct((count, rows, width), BF16),
        jax.ShapeDtypeStruct((16, width), F32),
        jax.ShapeDtypeStruct(served.shape, BF16),
        jax.ShapeDtypeStruct(flags.shape, flags.dtype),
    ]
    for x in (joint, expand):
        outs += [jax.ShapeDtypeStruct((count, ring) + x.shape[2:], BF16)] * layers
    outs += [jax.ShapeDtypeStruct((ring,) + x.shape, BF16) for x in talls]

    def pair(*shape):
        return [dma(shape), dma(shape)]

    return pl.pallas_call(
        functools.partial(first_kernel, count, ring, layers, len(talls)),
        out_shape=tuple(outs),
        in_specs=[near, near, far, near, near, near] + [far] * len(talls),
        out_specs=tuple([far, near, far, near] + [far] * (2 * layers + len(talls))),
        scratch_shapes=[
            VMEM((count, ring, 16, 128), F32),
            VMEM(joint.shape, BF16),
            VMEM(expand.shape, BF16),
            dma((4 + 2 * layers + len(talls),)),
            VMEM((rows, width), BF16),
        ]
        + gather_sems(count)
        + pair(count - 1)
        + pair(ring - 1)
        + pair(2, count - 1)
        + pair(2 * layers + len(talls), 2, ring - 1)
        + pair(ring - 1)
        + pair(count - 1),
        compiler_params=pltpu.CompilerParams(
            collective_id=call_id, has_side_effects=True, vmem_limit_bytes=16 * 1024 * 1024
        ),
        cost_estimate=pl.CostEstimate(flops=0, bytes_accessed=200 << 20, transcendentals=0),
    )(tokens, small, served, flags, joint, expand, *talls)


def last_kernel(
    count,
    ring,
    layers,
    sums_ref,
    wide_ref,
    rows_ref,
    *refs,
):
    refs = list(refs)
    joint_refs = [refs.pop(0) for _ in range(layers - 1)]
    expand_refs = [refs.pop(0) for _ in range(layers)]
    total_ref, joint_grad_ref, expand_grad_ref, home_ref = (refs.pop(0) for _ in range(4))
    sums_in, across_ref, mixed_ref, rows_in = (refs.pop(0) for _ in range(4))
    (
        own_sem,
        swap_send,
        swap_recv,
        sums_send,
        sums_recv,
        wide_send,
        wide_recv,
        across_send,
        across_recv,
    ) = refs
    me = lax.axis_index("dp")
    plane = lax.axis_index("ctx")
    partner, away = partner_of(me, plane, ring)
    greet = [((me + k) % count, plane) for k in range(1, count)]
    greet += [(me, (plane + j) % ring) for j in range(1, ring)]
    greet_all(greet, partner, away)

    pending, sums = [], []
    for k in range(1, count):
        there = (me + k) % count
        sums.append(
            send(
                sums_ref.at[there],
                sums_in.at[me],
                sums_send.at[k - 1],
                sums_recv.at[k - 1],
                (there, plane),
            )
        )
    swap = swap_begin(rows_ref, rows_in, swap_send, swap_recv, partner, away)
    for k in range(1, count):
        there = (me + k) % count
        pending.append(
            send(
                wide_ref.at[there],
                mixed_ref.at[me],
                wide_send.at[k - 1],
                wide_recv.at[k - 1],
                (there, plane),
            )
        )
    sums_in[me] = sums_ref[me]
    stay = pltpu.make_async_copy(wide_ref.at[me], mixed_ref.at[me], own_sem)
    stay.start()
    for copy in sums:
        copy.wait_recv()
    total = sums_in[0]
    for k in range(1, count):
        total = total + sums_in[k]
    across_ref[plane] = total
    across = [
        send(
            across_ref.at[plane],
            across_ref.at[plane],
            across_send.at[j - 1],
            across_recv.at[j - 1],
            (me, (plane + j) % ring),
        )
        for j in range(1, ring)
    ]
    inner = expand_refs[0].shape[2]
    size = wide_ref.shape[2] // 3
    for layer in range(layers):
        for k in range(count):
            expand_grad_ref[layer, :, k * inner : (k + 1) * inner] = expand_refs[layer][k].astype(F32)

    def spread(layer, ref):
        for k in range(count):
            for i in range(3):
                at = (i * count + k) * size
                joint_grad_ref[layer, :, at : at + size] = ref[
                    k, :, i * size : (i + 1) * size
                ].astype(F32)

    for layer in range(1, layers):
        spread(layer, joint_refs[layer - 1])
    for copy in across:
        copy.wait_recv()
    total = across_ref[0]
    for j in range(1, ring):
        total = total + across_ref[j]
    total_ref[...] = total
    for copy in pending:
        copy.wait_recv()
    stay.wait()
    spread(0, mixed_ref)
    swap_end(swap)
    home_ref[...] = rows_in[...].astype(F32)
    for copy in pending + sums + across:
        copy.wait_send()


def last_exchange(count, ring, call_id, sums, wide, rows, joints, expands):
    dma = pltpu.SemaphoreType.DMA
    layers = len(expands)
    part = wide.shape[1]
    operands = (sums, wide, rows, *joints, *expands)
    outs = (
        jax.ShapeDtypeStruct(sums.shape[1:], F32),
        jax.ShapeDtypeStruct((layers, part, count * wide.shape[2]), F32),
        jax.ShapeDtypeStruct((layers, part, count * expands[0].shape[2]), F32),
        jax.ShapeDtypeStruct(rows.shape, F32),
    )
    spec = pl.BlockSpec(memory_space=VMEM)
    return pl.pallas_call(
        functools.partial(last_kernel, count, ring, layers),
        out_shape=outs,
        in_specs=[spec] * len(operands),
        out_specs=(spec,) * len(outs),
        scratch_shapes=[
            VMEM(sums.shape, F32),
            VMEM((ring,) + sums.shape[1:], F32),
            VMEM(wide.shape, BF16),
            VMEM(rows.shape, BF16),
            dma,
            dma,
            dma,
            dma((count - 1,)),
            dma((count - 1,)),
            dma((count - 1,)),
            dma((count - 1,)),
            dma((ring - 1,)),
            dma((ring - 1,)),
        ],
        compiler_params=pltpu.CompilerParams(
            collective_id=call_id, has_side_effects=True, vmem_limit_bytes=16 * 1024 * 1024
        ),
    )(*operands)


GATE_SCALE = math.sqrt(2.0 / math.pi)
GATE_CUBE = 0.044715


def after(*arrays):
    return lax.optimization_barrier(arrays)


def dot(left, right):
    return jnp.dot(left, right, preferred_element_type=F32)


def contract_rows(left, right):
    return lax.dot_general(left, right, (((0,), (0,)), ((), ())), preferred_element_type=F32)


def contract_cols(left, right):
    return lax.dot_general(left, right, (((1,), (1,)), ((), ())), preferred_element_type=F32)


def local_call(body, outs, operands, grid, in_specs, out_specs, scratch=(), flops=0):
    moved = sum(math.prod(x.shape) * x.dtype.itemsize for x in list(operands) + list(outs))
    return pl.pallas_call(
        body,
        out_shape=tuple(outs),
        grid=grid,
        in_specs=in_specs,
        out_specs=tuple(out_specs),
        scratch_shapes=list(scratch),
        compiler_params=pltpu.CompilerParams(vmem_limit_bytes=32 * 1024 * 1024),
        cost_estimate=pl.CostEstimate(flops=flops, bytes_accessed=moved, transcendentals=0),
    )(*operands)


def whole(x):
    return pl.BlockSpec(x.shape, lambda *_, n=len(x.shape): (0,) * n)


def stripe(shape):
    return pl.BlockSpec(shape, lambda i: (i,) + (0,) * (len(shape) - 1))


def probabilities(queries, keys, begin):
    scores = contract_cols(queries, keys) * (queries.shape[-1] ** (-0.5))
    row = begin + lax.broadcasted_iota(jnp.int32, scores.shape, 0)
    allowed = row >= lax.broadcasted_iota(jnp.int32, scores.shape, 1)
    scores = jnp.where(allowed, scores, FLOOR)
    raised = jnp.exp(scores - jnp.max(scores, axis=-1, keepdims=True))
    return raised / jnp.sum(raised, axis=-1, keepdims=True)


def attend_kernel(heads, block, x_ref, joint_ref, project_ref, packed_ref, attended_ref, partial_ref):
    packed_ref[...] = dot(x_ref[...], joint_ref[...]).astype(BF16)
    length, width = attended_ref.shape
    size = width // heads
    for head in range(heads):
        at = head * size
        for begin in range(0, length, block):
            end = begin + block
            probs = probabilities(
                packed_ref[begin:end, at : at + size], packed_ref[:end, width + at : width + at + size], begin
            )
            values = packed_ref[:end, 2 * width + at : 2 * width + at + size]
            attended_ref[begin:end, at : at + size] = dot(probs.astype(BF16), values).astype(BF16)
    partial_ref[...] = dot(attended_ref[...], project_ref[...]).astype(BF16)


def attend(normed, joint, project, seqs, heads):
    rows, width = normed.shape
    length, inner = rows // seqs, project.shape[0]
    outs = [
        jax.ShapeDtypeStruct((rows, 3 * inner), BF16),
        jax.ShapeDtypeStruct((rows, inner), BF16),
        jax.ShapeDtypeStruct((rows, width), BF16),
    ]
    return local_call(
        functools.partial(attend_kernel, heads, min(256, length)),
        outs,
        (normed, joint, project),
        (seqs,),
        [stripe((length, width)), whole(joint), whole(project)],
        [stripe((length, 3 * inner)), stripe((length, inner)), stripe((length, width))],
        flops=8 * rows * width * inner,
    )


def attend_backward_kernel(
    heads,
    block,
    grad_ref,
    x_ref,
    packed_ref,
    attended_ref,
    joint_ref,
    project_ref,
    joint_grad_ref,
    project_grad_ref,
    partial_ref,
    joint_sum,
    project_sum,
    key_sum,
    value_sum,
    low_ref,
):
    step = pl.program_id(0)
    length, width = attended_ref.shape
    size = width // heads
    scale = size ** (-0.5)
    grad = contract_cols(grad_ref[...], project_ref[...]).astype(BF16)
    key_sum[...] = jnp.zeros_like(key_sum)
    value_sum[...] = jnp.zeros_like(value_sum)
    for head in range(heads):
        at = head * size
        for begin in range(0, length, block):
            end = begin + block
            queries = packed_ref[begin:end, at : at + size]
            keys = packed_ref[:end, width + at : width + at + size]
            values = packed_ref[:end, 2 * width + at : 2 * width + at + size]
            here = grad[begin:end, at : at + size]
            probs = probabilities(queries, keys, begin)
            grad_probs = contract_cols(here, values)
            delta = jnp.sum(probs * grad_probs, axis=-1, keepdims=True)
            grad_scores = (probs * (grad_probs - delta)).astype(BF16)
            low_ref[begin:end, at : at + size] = (dot(grad_scores, keys) * scale).astype(BF16)
            key_sum[:end, at : at + size] += contract_rows(grad_scores, queries) * scale
            value_sum[:end, at : at + size] += contract_rows(probs.astype(BF16), here)
    low_ref[:, width : 2 * width] = key_sum[...].astype(BF16)
    low_ref[:, 2 * width :] = value_sum[...].astype(BF16)
    partial_ref[...] = contract_cols(low_ref[...], joint_ref[...]).astype(BF16)
    joint_part = contract_rows(x_ref[...], low_ref[...])
    project_part = contract_rows(attended_ref[...], grad_ref[...])

    @pl.when(step == 0)
    def _():
        joint_sum[...] = joint_part
        project_sum[...] = project_part

    @pl.when(step > 0)
    def _():
        joint_sum[...] += joint_part
        project_sum[...] += project_part

    @pl.when(step == pl.num_programs(0) - 1)
    def _():
        joint_grad_ref[...] = joint_sum[...].astype(BF16)
        project_grad_ref[...] = project_sum[...].astype(BF16)


def attend_backward(grad_out, normed, packed, attended, joint, project, seqs, heads):
    rows, width = normed.shape
    length, inner = rows // seqs, project.shape[0]
    outs = [
        jax.ShapeDtypeStruct(joint.shape, BF16),
        jax.ShapeDtypeStruct(project.shape, BF16),
        jax.ShapeDtypeStruct((rows, width), BF16),
    ]
    return local_call(
        functools.partial(attend_backward_kernel, heads, min(256, length)),
        outs,
        (grad_out, normed, packed, attended, joint, project),
        (seqs,),
        [
            stripe((length, width)),
            stripe((length, width)),
            stripe((length, 3 * inner)),
            stripe((length, inner)),
            whole(joint),
            whole(project),
        ],
        [whole(outs[0]), whole(outs[1]), stripe((length, width))],
        [
            VMEM(joint.shape, F32),
            VMEM(project.shape, F32),
            VMEM((length, inner), F32),
            VMEM((length, inner), F32),
            VMEM((length, 3 * inner), BF16),
        ],
        flops=16 * rows * width * inner,
    )


def forward_kernel(x_ref, expand_ref, shrink_ref, inner_ref, partial_ref):
    inner = dot(x_ref[...], expand_ref[...])
    inner_ref[...] = inner
    turn = jnp.tanh(GATE_SCALE * (inner + GATE_CUBE * (inner * inner * inner)))
    active = (0.5 * inner * (1.0 + turn)).astype(BF16)
    partial_ref[...] = dot(active, shrink_ref[...]).astype(BF16)


def forward(normed, expand, shrink):
    rows, width = normed.shape
    inner, block = expand.shape[1], 256
    outs = [jax.ShapeDtypeStruct((rows, inner), F32), jax.ShapeDtypeStruct((rows, width), BF16)]
    return local_call(
        forward_kernel,
        outs,
        (normed, expand, shrink),
        (rows // block,),
        [stripe((block, width)), whole(expand), whole(shrink)],
        [stripe((block, inner)), stripe((block, width))],
        flops=4 * rows * width * inner,
    )


def backward_kernel(
    branch_ref,
    x_ref,
    inner_ref,
    expand_ref,
    shrink_ref,
    expand_grad_ref,
    shrink_grad_ref,
    partial_ref,
    expand_sum,
    shrink_sum,
):
    step = pl.program_id(0)
    branch, inner = branch_ref[...], inner_ref[...]
    square = inner * inner
    turn = jnp.tanh(GATE_SCALE * (inner + GATE_CUBE * (square * inner)))
    active = (0.5 * inner * (1.0 + turn)).astype(BF16)
    slope = GATE_SCALE * (1.0 + (3.0 * GATE_CUBE) * square)
    slope = 0.5 * (1.0 + turn) + 0.5 * inner * (1.0 - turn * turn) * slope
    grad_inner = (contract_cols(branch, shrink_ref[...]) * slope).astype(BF16)
    partial_ref[...] = contract_cols(grad_inner, expand_ref[...]).astype(BF16)
    expand_part = contract_rows(x_ref[...], grad_inner)
    shrink_part = contract_rows(active, branch)

    @pl.when(step == 0)
    def _():
        expand_sum[...] = expand_part
        shrink_sum[...] = shrink_part

    @pl.when(step > 0)
    def _():
        expand_sum[...] += expand_part
        shrink_sum[...] += shrink_part

    @pl.when(step == pl.num_programs(0) - 1)
    def _():
        expand_grad_ref[...] = expand_sum[...].astype(BF16)
        shrink_grad_ref[...] = shrink_sum[...].astype(BF16)


def backward(branch, normed, inner, expand, shrink):
    rows, width = normed.shape
    block = 256
    outs = [
        jax.ShapeDtypeStruct(expand.shape, BF16),
        jax.ShapeDtypeStruct(shrink.shape, BF16),
        jax.ShapeDtypeStruct((rows, width), BF16),
    ]
    return local_call(
        backward_kernel,
        outs,
        (branch, normed, inner, expand, shrink),
        (rows // block,),
        [
            stripe((block, width)),
            stripe((block, width)),
            stripe((block, inner.shape[1])),
            whole(expand),
            whole(shrink),
        ],
        [whole(outs[0]), whole(outs[1]), stripe((block, width))],
        [VMEM(expand.shape, F32), VMEM(shrink.shape, F32)],
        flops=8 * rows * width * inner.shape[1],
    )


def ranks_of(flags):
    planes, groups, rows = flags.shape
    upto = jnp.arange(rows)[:, None] <= jnp.arange(rows)[None, :]
    inside = dot(flags.astype(BF16), upto.astype(BF16))
    before = jnp.where(
        jnp.arange(groups)[None, :, None] < jnp.arange(groups)[None, None, :],
        inside[:, :, -1:],
        0.0,
    )
    rank = inside + jnp.sum(before, axis=1)[:, :, None]
    return rank.reshape(planes, groups * rows), rank[:, -1, -1]


def pieces_of(values, terms):
    pieces = []
    for _ in range(terms):
        pieces.append(values.astype(BF16))
        values = values - pieces[-1].astype(F32)
    return jnp.concatenate(pieces, axis=0)


def recall_kernel(
    tile,
    hidden_ref,
    vector_ref,
    cotangent_ref,
    token_ref,
    stored_ref,
    mixed_ref,
    grad_ref,
    sums_ref,
    scaled_ref,
    pull_ref,
):
    rows, width = hidden_ref.shape
    tiles = stored_ref.shape[0] // tile
    unit, inverse = norm_parts(hidden_ref[...])
    gains = vector_ref[8:9, :]
    query = unit * gains + vector_ref[9:10, :]
    scale = DISTANCE_SCALE * math.sqrt(width)
    terms = jnp.concatenate([pieces_of(query, 3), cotangent_ref[...]], axis=0)
    ones = jnp.ones((8, width), BF16)

    def look(n, carry):
        at = pl.ds(pl.multiple_of(n * tile, tile), tile)
        stored = stored_ref[at, :]
        near = contract_cols(terms, stored)
        squares = jnp.square(stored.astype(F32))
        high = squares.astype(BF16)
        low = (squares - high.astype(F32)).astype(BF16)
        lengths = (contract_cols(ones, high) + contract_cols(ones, low))[0:1, :]
        scaled_ref[:, at] = (
            2.0 * (near[:rows] + (near[rows : 2 * rows] + near[2 * rows : 3 * rows])) - lengths
        ) / scale
        pull_ref[:, at] = RECALL_SHARE * near[3 * rows :]
        return carry

    lax.fori_loop(0, tiles, look, 0)
    usable = token_ref[...] == lax.broadcasted_iota(jnp.int32, scaled_ref.shape, 0)
    scaled = jnp.where(usable, scaled_ref[...], FLOOR)
    raised = jnp.where(usable, jnp.exp(scaled - jnp.max(scaled, axis=1, keepdims=True)), 0.0)
    weights = raised / jnp.sum(raised, axis=1, keepdims=True)
    pull = pull_ref[...]
    grad_scaled = weights * (pull - jnp.sum(weights * pull, axis=1, keepdims=True))
    scaled_ref[...] = weights
    pull_ref[...] = grad_scaled
    rest = jnp.sum(grad_scaled, axis=1, keepdims=True)

    def gather(n, total):
        at = pl.ds(pl.multiple_of(n * tile, tile), tile)
        both = jnp.concatenate(
            [pieces_of(scaled_ref[:, at], 2), pieces_of(pull_ref[:, at], 2)], axis=0
        )
        return total + dot(both, stored_ref[at, :])

    total = lax.fori_loop(0, tiles, gather, jnp.zeros((4 * rows, width), F32))
    recalled = total[:rows] + total[rows : 2 * rows]
    moved = total[2 * rows : 3 * rows] + total[3 * rows :] - rest * query
    mixed_ref[...] = (1.0 - RECALL_SHARE) * query + RECALL_SHARE * recalled
    grad_query = (1.0 - RECALL_SHARE) * cotangent_ref[...].astype(F32) + moved * (2.0 / scale)
    sums_ref[0:1, :] = jnp.sum(grad_query * unit, axis=0, keepdims=True)
    sums_ref[1:2, :] = jnp.sum(grad_query, axis=0, keepdims=True)
    grad_ref[...] = norm_backward(grad_query, unit, inverse, gains)


def recall_padded(hidden, vectors, stored, usable, cotangent):
    unit, inverse = norm_parts(hidden)
    query = unit * vectors[8] + vectors[9]
    scale = DISTANCE_SCALE * math.sqrt(query.shape[-1])
    stored, cotangent = stored.astype(F32), cotangent.astype(F32)
    distance = jnp.sum(jnp.square(query[None] - stored), axis=-1)
    pull = RECALL_SHARE * jnp.sum(cotangent[None] * stored, axis=-1)
    scaled = jnp.where(usable, -distance / scale, FLOOR)
    raised = jnp.where(usable, jnp.exp(scaled - jnp.max(scaled, axis=0, keepdims=True)), 0.0)
    weights = raised / jnp.sum(raised, axis=0, keepdims=True)
    grad_scaled = weights * (pull - jnp.sum(weights * pull, axis=0, keepdims=True))
    recalled = jnp.sum(weights[..., None] * stored, axis=0)
    moved = jnp.sum(grad_scaled[..., None] * stored, axis=0)
    moved = moved - jnp.sum(grad_scaled, axis=0)[:, None] * query
    mixed = (1.0 - RECALL_SHARE) * query + RECALL_SHARE * recalled
    grad_query = (1.0 - RECALL_SHARE) * cotangent + moved * (2.0 / scale)
    sums = jnp.stack([jnp.sum(grad_query * unit, axis=0), jnp.sum(grad_query, axis=0)])
    grad = norm_backward(grad_query, unit, inverse, vectors[8])
    return mixed, grad, jnp.pad(sums, ((0, 6), (0, 0)))


def recall(hidden, vectors, stored, token_of, cotangent):
    rows, width = hidden.shape
    entries = stored.shape[0]
    operands = (hidden, vectors, cotangent, token_of.reshape(1, entries), stored)
    outs = [
        jax.ShapeDtypeStruct((rows, width), F32),
        jax.ShapeDtypeStruct((rows, width), F32),
        jax.ShapeDtypeStruct((8, width), F32),
    ]
    return local_call(
        functools.partial(recall_kernel, min(512, entries)),
        outs,
        operands,
        (1,),
        [whole(x) for x in operands],
        [whole(x) for x in outs],
        [VMEM((rows, entries), F32), VMEM((rows, entries), F32)],
        flops=16 * rows * width * entries,
    )


def shards(
    tokens,
    ln1_gain,
    ln1_bias,
    qkv_weight,
    out_weight,
    ln2_gain,
    ln2_bias,
    in_weight,
    fc_weight,
    final_gain,
    final_bias,
    datastore,
    neighbour_owner,
    neighbour_row,
    neighbour_count,
    cotangent,
):
    local_seqs, local_rows, width = tokens.shape
    rows = local_seqs * local_rows
    count, ring = lax.axis_size("dp"), lax.axis_size("ctx")
    devices = count * ring
    both = ("dp", "ctx")
    seqs = count * local_seqs // ring
    heads = HEADS // count
    slots = neighbour_owner.shape[2]
    part = width // devices
    head_width = width // count
    inner_width = in_weight.shape[2] // count

    forth = []
    for s in range(count):
        for p in range(ring):
            forth.append((s * ring + p, ((s // ring) * ring + p) * ring + s % ring))

    pair_room = -(-(3 * rows * slots) // (2 * devices * 16)) * 16
    room = rows * slots // ring
    owners = neighbour_owner.reshape(rows, slots)
    live = neighbour_count.reshape(rows, 1)
    hits = (owners[:, :, None] == jnp.arange(devices)[None, None, :]) & (
        jnp.arange(slots)[None, :, None] < live[:, :, None]
    )
    asked_all = jnp.sum(jnp.where(hits, neighbour_row.reshape(rows, slots, 1), 0), axis=1).T
    usable_all = jnp.any(hits, axis=1).T
    upto = jnp.arange(rows)[:, None] <= jnp.arange(rows)[None, :]
    order = dot(usable_all.astype(BF16), upto.astype(BF16))
    taken = usable_all[:, None, :] & (
        order[:, None, :] == jnp.arange(1, pair_room + 1, dtype=F32)[None, :, None]
    )
    asked = jnp.sum(jnp.where(taken, asked_all[:, None, :], 0), axis=-1)
    asked = lax.all_to_all(asked, both, split_axis=0, concat_axis=0, tiled=True)
    asked = asked.reshape(count // ring, ring, ring, pair_room).swapaxes(1, 2)

    def by_plane(x):
        return x.reshape((count, ring) + x.shape[1:]).swapaxes(0, 1)

    token_at = by_plane(jnp.sum(jnp.where(taken, jnp.arange(rows)[None, None, :], 0), axis=-1))
    amounts = order[:, -1]
    usable = by_plane(jnp.arange(pair_room, dtype=F32)[None, :] < amounts[:, None])
    crowded = (jnp.max(amounts) > pair_room) | (jnp.max(jnp.sum(by_plane(amounts), axis=1)) > room)

    small = jnp.stack(
        [ln1_gain[0], ln1_bias[0], ln1_gain[1], ln1_bias[1], ln2_gain[0], ln2_bias[0]]
        + [ln2_gain[1], ln2_bias[1], final_gain, final_bias]
    ).astype(F32)
    small = jnp.concatenate([small, jnp.broadcast_to(crowded.astype(F32), (1, part))])
    here = lax.axis_index("dp") * ring + lax.axis_index("ctx")
    places = 128 // part
    small = jnp.tile(jnp.pad(small, ((0, 5), (0, 0))), (1, places))
    small = jnp.where(jnp.arange(128)[None, :] // part == here % places, small, 0.0)

    joint_own = qkv_weight.reshape(LAYERS, part, 3, count, head_width).transpose(3, 0, 1, 2, 4)
    joint_own = joint_own.reshape(count, LAYERS, part, 3 * head_width)
    expand_own = in_weight.reshape(LAYERS, part, count, inner_width).transpose(2, 0, 1, 3)

    notes = jnp.concatenate([usable.astype(jnp.int32), token_at], axis=-1)
    my_tokens, notes, asked = after(tokens.reshape(rows, width), notes, asked)
    served = datastore.at[asked.reshape(-1)].get(mode="promise_in_bounds")
    my_tokens = lax.ppermute(my_tokens, both, forth)
    notes = lax.ppermute(notes, both, forth)
    usable, token_at = notes[..., :pair_room], notes[..., pair_room:]
    last_all = lax.all_gather(fc_weight[1], "ctx", axis=0, tiled=False)
    exchange = functools.partial(plane_exchange, count, ring)
    first = first_exchange(
        count,
        ring,
        0,
        my_tokens,
        small,
        served.reshape(count, ring * pair_room, width),
        usable,
        joint_own,
        expand_own,
        (out_weight[0], fc_weight[0], out_weight[1]),
    )
    normed, vectors, served, flags = first[:4]
    joint, expand = list(first[4 : 4 + LAYERS]), list(first[4 + LAYERS : 4 + 2 * LAYERS])
    project, shrink = [first[-3], first[-1]], [first[-2], None]
    gain_one, shift_one = [vectors[0], vectors[2]], [vectors[1], vectors[3]]
    gain_two, shift_two = [vectors[4], vectors[6]], [vectors[5], vectors[7]]
    crowded = jnp.max(vectors[10]) > 0.5
    rank, _ = ranks_of(flags)
    served = served.reshape(count, ring, pair_room, width)

    chosen = flags.reshape(ring, 1, count * pair_room) * (
        rank[:, None, :] == jnp.arange(1, room + 1, dtype=F32)[None, :, None]
    )
    stored = jnp.einsum(
        "cpdt,dctw->cpw",
        chosen.astype(BF16).reshape(ring, room, count, pair_room),
        served,
        preferred_element_type=F32,
    ).astype(BF16)
    stored = lax.all_to_all(stored, "ctx", split_axis=0, concat_axis=0, tiled=True)

    hidden = my_tokens.astype(F32)
    saved = []
    for layer in range(LAYERS):
        normed = normed.reshape(count * rows, width)
        joint[layer] = joint[layer].reshape(width, 3 * head_width)
        project[layer] = project[layer].reshape(-1, width)
        packed, attended, partial = attend(normed, joint[layer], project[layer], seqs, heads)
        partial = partial.reshape(count, rows, width)
        normed_two, middle = exchange(2, partial, hidden, gain_two[layer], shift_two[layer])
        if layer + 1 == LAYERS:
            shrink[layer], normed_two = after(last_all, normed_two)
        normed_two = normed_two.reshape(count * rows, width)
        expand[layer] = expand[layer].reshape(width, inner_width)
        shrink[layer] = shrink[layer].reshape(-1, width)
        inner, partial = forward(normed_two, expand[layer], shrink[layer])
        partial = partial.reshape(count, rows, width)
        saved.append((hidden, normed, packed, attended, middle, normed_two, inner))
        if layer + 1 < LAYERS:
            normed, hidden = exchange(
                2, partial, middle, gain_one[layer + 1], shift_one[layer + 1]
            )
        else:
            hidden, my_cotangent = exchange(
                5, partial, middle, gather=False, swaps=(cotangent.reshape(rows, width),)
            )

    def few():
        rank, _ = ranks_of(usable)
        chosen = (usable.reshape(ring, 1, -1) > 0) & (
            rank[:, None, :] == jnp.arange(1, room + 1, dtype=F32)[None, :, None]
        )
        token_of = jnp.sum(jnp.where(chosen, token_at.reshape(ring, 1, -1) + 1, 0), axis=-1) - 1
        entries = stored.reshape(ring * room, width)
        return recall(hidden, vectors, entries, token_of.reshape(-1), my_cotangent)

    def many():
        asked = lax.all_to_all(asked_all, both, split_axis=0, concat_axis=0, tiled=True)
        padded = datastore.at[asked.reshape(-1)].get(mode="promise_in_bounds")
        padded = padded.reshape(devices, rows, width)
        padded = lax.all_to_all(padded, both, split_axis=0, concat_axis=0, tiled=True)
        padded = lax.ppermute(padded, both, forth)
        marks = lax.ppermute(usable_all.astype(jnp.int32), both, forth)
        return recall_padded(hidden, vectors, padded, marks > 0, my_cotangent)

    mixed, grad_hidden, head_sums = lax.cond(crowded, many, few)
    branch, mixed = exchange(6, base=grad_hidden, swaps=(mixed.astype(BF16),))
    sums_one, sums_two = [None] * LAYERS, [None] * LAYERS
    joint_sums, expand_sums = [None] * LAYERS, [None] * LAYERS
    grad_tall = [None] * LAYERS
    for layer in reversed(range(LAYERS)):
        start, normed, packed, attended, middle, normed_two, inner = saved[layer]
        grad_expand, grad_shrink, partial = backward(
            branch.reshape(count * rows, width), normed_two, inner, expand[layer], shrink[layer]
        )
        grad_expand = grad_expand.reshape(count, ring, part, inner_width)
        grad_shrink = grad_shrink.reshape(ring, -1, width)
        cut = grad_shrink.shape[1] // 2
        grad_out, grad_middle, sums_two[layer], upper_sum, expand_sum = exchange(
            7,
            partial.reshape(count, rows, width),
            grad_hidden,
            gain_two[layer],
            saved=middle,
            sums=(grad_shrink[:, :cut], grad_expand),
        )
        expand_sums[layer] = expand_sum
        grad_joint, grad_project, partial = attend_backward(
            grad_out.reshape(count * rows, width),
            normed,
            packed,
            attended,
            joint[layer],
            project[layer],
            seqs,
            heads,
        )
        rides = (
            grad_project.reshape(ring, part, width),
            grad_shrink[:, cut:],
            grad_joint.reshape(count, ring, part, 3 * head_width),
        )
        partial = partial.reshape(count, rows, width)
        if layer > 0:
            branch, grad_hidden, sums_one[layer], project_sum, lower_sum, joint_sum = exchange(
                8, partial, grad_middle, gain_one[layer], saved=start, sums=rides
            )
        else:
            grad_hidden, sums_one[layer], project_sum, lower_sum, joint_sum, *mixes = exchange(
                9,
                partial,
                grad_middle,
                gain_one[layer],
                saved=start,
                gather=False,
                sums=rides,
                mixes=tuple(joint_sums[1:]) + tuple(expand_sums),
            )
        shrink_sum = jnp.concatenate([upper_sum, lower_sum], axis=0)
        joint_sums[layer] = joint_sum
        grad_tall[layer] = (project_sum, shrink_sum)

    sums = jnp.concatenate(
        [sums_one[0][:2], sums_one[1][:2], sums_two[0][:2], sums_two[1][:2], head_sums[:2]]
    )
    sums = jnp.pad(sums, ((0, 6), (0, 0))).reshape(16, count, head_width).transpose(1, 0, 2)
    sums, qkv_grad, in_grad, tokens_grad = last_exchange(
        count,
        ring,
        10,
        sums,
        joint_sums[0],
        grad_hidden.astype(BF16),
        mixes[: LAYERS - 1],
        mixes[LAYERS - 1 :],
    )
    sums = lax.dynamic_slice_in_dim(sums, lax.axis_index("ctx") * part, part, axis=1)

    return (
        mixed.astype(F32).reshape(local_seqs, local_rows, width),
        tokens_grad.reshape(local_seqs, local_rows, width),
        jnp.stack([sums[0], sums[2]]),
        jnp.stack([sums[1], sums[3]]),
        qkv_grad,
        jnp.stack([pair[0] for pair in grad_tall]),
        jnp.stack([sums[4], sums[6]]),
        jnp.stack([sums[5], sums[7]]),
        in_grad,
        jnp.stack([pair[1] for pair in grad_tall]),
        sums[8],
        sums[9],
    )


def solution(mesh):
    both = ("dp", "ctx")
    return jax.shard_map(
        shards,
        mesh=mesh,
        in_specs=(
            P("dp", "ctx", None),
            P(None, both),
            P(None, both),
            P(None, both, None),
            P(None, both, None),
            P(None, both),
            P(None, both),
            P(None, both, None),
            P(None, both, None),
            P(both),
            P(both),
            P(both, None),
            P("dp", "ctx", None),
            P("dp", "ctx", None),
            P("dp", "ctx"),
            P("dp", "ctx", None),
        ),
        out_specs=(
            P("dp", "ctx", None),
            P("dp", "ctx", None),
            P(None, both),
            P(None, both),
            P(None, both, None),
            P(None, both, None),
            P(None, both),
            P(None, both),
            P(None, both, None),
            P(None, both, None),
            P(both),
            P(both),
        ),
        check_vma=False,
    )
```

```python
import functools
import math

import jax
import jax.numpy as jnp
from jax import lax
from jax.experimental import pallas as pl
from jax.experimental.pallas import tpu as pltpu
from jax.sharding import PartitionSpec as P

HEADS = 16
LAYERS = 2

EPSILON = 1e-05
FLOOR = -1e30
RECALL_SHARE = 0.25
DISTANCE_SCALE = 1.5

MESH = pl.DeviceIdType.MESH
VMEM = pltpu.VMEM
BF16 = jnp.bfloat16
F32 = jnp.float32


def norm_parts(values):
    average = jnp.mean(values, axis=-1, keepdims=True)
    centered = values - average
    variance = jnp.mean(centered * centered, axis=-1, keepdims=True)
    inverse = lax.rsqrt(variance + EPSILON)
    return centered * inverse, inverse


def norm_backward(grad, unit, inverse, gains):
    scaled = grad * gains
    return inverse * (
        scaled
        - jnp.mean(scaled, axis=-1, keepdims=True)
        - unit * jnp.mean(scaled * unit, axis=-1, keepdims=True)
    )


def send(source, target, send_sem, recv_sem, where):
    copy = pltpu.make_async_remote_copy(
        src_ref=source,
        dst_ref=target,
        send_sem=send_sem,
        recv_sem=recv_sem,
        device_id=where,
        device_id_type=MESH,
    )
    copy.start()
    return copy


def partner_of(me, plane, ring):
    return ((me // ring) * ring + plane, me % ring), me % ring != plane


def greet_all(targets, partner=None, away=None):
    barrier = pltpu.get_barrier_semaphore()
    for target in targets:
        pl.semaphore_signal(barrier, inc=1, device_id=target, device_id_type=MESH)
    if partner is None:
        pl.semaphore_wait(barrier, len(targets))
        return

    @pl.when(away)
    def _():
        pl.semaphore_signal(barrier, inc=1, device_id=partner, device_id_type=MESH)

    pl.semaphore_wait(barrier, len(targets) + away.astype(jnp.int32))


def swap_begin(source, target, send_sem, recv_sem, partner, away):
    copy = pltpu.make_async_remote_copy(
        src_ref=source,
        dst_ref=target,
        send_sem=send_sem,
        recv_sem=recv_sem,
        device_id=partner,
        device_id_type=MESH,
    )
    stay = pltpu.make_async_copy(source, target, recv_sem)

    @pl.when(away)
    def _():
        copy.start()

    @pl.when(jnp.logical_not(away))
    def _():
        stay.start()

    return copy, stay, away


def swap_end(swap):
    copy, stay, away = swap

    @pl.when(away)
    def _():
        copy.wait()

    @pl.when(jnp.logical_not(away))
    def _():
        stay.wait()


def square_of(me):
    core, x, y = me % 2, (me // 2) % 2, me // 4
    return (
        4 * y + 2 * (1 - x) + core,
        4 * (1 - y) + 2 * x + core,
        4 * (1 - y) + 2 * (1 - x) + core,
    )


def gather_sems(count):
    half = count // 2
    dma = pltpu.SemaphoreType.DMA
    if count == 8:
        return [dma((7,)), dma((7,)), dma((6,)), dma((6,))]
    return [dma((half,)), dma((half,)), dma((half - 1,)), dma((half - 1,))]


def gather_begin(count, me, plane, own_ref, full_ref, send_sem, recv_sem):
    half = count // 2
    chip, core = me // 2, me % 2
    sibling = 2 * chip + (1 - core)
    if count == 8:
        beside, beyond, _ = square_of(me)
        cut = own_ref.shape[0] // 2
        sends = {}
        for n, target, begin in ((1, beside, 0), (3, beyond, 1), (2, beside, 1), (4, beyond, 0)):
            at = pl.ds(begin * cut, cut)
            sends[n] = send(
                own_ref.at[at],
                full_ref.at[me, at],
                send_sem.at[n],
                recv_sem.at[n],
                (target, plane),
            )
        sends[0] = send(
            own_ref, full_ref.at[me], send_sem.at[0], recv_sem.at[0], (sibling, plane)
        )
        return sends
    targets = [sibling] + [2 * ((chip + j) % half) + core for j in range(1, half)]
    return {
        j: send(own_ref, full_ref.at[me], send_sem.at[j], recv_sem.at[j], (target, plane))
        for j, target in enumerate(targets)
    }


def hand_on(me, plane, passes, block, pass_send, pass_recv):
    n = len(passes)
    sibling = 2 * (me // 2) + (1 - me % 2)
    passes.append(send(block, block, pass_send.at[n], pass_recv.at[n], (sibling, plane)))


def gather_middle(count, me, plane, full_ref, sends, send_sem, recv_sem, pass_send, pass_recv):
    passes = []
    if count == 8:
        beside, beyond, _ = square_of(me)
        cut = full_ref.shape[1] // 2
        for n, device, begin, target in ((1, beside, 0, beyond), (3, beyond, 1, beside)):
            sends[n].wait_recv()
            block = full_ref.at[device, pl.ds(begin * cut, cut)]
            far = 5 if n == 1 else 6
            sends[far] = send(block, block, send_sem.at[far], recv_sem.at[far], (target, plane))
            hand_on(me, plane, passes, block, pass_send, pass_recv)
    return passes


def gather_end(count, me, plane, full_ref, sends, passes, pass_send, pass_recv):
    half = count // 2
    chip, core = me // 2, me % 2
    if count == 8:
        beside, beyond, across = square_of(me)
        cut = full_ref.shape[1] // 2
        for n, device, begin in ((2, beside, 1), (4, beyond, 0), (5, across, 0), (6, across, 1)):
            sends[n].wait_recv()
            block = full_ref.at[device, pl.ds(begin * cut, cut)]
            hand_on(me, plane, passes, block, pass_send, pass_recv)
    else:
        for j in range(1, half):
            sends[j].wait_recv()
            block = full_ref.at[2 * ((chip + half - j) % half) + core]
            hand_on(me, plane, passes, block, pass_send, pass_recv)
    sends[0].wait_recv()
    for copy in passes:
        copy.wait_recv()
    return list(sends.values()) + passes


def plane_kernel(count, ring, reduce, mode, gather, kinds, *refs):
    refs = list(refs)
    half = count // 2
    partial_ref = refs.pop(0) if reduce else None
    base_ref = refs.pop(0) if mode != "none" else None
    gain_ref = refs.pop(0) if mode in ("norm", "back") else None
    shift_ref = refs.pop(0) if mode == "norm" else None
    saved_ref = refs.pop(0) if mode == "back" else None
    ride_refs = [refs.pop(0) for _ in kinds]
    full_ref = refs.pop(0) if gather else None
    new_ref = refs.pop(0) if reduce else None
    stat_ref = refs.pop(0) if mode == "back" else None
    ride_outs = [refs.pop(0) for _ in kinds]
    square, paired = count == 8, ring == 4
    if reduce:
        mine_ref, side_ref, out_ref, in_ref = (refs.pop(0) for _ in range(4))
        mine_sem, side_send, side_recv, far_send, far_recv = (refs.pop(0) for _ in range(5))
    if gather:
        own_ref, own_sem = refs.pop(0), refs.pop(0)
        gather_send, gather_recv, pass_send, pass_recv = (refs.pop(0) for _ in range(4))
    land_refs = [refs.pop(0) if kind in ("sum0", "sum1") else None for kind in kinds]
    if kinds:
        ride_send, ride_recv, ride_own = refs.pop(0), refs.pop(0), refs.pop(0)

    me = lax.axis_index("dp")
    plane = lax.axis_index("ctx")
    chip, core = me // 2, me % 2
    sibling = 2 * chip + (1 - core)
    if square:
        peers = list(square_of(me))
    else:
        peers = [2 * ((chip + j) % half) + core for j in range(1, half)]

    greet = []
    if "mix" in kinds:
        greet += [((me + k) % count, plane) for k in range(1, count)]
    elif reduce or gather:
        greet += [(sibling, plane)] + [(peer, plane) for peer in peers]
    mate, twin = 2 * (plane // 2) + (1 - plane % 2), (plane + 2) % ring
    if any(kind in ("get0", "get1", "hop") for kind in kinds) or (kinds and not paired):
        greet += [(me, (plane + j) % ring) for j in range(1, ring)]
    elif "sum0" in kinds or "sum1" in kinds:
        greet += [(me, mate), (me, twin)]
    partner, away = partner_of(me, plane, ring)
    if "swap" in kinds:
        greet_all(greet, partner, away)
    else:
        greet_all(greet)
    pending = []
    rides, stays, swaps, mixes = [], [], [], []

    def to_mate(i, n, t):
        return send(
            ride_refs[i].at[t] if kinds[i] == "sum0" else ride_refs[i].at[:, t],
            land_refs[i].at[n],
            ride_send.at[i, n],
            ride_recv.at[i, n],
            (me, mate),
        )

    for i, kind in enumerate(kinds):
        if kind == "swap":
            swaps.append(
                swap_begin(
                    ride_refs[i],
                    ride_outs[i],
                    ride_send.at[i, 0],
                    ride_recv.at[i, 0],
                    partner,
                    away,
                )
            )
        if kind in ("sum0", "sum1") and paired:
            rides.append(to_mate(i, 0, 2 * (1 - plane // 2) + (1 - plane % 2)))
            continue
        for j in range(1, ring) if kind not in ("mix", "swap") else ():
            there = (plane + j) % ring
            if kind == "sum0":
                source, target = ride_refs[i].at[there], land_refs[i].at[j - 1]
            elif kind == "sum1":
                source, target = ride_refs[i].at[:, there], land_refs[i].at[j - 1]
            elif kind == "get0":
                source, target = ride_refs[i], ride_outs[i].at[plane]
            elif kind == "hop":
                source, target = ride_refs[i].at[there], ride_outs[i].at[plane]
            else:
                source, target = ride_refs[i], ride_outs[i].at[:, plane]
            rides.append(
                send(source, target, ride_send.at[i, j - 1], ride_recv.at[i, j - 1], (me, there))
            )
        if kind not in ("sum0", "sum1", "swap"):
            if kind == "mix":
                source, target = ride_refs[i].at[me], ride_outs[i].at[me]
            elif kind == "hop":
                source, target = ride_refs[i].at[plane], ride_outs[i].at[plane]
            elif kind == "get0":
                source, target = ride_refs[i], ride_outs[i].at[plane]
            else:
                source, target = ride_refs[i], ride_outs[i].at[:, plane]
            stay = pltpu.make_async_copy(source, target, ride_own.at[i])
            stay.start()
            stays.append(stay)
    pending += rides

    def chunks_of(i):
        steps = ride_outs[i].shape[0]
        chunk = 1 if kinds[i] == "sum1" else min(steps, 32)
        return steps // chunk, chunk

    def own_part(i, at, t):
        return (ride_refs[i][t, at] if kinds[i] == "sum0" else ride_refs[i][at, t]).astype(F32)

    pairs = [i for i, kind in enumerate(kinds) if kind in ("sum0", "sum1") and paired]

    def add_pairs(most):
        for i in pairs[len(crossing) : len(crossing) + most]:
            rides[i].wait_recv()
            steps, chunk = chunks_of(i)

            def add(step, carry, i=i, chunk=chunk):
                at = pl.ds(pl.multiple_of(step * chunk, chunk), chunk)
                total = own_part(i, at, twin) + land_refs[i][0, at].astype(F32)
                land_refs[i][3, at] = total.astype(BF16)
                return carry

            lax.fori_loop(0, steps, add, 0)
            crossing.append(
                send(
                    land_refs[i].at[3],
                    land_refs[i].at[2],
                    ride_send.at[i, 2],
                    ride_recv.at[i, 2],
                    (me, twin),
                )
            )
        if len(crossing) == len(pairs) and not staying:
            staying.extend(to_mate(i, 1, mate) for i in pairs)

    def begin_mixes():
        for i, kind in enumerate(kinds):
            for k in range(1, count) if kind == "mix" else ():
                there = (me + k) % count
                mixes.append(
                    send(
                        ride_refs[i].at[there],
                        ride_outs[i].at[me],
                        ride_send.at[i, k - 1],
                        ride_recv.at[i, k - 1],
                        (there, plane),
                    )
                )

    staying = []
    crossing = []
    if reduce:
        if square:
            beside, beyond, across = peers
            order = [across // 2, beside // 2, beyond // 2, chip]
        else:
            order = [(chip + j + 1) % half for j in range(half)]
        side, mine = [], []
        for j, where in enumerate(order):
            side.append(
                send(
                    partial_ref.at[2 * where + (1 - core)],
                    side_ref.at[j],
                    side_send.at[j],
                    side_recv.at[j],
                    (sibling, plane),
                )
            )
            mine.append(
                pltpu.make_async_copy(
                    partial_ref.at[2 * where + core], mine_ref.at[j], mine_sem.at[j]
                )
            )
            mine[-1].start()

        def pair_sum(j):
            mine[j].wait()
            side[j].wait_recv()
            return mine_ref[j].astype(F32) + side_ref[j].astype(F32)

        far = []
        if square:
            cut = out_ref.shape[1] // 2
            upper, lower = pl.ds(0, cut), pl.ds(cut, cut)

            def give(source, slot, target):
                far.append(
                    send(
                        source,
                        in_ref.at[slot],
                        far_send.at[slot],
                        far_recv.at[slot],
                        (target, plane),
                    )
                )

            out_ref[0] = pair_sum(0).astype(BF16)
            give(out_ref.at[0, upper], 0, beside)
            give(out_ref.at[0, lower], 3, beyond)
            out_ref[1] = pair_sum(1).astype(BF16)
            give(out_ref.at[1, upper], 1, beside)
            out_ref[2] = pair_sum(2).astype(BF16)
            give(out_ref.at[2, lower], 4, beyond)
            total = pair_sum(3)
            add_pairs(1)
            far[0].wait_recv()
            out_ref[3, upper] = (out_ref[2, upper].astype(F32) + in_ref[0].astype(F32)).astype(BF16)
            give(out_ref.at[3, upper], 5, beyond)
            far[1].wait_recv()
            out_ref[3, lower] = (out_ref[1, lower].astype(F32) + in_ref[3].astype(F32)).astype(BF16)
            give(out_ref.at[3, lower], 2, beside)
            begin_mixes()
            add_pairs(1)
            far[2].wait_recv()
            far[3].wait_recv()
            far[4].wait_recv()
            far[5].wait_recv()
            total = total + jnp.concatenate(
                [
                    in_ref[1].astype(F32) + in_ref[5].astype(F32),
                    in_ref[4].astype(F32) + in_ref[2].astype(F32),
                ],
                axis=0,
            )
        else:
            for j in range(1, half):
                out_ref[j - 1] = pair_sum(j - 1).astype(BF16)
                far.append(
                    send(
                        out_ref.at[j - 1],
                        in_ref.at[j - 1],
                        far_send.at[j - 1],
                        far_recv.at[j - 1],
                        (peers[j - 1], plane),
                    )
                )
            total = pair_sum(half - 1)
            for j in range(1, half):
                far[j - 1].wait_recv()
                total = total + in_ref[j - 1].astype(F32)
        pending += side + far
    if mode == "norm":
        value = base_ref[...] + total
        new_ref[...] = value
        unit, _ = norm_parts(value)
        result = unit * gain_ref[...] + shift_ref[...]
    elif mode == "back":
        unit, inverse = norm_parts(saved_ref[...].astype(F32))
        stat_ref[0:1, :] = jnp.sum(total * unit, axis=0, keepdims=True)
        stat_ref[1:2, :] = jnp.sum(total, axis=0, keepdims=True)
        result = base_ref[...] + norm_backward(total, unit, inverse, gain_ref[...])
        new_ref[...] = result
    elif mode == "plain":
        result = base_ref[...]
        if reduce:
            result = result + total
            new_ref[...] = result

    if gather:
        own_ref[...] = result.astype(BF16)
        sends = gather_begin(count, me, plane, own_ref, full_ref, gather_send, gather_recv)
        stay = pltpu.make_async_copy(own_ref, full_ref.at[me], own_sem)
        stay.start()
        stays.append(stay)
    if not (reduce and square):
        begin_mixes()
    add_pairs(len(pairs))
    if gather:
        passes = gather_middle(
            count, me, plane, full_ref, sends, gather_send, gather_recv, pass_send, pass_recv
        )
        pending += gather_end(count, me, plane, full_ref, sends, passes, pass_send, pass_recv)
    n = len(pairs)
    for copy in rides[n:] + mixes + staying + crossing:
        copy.wait_recv()
    pending += mixes + staying + crossing
    for copy in stays:
        copy.wait()
    for swap in swaps:
        swap_end(swap)
    for i, kind in enumerate(kinds):
        if kind not in ("sum0", "sum1"):
            continue
        steps, chunk = chunks_of(i)

        def add(step, carry, i=i, chunk=chunk):
            at = pl.ds(pl.multiple_of(step * chunk, chunk), chunk)
            total = own_part(i, at, plane)
            for j in (1, 2) if paired else range(ring - 1):
                total = total + land_refs[i][j, at].astype(F32)
            ride_outs[i][at] = total.astype(ride_outs[i].dtype)
            return carry

        lax.fori_loop(0, steps, add, 0)
    for copy in pending:
        copy.wait_send()


def plane_exchange(
    count,
    ring,
    call_id,
    partial=None,
    base=None,
    gains=None,
    shifts=None,
    saved=None,
    gather=True,
    sums=(),
    gets=(),
    mixes=(),
    hops=(),
    swaps=(),
):
    reduce = partial is not None
    mode = "none" if base is None else "plain"
    if gains is not None:
        mode = "norm" if saved is None else "back"
    half = count // 2
    operands = [partial] if reduce else []
    if base is not None:
        operands.append(base)
        rows, width = base.shape
    if gains is not None:
        operands.append(gains.reshape(1, width))
    if mode == "norm":
        operands.append(shifts.reshape(1, width))
    if mode == "back":
        operands.append(saved)
    operands += sums
    specs = [pl.BlockSpec(memory_space=VMEM)] * len(operands)
    if reduce:
        specs[0] = pl.BlockSpec(memory_space=pltpu.HBM)
    operands += list(gets) + list(mixes) + list(hops) + list(swaps)
    specs += [pl.BlockSpec(memory_space=pltpu.HBM)] * (len(operands) - len(specs))
    kinds = tuple("sum" + str(x.ndim - 3) for x in sums)
    kinds += tuple("get" + str(x.ndim - 2) for x in gets)
    kinds += ("mix",) * len(mixes) + ("hop",) * len(hops) + ("swap",) * len(swaps)
    outs, scratch = [], []
    if gather:
        outs.append(jax.ShapeDtypeStruct((count, rows, width), BF16))
    if reduce:
        outs.append(jax.ShapeDtypeStruct((rows, width), F32))
    if mode == "back":
        outs.append(jax.ShapeDtypeStruct((8, width), F32))
    lands = [x.shape[1:] if x.ndim == 3 else x.shape[:1] + x.shape[2:] for x in sums]
    outs += [
        jax.ShapeDtypeStruct(land, F32 if x.ndim == 3 else BF16) for land, x in zip(lands, sums)
    ]
    out_specs = [pl.BlockSpec(memory_space=VMEM)] * len(outs)
    if gather:
        out_specs[0] = pl.BlockSpec(memory_space=pltpu.HBM)
    outs += [
        jax.ShapeDtypeStruct((ring,) + x.shape if x.ndim == 2 else (count, ring) + x.shape[1:], BF16)
        for x in gets
    ]
    outs += [jax.ShapeDtypeStruct(x.shape, x.dtype) for x in list(mixes) + list(hops) + list(swaps)]
    out_specs += [pl.BlockSpec(memory_space=pltpu.HBM)] * (len(outs) - len(out_specs))
    dma = pltpu.SemaphoreType.DMA
    if reduce:
        taken = (6, rows // 2, width) if count == 8 else (half - 1, rows, width)
        scratch += [
            VMEM((half, rows, width), BF16),
            VMEM((half, rows, width), BF16),
            VMEM((half, rows, width), BF16),
            VMEM(taken, BF16),
            dma((half,)),
            dma((half,)),
            dma((half,)),
            dma(taken[:1]),
            dma(taken[:1]),
        ]
    if gather:
        scratch += [VMEM((rows, width), BF16), dma] + gather_sems(count)
    scratch += [VMEM((4 if ring == 4 else ring - 1,) + land, BF16) for land in lands]
    if kinds:
        most = max(ring, count if mixes else 0) - 1
        scratch += [dma((len(kinds), most)), dma((len(kinds), most)), dma((len(kinds),))]
    return pl.pallas_call(
        functools.partial(plane_kernel, count, ring, reduce, mode, gather, kinds),
        out_shape=tuple(outs),
        in_specs=specs,
        out_specs=tuple(out_specs),
        scratch_shapes=scratch,
        compiler_params=pltpu.CompilerParams(
            collective_id=call_id, has_side_effects=True, vmem_limit_bytes=16 * 1024 * 1024
        ),
        cost_estimate=pl.CostEstimate(
            flops=0, bytes_accessed=(60 if reduce else 30) << 20, transcendentals=0
        ),
    )(*operands)


def relay(source, target, sems, where, begin):
    copy = pltpu.make_async_remote_copy(
        src_ref=source,
        dst_ref=target,
        send_sem=sems[0],
        recv_sem=sems[1],
        device_id=where,
        device_id_type=MESH,
    )
    if begin:
        copy.start()
    return copy


def relay_begin(ring, me, plane, own, place, send_sem, recv_sem):
    for side, shift in ((0, 1), (1, -1)):
        there = (me, (plane + ring + shift) % ring)
        sems = (send_sem.at[side, 0], recv_sem.at[side, 0])

        @pl.when(plane < ring - 1 if side == 0 else plane > 0)
        def _(there=there, sems=sems):
            relay(own, place(plane), sems, there, True)


def relay_step(ring, me, plane, step, place, send_sem, recv_sem):
    for side, shift in ((0, 1), (1, -1)):
        there = (me, (plane + ring + shift) % ring)
        origin = (plane + ring - shift * step) % ring
        came = plane >= step if side == 0 else plane < ring - step
        more = plane < ring - 1 if side == 0 else plane > 0

        @pl.when(came)
        def _(side=side, there=there, origin=origin):
            block = place(origin)
            sems = (send_sem.at[side, step - 1], recv_sem.at[side, step - 1])
            relay(block, block, sems, there, False).wait_recv()

        if step < ring - 1:

            @pl.when(jnp.logical_and(came, more))
            def _(side=side, there=there, origin=origin):
                block = place(origin)
                sems = (send_sem.at[side, step], recv_sem.at[side, step])
                relay(block, block, sems, there, True)


def relay_end(ring, me, plane, place, send_sem, recv_sem):
    for step in range(ring - 1):
        for side, shift in ((0, 1), (1, -1)):
            there = (me, (plane + ring + shift) % ring)
            came = plane >= step if side == 0 else plane < ring - step
            more = plane < ring - 1 if side == 0 else plane > 0

            @pl.when(jnp.logical_and(came, more))
            def _(side=side, there=there):
                block = place(plane)
                sems = (send_sem.at[side, step], recv_sem.at[side, step])
                relay(block, block, sems, there, False).wait_send()


def first_kernel(count, ring, layers, talls, picks, *refs):
    refs = list(refs)
    token_ref, small_ref, asked_ref, flag_ref, store_ref = (refs.pop(0) for _ in range(5))
    column_refs = [refs.pop(0) for _ in range(2)]
    tall_refs = [refs.pop(0) for _ in range(talls)]
    full_ref, vector_ref, rows_ref, flags_ref = (refs.pop(0) for _ in range(4))
    wide_refs = [[refs.pop(0) for _ in range(layers)] for _ in range(2)]
    whole_refs = [refs.pop(0) for _ in picks]
    small_all = refs.pop(0)
    column_all = [refs.pop(0) for _ in range(2)]
    own_sem, own_ref = refs.pop(0), refs.pop(0)
    held_ref, total_ref, served_ref, held_sem = (refs.pop(0) for _ in range(4))
    (
        gather_send,
        gather_recv,
        pass_send,
        pass_recv,
        small_send,
        small_recv,
        across_send,
        across_recv,
        column_send,
        column_recv,
        relay_send,
        relay_recv,
        flag_send,
        flag_recv,
        rows_send,
        rows_recv,
    ) = refs
    me = lax.axis_index("dp")
    plane = lax.axis_index("ctx")
    hold = pltpu.make_async_copy(store_ref, held_ref, held_sem)
    hold.start()
    mates = [(me + k) % count for k in range(1, count)]
    planes = [(plane + j) % ring for j in range(1, ring)]
    greet_all([(mate, plane) for mate in mates] + [(me, there) for there in planes])

    stays = []

    def stay(source, target):
        copy = pltpu.make_async_copy(source, target, own_sem.at[len(stays)])
        copy.start()
        stays.append(copy)

    small_all[me, plane] = small_ref[...]
    smalls = [
        send(small_ref, small_all.at[me, plane], small_send.at[k], small_recv.at[k], (mate, plane))
        for k, mate in enumerate(mates)
    ]
    columns = []
    for i in range(2):
        pieces = 3 if i == 0 and len(column_refs[0].shape) == 3 else 1
        lanes = column_all[i].shape[-1] // pieces
        for n in range(pieces):

            def block(device, i=i, n=n, lanes=lanes, pieces=pieces):
                if len(column_refs[i].shape) == 4:
                    return column_refs[i].at[device]
                at = pl.multiple_of((n * count + device) * lanes, 128)
                return column_refs[i].at[:, :, pl.ds(at, lanes)]

            target = column_all[i].at[me]
            if pieces > 1:
                target = column_all[i].at[me, :, :, n * lanes : (n + 1) * lanes]
            stay(block(me), target)
            for k, mate in enumerate(mates):
                columns.append(
                    send(
                        block(mate),
                        target,
                        column_send.at[3 * i + n, k],
                        column_recv.at[3 * i + n, k],
                        (mate, plane),
                    )
                )
    column_stays = stays[:]
    pending = smalls + columns
    late = []
    for j, there in enumerate(planes):
        late.append(
            send(
                flag_ref.at[there],
                flags_ref.at[plane],
                flag_send.at[j],
                flag_recv.at[j],
                (me, there),
            )
        )
    flags_ref[plane] = flag_ref[plane]
    for copy in smalls:
        copy.wait_recv()
    across = [
        send(
            small_all.at[:, plane],
            small_all.at[:, plane],
            across_send.at[j],
            across_recv.at[j],
            (me, there),
        )
        for j, there in enumerate(planes)
    ]

    relays = []

    def spread(own, place):
        n = len(relays)
        relays.append((place, relay_send.at[n], relay_recv.at[n]))
        stay(own, place(plane))
        relay_begin(ring, me, plane, own, *relays[-1])

    def spread_tall(i):
        array, layer = picks[i]
        spread(tall_refs[array].at[layer], lambda p: whole_refs[i].at[p])

    for i in range(2):
        spread_tall(i)
    for copy in across:
        copy.wait_recv()
    groups = vector_ref.shape[1] // 128
    members = count * ring // groups
    for group in range(groups):
        total = small_all[group * members // ring, group * members % ring]
        for n in range(group * members + 1, (group + 1) * members):
            total = total + small_all[n // ring, n % ring]
        vector_ref[:, group * 128 : (group + 1) * 128] = total
    unit, _ = norm_parts(token_ref[...].astype(F32))
    own_ref[...] = (unit * vector_ref[0:1, :] + vector_ref[1:2, :]).astype(BF16)
    stay(own_ref, full_ref.at[me])
    sends = gather_begin(count, me, plane, own_ref, full_ref, gather_send, gather_recv)
    for copy in columns:
        copy.wait_recv()
    for copy in column_stays:
        copy.wait()
    for layer in range(layers):
        for i in range(2):
            spread(
                column_all[i].at[:, layer],
                lambda p, layer=layer, i=i: wide_refs[i][layer].at[:, p],
            )
    for i in range(2, len(picks)):
        spread_tall(i)
    hold.wait()
    size = served_ref.shape[1]
    depth = min(1024, held_ref.shape[0])

    def rows_copy(k):
        mate = (me + k) % count
        return pltpu.make_async_remote_copy(
            src_ref=served_ref.at[mate],
            dst_ref=rows_ref.at[me],
            send_sem=rows_send.at[k - 1],
            recv_sem=rows_recv.at[k - 1],
            device_id=(mate, plane),
            device_id_type=MESH,
        )

    def pick(k):
        mate = (me + k) % count
        wanted = asked_ref[pl.ds(pl.multiple_of(mate * size, 8), size), :]
        total_ref[...] = jnp.zeros_like(total_ref)

        def look(n, carry):
            at = pl.ds(pl.multiple_of(n * depth, depth), depth)
            marks = wanted == n * depth + lax.broadcasted_iota(jnp.int32, (size, depth), 1)
            total_ref[...] += dot(marks.astype(F32).astype(BF16), held_ref[at, :])
            return carry

        lax.fori_loop(0, held_ref.shape[0] // depth, look, 0)
        served_ref[mate] = total_ref[...].astype(BF16)

    def serve(k, carry):
        pick(k)
        rows_copy(k).start()
        return carry

    serve(1, 0)
    passes = gather_middle(
        count, me, plane, full_ref, sends, gather_send, gather_recv, pass_send, pass_recv
    )
    lax.fori_loop(2, count // 2, serve, 0)
    for one in relays:
        relay_step(ring, me, plane, 1, *one)
    lax.fori_loop(count // 2, count - 1, serve, 0)
    for one in relays:
        relay_step(ring, me, plane, 2, *one)
    serve(count - 1, 0)
    pick(0)
    stay(served_ref.at[me], rows_ref.at[me])
    for step in range(3, ring):
        for one in relays:
            relay_step(ring, me, plane, step, *one)
    pending += gather_end(count, me, plane, full_ref, sends, passes, pass_send, pass_recv)
    for copy in late:
        copy.wait_recv()

    def rows_done(k, carry):
        rows_copy(k).wait()
        return carry

    lax.fori_loop(1, count, rows_done, 0)
    for copy in stays[len(column_stays) :]:
        copy.wait()
    for copy in pending + across + late:
        copy.wait_send()
    for one in relays:
        relay_end(ring, me, plane, *one)


def first_exchange(
    count, ring, call_id, tokens, small, asked, flags, store, joint, expand, talls, picks
):
    rows, width = tokens.shape
    layers, part = talls[0].shape[0], joint.shape[-2]
    size = asked.shape[0] // count
    columns = []
    for x in (joint, expand):
        columns.append((count, layers, part, x.shape[-1] if x.ndim == 4 else x.shape[-1] // count))
    dma = pltpu.SemaphoreType.DMA
    near, far = pl.BlockSpec(memory_space=VMEM), pl.BlockSpec(memory_space=pltpu.HBM)
    outs = [
        jax.ShapeDtypeStruct((count, rows, width), BF16),
        jax.ShapeDtypeStruct((16, width), F32),
        jax.ShapeDtypeStruct((count, size, width), BF16),
        jax.ShapeDtypeStruct(flags.shape, flags.dtype),
    ]
    for shape in columns:
        outs += [jax.ShapeDtypeStruct((count, ring) + shape[2:], BF16)] * layers
    outs += [jax.ShapeDtypeStruct((ring,) + talls[i].shape[1:], BF16) for i, _ in picks]

    def pair(*shape):
        return [dma(shape), dma(shape)]

    return pl.pallas_call(
        functools.partial(first_kernel, count, ring, layers, len(talls), picks),
        out_shape=tuple(outs),
        in_specs=[near] * 4 + [far] * (3 + len(talls)),
        out_specs=tuple([far, near, far, near] + [far] * (2 * layers + len(picks))),
        scratch_shapes=[
            VMEM((count, ring, 16, 128), F32),
            VMEM(columns[0], BF16),
            VMEM(columns[1], BF16),
            dma((6 + 2 * layers + len(picks),)),
            VMEM((rows, width), BF16),
            VMEM(store.shape, BF16),
            VMEM((size, width), F32),
            VMEM((count, size, width), BF16),
            dma,
        ]
        + gather_sems(count)
        + pair(count - 1)
        + pair(ring - 1)
        + pair(4, count - 1)
        + pair(2 * layers + len(picks), 2, ring - 1)
        + pair(ring - 1)
        + pair(count - 1),
        compiler_params=pltpu.CompilerParams(
            collective_id=call_id, has_side_effects=True, vmem_limit_bytes=40 * 1024 * 1024
        ),
        cost_estimate=pl.CostEstimate(flops=0, bytes_accessed=200 << 20, transcendentals=0),
    )(tokens, small, asked, flags, store, joint, expand, *talls)


def last_kernel(
    count,
    ring,
    layers,
    sums_ref,
    wide_ref,
    rows_ref,
    *refs,
):
    refs = list(refs)
    joint_refs = [refs.pop(0) for _ in range(layers - 1)]
    expand_refs = [refs.pop(0) for _ in range(layers)]
    total_ref, joint_grad_ref, expand_grad_ref, home_ref = (refs.pop(0) for _ in range(4))
    sums_in, across_ref, mixed_ref, rows_in = (refs.pop(0) for _ in range(4))
    (
        own_sem,
        swap_send,
        swap_recv,
        sums_send,
        sums_recv,
        wide_send,
        wide_recv,
        across_send,
        across_recv,
    ) = refs
    me = lax.axis_index("dp")
    plane = lax.axis_index("ctx")
    partner, away = partner_of(me, plane, ring)
    greet = [((me + k) % count, plane) for k in range(1, count)]
    greet += [(me, (plane + j) % ring) for j in range(1, ring)]
    greet_all(greet, partner, away)

    pending, sums = [], []
    for k in range(1, count):
        there = (me + k) % count
        sums.append(
            send(
                sums_ref.at[there],
                sums_in.at[me],
                sums_send.at[k - 1],
                sums_recv.at[k - 1],
                (there, plane),
            )
        )
    swap = swap_begin(rows_ref, rows_in, swap_send, swap_recv, partner, away)
    for k in range(1, count):
        there = (me + k) % count
        pending.append(
            send(
                wide_ref.at[there],
                mixed_ref.at[me],
                wide_send.at[k - 1],
                wide_recv.at[k - 1],
                (there, plane),
            )
        )
    sums_in[me] = sums_ref[me]
    stay = pltpu.make_async_copy(wide_ref.at[me], mixed_ref.at[me], own_sem)
    stay.start()
    for copy in sums:
        copy.wait_recv()
    total = sums_in[0]
    for k in range(1, count):
        total = total + sums_in[k]
    across_ref[plane] = total
    across = [
        send(
            across_ref.at[plane],
            across_ref.at[plane],
            across_send.at[j - 1],
            across_recv.at[j - 1],
            (me, (plane + j) % ring),
        )
        for j in range(1, ring)
    ]
    inner = expand_refs[0].shape[2]
    size = wide_ref.shape[2] // 3
    for layer in range(layers):
        for k in range(count):
            expand_grad_ref[layer, :, k * inner : (k + 1) * inner] = expand_refs[layer][k].astype(F32)

    def spread(layer, ref):
        for k in range(count):
            for i in range(3):
                at = (i * count + k) * size
                joint_grad_ref[layer, :, at : at + size] = ref[
                    k, :, i * size : (i + 1) * size
                ].astype(F32)

    for layer in range(1, layers):
        spread(layer, joint_refs[layer - 1])
    for copy in across:
        copy.wait_recv()
    total = across_ref[0]
    for j in range(1, ring):
        total = total + across_ref[j]
    total_ref[...] = total
    for copy in pending:
        copy.wait_recv()
    stay.wait()
    spread(0, mixed_ref)
    swap_end(swap)
    home_ref[...] = rows_in[...].astype(F32)
    for copy in pending + sums + across:
        copy.wait_send()


def last_exchange(count, ring, call_id, sums, wide, rows, joints, expands):
    dma = pltpu.SemaphoreType.DMA
    layers = len(expands)
    part = wide.shape[1]
    operands = (sums, wide, rows, *joints, *expands)
    outs = (
        jax.ShapeDtypeStruct(sums.shape[1:], F32),
        jax.ShapeDtypeStruct((layers, part, count * wide.shape[2]), F32),
        jax.ShapeDtypeStruct((layers, part, count * expands[0].shape[2]), F32),
        jax.ShapeDtypeStruct(rows.shape, F32),
    )
    spec = pl.BlockSpec(memory_space=VMEM)
    return pl.pallas_call(
        functools.partial(last_kernel, count, ring, layers),
        out_shape=outs,
        in_specs=[spec] * len(operands),
        out_specs=(spec,) * len(outs),
        scratch_shapes=[
            VMEM(sums.shape, F32),
            VMEM((ring,) + sums.shape[1:], F32),
            VMEM(wide.shape, BF16),
            VMEM(rows.shape, BF16),
            dma,
            dma,
            dma,
            dma((count - 1,)),
            dma((count - 1,)),
            dma((count - 1,)),
            dma((count - 1,)),
            dma((ring - 1,)),
            dma((ring - 1,)),
        ],
        compiler_params=pltpu.CompilerParams(
            collective_id=call_id, has_side_effects=True, vmem_limit_bytes=16 * 1024 * 1024
        ),
    )(*operands)


GATE_SCALE = math.sqrt(2.0 / math.pi)
GATE_CUBE = 0.044715


def after(*arrays):
    return lax.optimization_barrier(arrays)


def dot(left, right):
    return jnp.dot(left, right, preferred_element_type=F32)


def contract_rows(left, right):
    return lax.dot_general(left, right, (((0,), (0,)), ((), ())), preferred_element_type=F32)


def contract_cols(left, right):
    return lax.dot_general(left, right, (((1,), (1,)), ((), ())), preferred_element_type=F32)


def local_call(body, outs, operands, grid, in_specs, out_specs, scratch=(), flops=0):
    moved = sum(math.prod(x.shape) * x.dtype.itemsize for x in list(operands) + list(outs))
    return pl.pallas_call(
        body,
        out_shape=tuple(outs),
        grid=grid,
        in_specs=in_specs,
        out_specs=tuple(out_specs),
        scratch_shapes=list(scratch),
        compiler_params=pltpu.CompilerParams(vmem_limit_bytes=32 * 1024 * 1024),
        cost_estimate=pl.CostEstimate(flops=flops, bytes_accessed=moved, transcendentals=0),
    )(*operands)


def whole(x):
    return pl.BlockSpec(x.shape, lambda *_, n=len(x.shape): (0,) * n)


def stripe(shape):
    return pl.BlockSpec(shape, lambda i: (i,) + (0,) * (len(shape) - 1))


def probabilities(queries, keys, begin):
    scores = contract_cols(queries, keys) * (queries.shape[-1] ** (-0.5))
    row = begin + lax.broadcasted_iota(jnp.int32, scores.shape, 0)
    allowed = row >= lax.broadcasted_iota(jnp.int32, scores.shape, 1)
    scores = jnp.where(allowed, scores, FLOOR)
    raised = jnp.exp(scores - jnp.max(scores, axis=-1, keepdims=True))
    return raised / jnp.sum(raised, axis=-1, keepdims=True)


def attend_kernel(heads, block, x_ref, joint_ref, project_ref, packed_ref, attended_ref, partial_ref):
    packed_ref[...] = dot(x_ref[...], joint_ref[...]).astype(BF16)
    length, width = attended_ref.shape
    size = width // heads
    for head in range(heads):
        at = head * size
        for begin in range(0, length, block):
            end = begin + block
            probs = probabilities(
                packed_ref[begin:end, at : at + size], packed_ref[:end, width + at : width + at + size], begin
            )
            values = packed_ref[:end, 2 * width + at : 2 * width + at + size]
            attended_ref[begin:end, at : at + size] = dot(probs.astype(BF16), values).astype(BF16)
    partial_ref[...] = dot(attended_ref[...], project_ref[...]).astype(BF16)


def attend(normed, joint, project, seqs, heads):
    rows, width = normed.shape
    length, inner = rows // seqs, project.shape[0]
    outs = [
        jax.ShapeDtypeStruct((rows, 3 * inner), BF16),
        jax.ShapeDtypeStruct((rows, inner), BF16),
        jax.ShapeDtypeStruct((rows, width), BF16),
    ]
    return local_call(
        functools.partial(attend_kernel, heads, min(256, length)),
        outs,
        (normed, joint, project),
        (seqs,),
        [stripe((length, width)), whole(joint), whole(project)],
        [stripe((length, 3 * inner)), stripe((length, inner)), stripe((length, width))],
        flops=8 * rows * width * inner,
    )


def attend_backward_kernel(
    heads,
    block,
    grad_ref,
    x_ref,
    packed_ref,
    attended_ref,
    joint_ref,
    project_ref,
    joint_grad_ref,
    project_grad_ref,
    partial_ref,
    joint_sum,
    project_sum,
    key_sum,
    value_sum,
    low_ref,
):
    step = pl.program_id(0)
    length, width = attended_ref.shape
    size = width // heads
    scale = size ** (-0.5)
    grad = contract_cols(grad_ref[...], project_ref[...]).astype(BF16)
    key_sum[...] = jnp.zeros_like(key_sum)
    value_sum[...] = jnp.zeros_like(value_sum)
    for head in range(heads):
        at = head * size
        for begin in range(0, length, block):
            end = begin + block
            queries = packed_ref[begin:end, at : at + size]
            keys = packed_ref[:end, width + at : width + at + size]
            values = packed_ref[:end, 2 * width + at : 2 * width + at + size]
            here = grad[begin:end, at : at + size]
            probs = probabilities(queries, keys, begin)
            grad_probs = contract_cols(here, values)
            delta = jnp.sum(probs * grad_probs, axis=-1, keepdims=True)
            grad_scores = (probs * (grad_probs - delta)).astype(BF16)
            low_ref[begin:end, at : at + size] = (dot(grad_scores, keys) * scale).astype(BF16)
            key_sum[:end, at : at + size] += contract_rows(grad_scores, queries) * scale
            value_sum[:end, at : at + size] += contract_rows(probs.astype(BF16), here)
    low_ref[:, width : 2 * width] = key_sum[...].astype(BF16)
    low_ref[:, 2 * width :] = value_sum[...].astype(BF16)
    partial_ref[...] = contract_cols(low_ref[...], joint_ref[...]).astype(BF16)
    joint_part = contract_rows(x_ref[...], low_ref[...])
    project_part = contract_rows(attended_ref[...], grad_ref[...])

    @pl.when(step == 0)
    def _():
        joint_sum[...] = joint_part
        project_sum[...] = project_part

    @pl.when(step > 0)
    def _():
        joint_sum[...] += joint_part
        project_sum[...] += project_part

    @pl.when(step == pl.num_programs(0) - 1)
    def _():
        joint_grad_ref[...] = joint_sum[...].astype(BF16)
        project_grad_ref[...] = project_sum[...].astype(BF16)


def attend_backward(grad_out, normed, packed, attended, joint, project, seqs, heads):
    rows, width = normed.shape
    length, inner = rows // seqs, project.shape[0]
    outs = [
        jax.ShapeDtypeStruct(joint.shape, BF16),
        jax.ShapeDtypeStruct(project.shape, BF16),
        jax.ShapeDtypeStruct((rows, width), BF16),
    ]
    return local_call(
        functools.partial(attend_backward_kernel, heads, min(256, length)),
        outs,
        (grad_out, normed, packed, attended, joint, project),
        (seqs,),
        [
            stripe((length, width)),
            stripe((length, width)),
            stripe((length, 3 * inner)),
            stripe((length, inner)),
            whole(joint),
            whole(project),
        ],
        [whole(outs[0]), whole(outs[1]), stripe((length, width))],
        [
            VMEM(joint.shape, F32),
            VMEM(project.shape, F32),
            VMEM((length, inner), F32),
            VMEM((length, inner), F32),
            VMEM((length, 3 * inner), BF16),
        ],
        flops=16 * rows * width * inner,
    )


def forward_kernel(x_ref, expand_ref, shrink_ref, inner_ref, partial_ref):
    inner = dot(x_ref[...], expand_ref[...])
    inner_ref[...] = inner
    turn = jnp.tanh(GATE_SCALE * (inner + GATE_CUBE * (inner * inner * inner)))
    active = (0.5 * inner * (1.0 + turn)).astype(BF16)
    partial_ref[...] = dot(active, shrink_ref[...]).astype(BF16)


def forward(normed, expand, shrink):
    rows, width = normed.shape
    inner, block = expand.shape[1], 256
    outs = [jax.ShapeDtypeStruct((rows, inner), F32), jax.ShapeDtypeStruct((rows, width), BF16)]
    return local_call(
        forward_kernel,
        outs,
        (normed, expand, shrink),
        (rows // block,),
        [stripe((block, width)), whole(expand), whole(shrink)],
        [stripe((block, inner)), stripe((block, width))],
        flops=4 * rows * width * inner,
    )


def backward_kernel(
    branch_ref,
    x_ref,
    inner_ref,
    expand_ref,
    shrink_ref,
    expand_grad_ref,
    shrink_grad_ref,
    partial_ref,
    expand_sum,
    shrink_sum,
):
    step = pl.program_id(0)
    branch, inner = branch_ref[...], inner_ref[...]
    square = inner * inner
    turn = jnp.tanh(GATE_SCALE * (inner + GATE_CUBE * (square * inner)))
    active = (0.5 * inner * (1.0 + turn)).astype(BF16)
    slope = GATE_SCALE * (1.0 + (3.0 * GATE_CUBE) * square)
    slope = 0.5 * (1.0 + turn) + 0.5 * inner * (1.0 - turn * turn) * slope
    grad_inner = (contract_cols(branch, shrink_ref[...]) * slope).astype(BF16)
    partial_ref[...] = contract_cols(grad_inner, expand_ref[...]).astype(BF16)
    expand_part = contract_rows(x_ref[...], grad_inner)
    shrink_part = contract_rows(active, branch)

    @pl.when(step == 0)
    def _():
        expand_sum[...] = expand_part
        shrink_sum[...] = shrink_part

    @pl.when(step > 0)
    def _():
        expand_sum[...] += expand_part
        shrink_sum[...] += shrink_part

    @pl.when(step == pl.num_programs(0) - 1)
    def _():
        expand_grad_ref[...] = expand_sum[...].astype(BF16)
        shrink_grad_ref[...] = shrink_sum[...].astype(BF16)


def backward(branch, normed, inner, expand, shrink):
    rows, width = normed.shape
    block = 256
    outs = [
        jax.ShapeDtypeStruct(expand.shape, BF16),
        jax.ShapeDtypeStruct(shrink.shape, BF16),
        jax.ShapeDtypeStruct((rows, width), BF16),
    ]
    return local_call(
        backward_kernel,
        outs,
        (branch, normed, inner, expand, shrink),
        (rows // block,),
        [
            stripe((block, width)),
            stripe((block, width)),
            stripe((block, inner.shape[1])),
            whole(expand),
            whole(shrink),
        ],
        [whole(outs[0]), whole(outs[1]), stripe((block, width))],
        [VMEM(expand.shape, F32), VMEM(shrink.shape, F32)],
        flops=8 * rows * width * inner.shape[1],
    )


def ranks_of(flags):
    planes, groups, rows = flags.shape
    upto = jnp.arange(rows)[:, None] <= jnp.arange(rows)[None, :]
    inside = dot(flags.astype(BF16), upto.astype(BF16))
    before = jnp.where(
        jnp.arange(groups)[None, :, None] < jnp.arange(groups)[None, None, :],
        inside[:, :, -1:],
        0.0,
    )
    rank = inside + jnp.sum(before, axis=1)[:, :, None]
    return rank.reshape(planes, groups * rows), rank[:, -1, -1]


def pieces_of(values, terms):
    pieces = []
    for _ in range(terms):
        pieces.append(values.astype(BF16))
        values = values - pieces[-1].astype(F32)
    return jnp.concatenate(pieces, axis=0)


def recall_kernel(
    tile,
    hidden_ref,
    vector_ref,
    cotangent_ref,
    token_ref,
    stored_ref,
    mixed_ref,
    grad_ref,
    sums_ref,
    scaled_ref,
    pull_ref,
):
    rows, width = hidden_ref.shape
    tiles = stored_ref.shape[0] // tile
    unit, inverse = norm_parts(hidden_ref[...])
    gains = vector_ref[8:9, :]
    query = unit * gains + vector_ref[9:10, :]
    scale = DISTANCE_SCALE * math.sqrt(width)
    terms = jnp.concatenate([pieces_of(query, 3), cotangent_ref[...]], axis=0)
    ones = jnp.ones((8, width), BF16)

    def look(n, carry):
        at = pl.ds(pl.multiple_of(n * tile, tile), tile)
        stored = stored_ref[at, :]
        near = contract_cols(terms, stored)
        squares = jnp.square(stored.astype(F32))
        high = squares.astype(BF16)
        low = (squares - high.astype(F32)).astype(BF16)
        lengths = (contract_cols(ones, high) + contract_cols(ones, low))[0:1, :]
        scaled_ref[:, at] = (
            2.0 * (near[:rows] + (near[rows : 2 * rows] + near[2 * rows : 3 * rows])) - lengths
        ) / scale
        pull_ref[:, at] = RECALL_SHARE * near[3 * rows :]
        return carry

    lax.fori_loop(0, tiles, look, 0)
    usable = token_ref[...] == lax.broadcasted_iota(jnp.int32, scaled_ref.shape, 0)
    scaled = jnp.where(usable, scaled_ref[...], FLOOR)
    raised = jnp.where(usable, jnp.exp(scaled - jnp.max(scaled, axis=1, keepdims=True)), 0.0)
    weights = raised / jnp.sum(raised, axis=1, keepdims=True)
    pull = pull_ref[...]
    grad_scaled = weights * (pull - jnp.sum(weights * pull, axis=1, keepdims=True))
    scaled_ref[...] = weights
    pull_ref[...] = grad_scaled
    rest = jnp.sum(grad_scaled, axis=1, keepdims=True)

    def gather(n, total):
        at = pl.ds(pl.multiple_of(n * tile, tile), tile)
        both = jnp.concatenate(
            [pieces_of(scaled_ref[:, at], 2), pieces_of(pull_ref[:, at], 2)], axis=0
        )
        return total + dot(both, stored_ref[at, :])

    total = lax.fori_loop(0, tiles, gather, jnp.zeros((4 * rows, width), F32))
    recalled = total[:rows] + total[rows : 2 * rows]
    moved = total[2 * rows : 3 * rows] + total[3 * rows :] - rest * query
    mixed_ref[...] = (1.0 - RECALL_SHARE) * query + RECALL_SHARE * recalled
    grad_query = (1.0 - RECALL_SHARE) * cotangent_ref[...].astype(F32) + moved * (2.0 / scale)
    sums_ref[0:1, :] = jnp.sum(grad_query * unit, axis=0, keepdims=True)
    sums_ref[1:2, :] = jnp.sum(grad_query, axis=0, keepdims=True)
    grad_ref[...] = norm_backward(grad_query, unit, inverse, gains)


def recall_padded(hidden, vectors, stored, usable, cotangent):
    unit, inverse = norm_parts(hidden)
    query = unit * vectors[8] + vectors[9]
    scale = DISTANCE_SCALE * math.sqrt(query.shape[-1])
    stored, cotangent = stored.astype(F32), cotangent.astype(F32)
    distance = jnp.sum(jnp.square(query[None] - stored), axis=-1)
    pull = RECALL_SHARE * jnp.sum(cotangent[None] * stored, axis=-1)
    scaled = jnp.where(usable, -distance / scale, FLOOR)
    raised = jnp.where(usable, jnp.exp(scaled - jnp.max(scaled, axis=0, keepdims=True)), 0.0)
    weights = raised / jnp.sum(raised, axis=0, keepdims=True)
    grad_scaled = weights * (pull - jnp.sum(weights * pull, axis=0, keepdims=True))
    recalled = jnp.sum(weights[..., None] * stored, axis=0)
    moved = jnp.sum(grad_scaled[..., None] * stored, axis=0)
    moved = moved - jnp.sum(grad_scaled, axis=0)[:, None] * query
    mixed = (1.0 - RECALL_SHARE) * query + RECALL_SHARE * recalled
    grad_query = (1.0 - RECALL_SHARE) * cotangent + moved * (2.0 / scale)
    sums = jnp.stack([jnp.sum(grad_query * unit, axis=0), jnp.sum(grad_query, axis=0)])
    grad = norm_backward(grad_query, unit, inverse, vectors[8])
    return mixed, grad, jnp.pad(sums, ((0, 6), (0, 0)))


def recall(hidden, vectors, stored, token_of, cotangent):
    rows, width = hidden.shape
    entries = stored.shape[0]
    operands = (hidden, vectors, cotangent, token_of.reshape(1, entries), stored)
    outs = [
        jax.ShapeDtypeStruct((rows, width), F32),
        jax.ShapeDtypeStruct((rows, width), F32),
        jax.ShapeDtypeStruct((8, width), F32),
    ]
    return local_call(
        functools.partial(recall_kernel, min(512, entries)),
        outs,
        operands,
        (1,),
        [whole(x) for x in operands],
        [whole(x) for x in outs],
        [VMEM((rows, entries), F32), VMEM((rows, entries), F32)],
        flops=16 * rows * width * entries,
    )


def shards(
    tokens,
    ln1_gain,
    ln1_bias,
    qkv_weight,
    out_weight,
    ln2_gain,
    ln2_bias,
    in_weight,
    fc_weight,
    final_gain,
    final_bias,
    datastore,
    neighbour_owner,
    neighbour_row,
    neighbour_count,
    cotangent,
):
    local_seqs, local_rows, width = tokens.shape
    rows = local_seqs * local_rows
    count, ring = lax.axis_size("dp"), lax.axis_size("ctx")
    devices = count * ring
    both = ("dp", "ctx")
    seqs = count * local_seqs // ring
    heads = HEADS // count
    slots = neighbour_owner.shape[2]
    part = width // devices
    head_width = width // count
    inner_width = in_weight.shape[2] // count

    forth = []
    for s in range(count):
        for p in range(ring):
            forth.append((s * ring + p, ((s // ring) * ring + p) * ring + s % ring))

    pair_room = -(-(3 * rows * slots) // (2 * devices * 16)) * 16
    room = rows * slots // ring
    owners = neighbour_owner.reshape(rows, slots)
    live = neighbour_count.reshape(rows, 1)
    hits = (owners[:, :, None] == jnp.arange(devices)[None, None, :]) & (
        jnp.arange(slots)[None, :, None] < live[:, :, None]
    )
    asked_all = jnp.sum(jnp.where(hits, neighbour_row.reshape(rows, slots, 1), 0), axis=1).T
    usable_all = jnp.any(hits, axis=1).T
    upto = jnp.arange(rows)[:, None] <= jnp.arange(rows)[None, :]
    order = dot(usable_all.astype(BF16), upto.astype(BF16))
    taken = usable_all[:, None, :] & (
        order[:, None, :] == jnp.arange(1, pair_room + 1, dtype=F32)[None, :, None]
    )
    asked = jnp.sum(jnp.where(taken, asked_all[:, None, :], 0), axis=-1)
    asked = lax.all_to_all(asked, both, split_axis=0, concat_axis=0, tiled=True)
    asked = asked.reshape(count // ring, ring, ring, pair_room).swapaxes(1, 2)

    def by_plane(x):
        return x.reshape((count, ring) + x.shape[1:]).swapaxes(0, 1)

    token_at = by_plane(jnp.sum(jnp.where(taken, jnp.arange(rows)[None, None, :], 0), axis=-1))
    amounts = order[:, -1]
    usable = by_plane(jnp.arange(pair_room, dtype=F32)[None, :] < amounts[:, None])
    crowded = (jnp.max(amounts) > pair_room) | (jnp.max(jnp.sum(by_plane(amounts), axis=1)) > room)

    small = jnp.stack(
        [ln1_gain[0], ln1_bias[0], ln1_gain[1], ln1_bias[1], ln2_gain[0], ln2_bias[0]]
        + [ln2_gain[1], ln2_bias[1], final_gain, final_bias]
    ).astype(F32)
    small = jnp.concatenate([small, jnp.broadcast_to(crowded.astype(F32), (1, part))])
    here = lax.axis_index("dp") * ring + lax.axis_index("ctx")
    places = 128 // part
    small = jnp.tile(jnp.pad(small, ((0, 5), (0, 0))), (1, places))
    small = jnp.where(jnp.arange(128)[None, :] // part == here % places, small, 0.0)

    joint_own, expand_own = qkv_weight, in_weight
    if head_width % 128:
        joint_own = qkv_weight.reshape(LAYERS, part, 3, count, head_width).transpose(3, 0, 1, 2, 4)
        joint_own = joint_own.reshape(count, LAYERS, part, 3 * head_width)
        expand_own = in_weight.reshape(LAYERS, part, count, inner_width).transpose(2, 0, 1, 3)

    notes = jnp.concatenate([usable.astype(jnp.int32), token_at], axis=-1)
    my_tokens = lax.ppermute(tokens.reshape(rows, width), both, forth)
    notes = lax.ppermute(notes, both, forth)
    usable, token_at = notes[..., :pair_room], notes[..., pair_room:]
    last_all = lax.all_gather(fc_weight[1], "ctx", axis=0, tiled=False)
    exchange = functools.partial(plane_exchange, count, ring)
    first = first_exchange(
        count,
        ring,
        0,
        my_tokens,
        small,
        asked.reshape(-1, 1),
        usable,
        datastore,
        joint_own,
        expand_own,
        (out_weight, fc_weight),
        ((0, 0), (1, 0), (0, 1)),
    )
    normed, vectors, served, flags = first[:4]
    joint, expand = list(first[4 : 4 + LAYERS]), list(first[4 + LAYERS : 4 + 2 * LAYERS])
    project, shrink = [first[-3], first[-1]], [first[-2], None]
    gain_one, shift_one = [vectors[0], vectors[2]], [vectors[1], vectors[3]]
    gain_two, shift_two = [vectors[4], vectors[6]], [vectors[5], vectors[7]]
    crowded = jnp.max(vectors[10]) > 0.5
    rank, _ = ranks_of(flags)
    served = served.reshape(count, ring, pair_room, width)

    chosen = flags.reshape(ring, 1, count * pair_room) * (
        rank[:, None, :] == jnp.arange(1, room + 1, dtype=F32)[None, :, None]
    )
    stored = jnp.einsum(
        "cpdt,dctw->cpw",
        chosen.astype(BF16).reshape(ring, room, count, pair_room),
        served,
        preferred_element_type=F32,
    ).astype(BF16)
    stored = lax.all_to_all(stored, "ctx", split_axis=0, concat_axis=0, tiled=True)

    hidden = my_tokens.astype(F32)
    saved = []
    for layer in range(LAYERS):
        normed = normed.reshape(count * rows, width)
        joint[layer] = joint[layer].reshape(width, 3 * head_width)
        project[layer] = project[layer].reshape(-1, width)
        packed, attended, partial = attend(normed, joint[layer], project[layer], seqs, heads)
        partial = partial.reshape(count, rows, width)
        normed_two, middle = exchange(2, partial, hidden, gain_two[layer], shift_two[layer])
        if layer + 1 == LAYERS:
            shrink[layer], normed_two = after(last_all, normed_two)
        normed_two = normed_two.reshape(count * rows, width)
        expand[layer] = expand[layer].reshape(width, inner_width)
        shrink[layer] = shrink[layer].reshape(-1, width)
        inner, partial = forward(normed_two, expand[layer], shrink[layer])
        partial = partial.reshape(count, rows, width)
        saved.append((hidden, normed, packed, attended, middle, normed_two, inner))
        if layer + 1 < LAYERS:
            normed, hidden = exchange(
                2, partial, middle, gain_one[layer + 1], shift_one[layer + 1]
            )
        else:
            hidden, my_cotangent = exchange(
                5, partial, middle, gather=False, swaps=(cotangent.reshape(rows, width),)
            )

    def few():
        rank, _ = ranks_of(usable)
        chosen = (usable.reshape(ring, 1, -1) > 0) & (
            rank[:, None, :] == jnp.arange(1, room + 1, dtype=F32)[None, :, None]
        )
        token_of = jnp.sum(jnp.where(chosen, token_at.reshape(ring, 1, -1) + 1, 0), axis=-1) - 1
        entries = stored.reshape(ring * room, width)
        return recall(hidden, vectors, entries, token_of.reshape(-1), my_cotangent)

    def many():
        asked = lax.all_to_all(asked_all, both, split_axis=0, concat_axis=0, tiled=True)
        padded = datastore.at[asked.reshape(-1)].get(mode="promise_in_bounds")
        padded = padded.reshape(devices, rows, width)
        padded = lax.all_to_all(padded, both, split_axis=0, concat_axis=0, tiled=True)
        padded = lax.ppermute(padded, both, forth)
        marks = lax.ppermute(usable_all.astype(jnp.int32), both, forth)
        return recall_padded(hidden, vectors, padded, marks > 0, my_cotangent)

    mixed, grad_hidden, head_sums = lax.cond(crowded, many, few)
    branch, mixed = exchange(6, base=grad_hidden, swaps=(mixed.astype(BF16),))
    sums_one, sums_two = [None] * LAYERS, [None] * LAYERS
    joint_sums, expand_sums = [None] * LAYERS, [None] * LAYERS
    grad_tall = [None] * LAYERS
    for layer in reversed(range(LAYERS)):
        start, normed, packed, attended, middle, normed_two, inner = saved[layer]
        grad_expand, grad_shrink, partial = backward(
            branch.reshape(count * rows, width), normed_two, inner, expand[layer], shrink[layer]
        )
        grad_expand = grad_expand.reshape(count, ring, part, inner_width)
        grad_shrink = grad_shrink.reshape(ring, -1, width)
        cut = grad_shrink.shape[1] // 2
        grad_out, grad_middle, sums_two[layer], upper_sum, expand_sum = exchange(
            7,
            partial.reshape(count, rows, width),
            grad_hidden,
            gain_two[layer],
            saved=middle,
            sums=(grad_shrink[:, :cut], grad_expand),
        )
        expand_sums[layer] = expand_sum
        grad_joint, grad_project, partial = attend_backward(
            grad_out.reshape(count * rows, width),
            normed,
            packed,
            attended,
            joint[layer],
            project[layer],
            seqs,
            heads,
        )
        rides = (
            grad_project.reshape(ring, part, width),
            grad_shrink[:, cut:],
            grad_joint.reshape(count, ring, part, 3 * head_width),
        )
        partial = partial.reshape(count, rows, width)
        if layer > 0:
            branch, grad_hidden, sums_one[layer], project_sum, lower_sum, joint_sum = exchange(
                8, partial, grad_middle, gain_one[layer], saved=start, sums=rides
            )
        else:
            grad_hidden, sums_one[layer], project_sum, lower_sum, joint_sum, *mixes = exchange(
                9,
                partial,
                grad_middle,
                gain_one[layer],
                saved=start,
                gather=False,
                sums=rides,
                mixes=tuple(joint_sums[1:]) + tuple(expand_sums),
            )
        shrink_sum = jnp.concatenate([upper_sum, lower_sum], axis=0)
        joint_sums[layer] = joint_sum
        grad_tall[layer] = (project_sum, shrink_sum)

    sums = jnp.concatenate(
        [sums_one[0][:2], sums_one[1][:2], sums_two[0][:2], sums_two[1][:2], head_sums[:2]]
    )
    sums = jnp.pad(sums, ((0, 6), (0, 0))).reshape(16, count, head_width).transpose(1, 0, 2)
    sums, qkv_grad, in_grad, tokens_grad = last_exchange(
        count,
        ring,
        10,
        sums,
        joint_sums[0],
        grad_hidden.astype(BF16),
        mixes[: LAYERS - 1],
        mixes[LAYERS - 1 :],
    )
    sums = lax.dynamic_slice_in_dim(sums, lax.axis_index("ctx") * part, part, axis=1)

    return (
        mixed.astype(F32).reshape(local_seqs, local_rows, width),
        tokens_grad.reshape(local_seqs, local_rows, width),
        jnp.stack([sums[0], sums[2]]),
        jnp.stack([sums[1], sums[3]]),
        qkv_grad,
        jnp.stack([pair[0] for pair in grad_tall]),
        jnp.stack([sums[4], sums[6]]),
        jnp.stack([sums[5], sums[7]]),
        in_grad,
        jnp.stack([pair[1] for pair in grad_tall]),
        sums[8],
        sums[9],
    )


def solution(mesh):
    both = ("dp", "ctx")
    return jax.shard_map(
        shards,
        mesh=mesh,
        in_specs=(
            P("dp", "ctx", None),
            P(None, both),
            P(None, both),
            P(None, both, None),
            P(None, both, None),
            P(None, both),
            P(None, both),
            P(None, both, None),
            P(None, both, None),
            P(both),
            P(both),
            P(both, None),
            P("dp", "ctx", None),
            P("dp", "ctx", None),
            P("dp", "ctx"),
            P("dp", "ctx", None),
        ),
        out_specs=(
            P("dp", "ctx", None),
            P("dp", "ctx", None),
            P(None, both),
            P(None, both),
            P(None, both, None),
            P(None, both, None),
            P(None, both),
            P(None, both),
            P(None, both, None),
            P(None, both, None),
            P(both),
            P(both),
        ),
        check_vma=False,
    )
```

```python
import functools
import math

import jax
import jax.numpy as jnp
from jax import lax
from jax.experimental import pallas as pl
from jax.experimental.pallas import tpu as pltpu
from jax.sharding import PartitionSpec as P

HEADS = 16
LAYERS = 2

EPSILON = 1e-05
FLOOR = -1e30
RECALL_SHARE = 0.25
DISTANCE_SCALE = 1.5

MESH = pl.DeviceIdType.MESH
VMEM = pltpu.VMEM
BF16 = jnp.bfloat16
F32 = jnp.float32


def norm_parts(values):
    average = jnp.mean(values, axis=-1, keepdims=True)
    centered = values - average
    variance = jnp.mean(centered * centered, axis=-1, keepdims=True)
    inverse = lax.rsqrt(variance + EPSILON)
    return centered * inverse, inverse


def norm_backward(grad, unit, inverse, gains):
    scaled = grad * gains
    return inverse * (
        scaled
        - jnp.mean(scaled, axis=-1, keepdims=True)
        - unit * jnp.mean(scaled * unit, axis=-1, keepdims=True)
    )


def send(source, target, send_sem, recv_sem, where):
    copy = pltpu.make_async_remote_copy(
        src_ref=source,
        dst_ref=target,
        send_sem=send_sem,
        recv_sem=recv_sem,
        device_id=where,
        device_id_type=MESH,
    )
    copy.start()
    return copy


def partner_of(me, plane, ring):
    return ((me // ring) * ring + plane, me % ring), me % ring != plane


def greet_all(targets, partner=None, away=None):
    barrier = pltpu.get_barrier_semaphore()
    for target in targets:
        pl.semaphore_signal(barrier, inc=1, device_id=target, device_id_type=MESH)
    if partner is None:
        pl.semaphore_wait(barrier, len(targets))
        return

    @pl.when(away)
    def _():
        pl.semaphore_signal(barrier, inc=1, device_id=partner, device_id_type=MESH)

    pl.semaphore_wait(barrier, len(targets) + away.astype(jnp.int32))


def swap_begin(source, target, send_sem, recv_sem, partner, away):
    copy = pltpu.make_async_remote_copy(
        src_ref=source,
        dst_ref=target,
        send_sem=send_sem,
        recv_sem=recv_sem,
        device_id=partner,
        device_id_type=MESH,
    )
    stay = pltpu.make_async_copy(source, target, recv_sem)

    @pl.when(away)
    def _():
        copy.start()

    @pl.when(jnp.logical_not(away))
    def _():
        stay.start()

    return copy, stay, away


def swap_end(swap):
    copy, stay, away = swap

    @pl.when(away)
    def _():
        copy.wait()

    @pl.when(jnp.logical_not(away))
    def _():
        stay.wait()


def mate_of(count, me, k):
    if count != 8:
        return (me + k) % count
    step = (2 * k - 1) % 7 + 1
    core, x, y = (me + step) % 2, (me // 2 + step // 2) % 2, (me // 4 + step // 4) % 2
    return 4 * y + 2 * x + core


def square_of(me):
    core, x, y = me % 2, (me // 2) % 2, me // 4
    return (
        4 * y + 2 * (1 - x) + core,
        4 * (1 - y) + 2 * x + core,
        4 * (1 - y) + 2 * (1 - x) + core,
    )


def gather_sems(count):
    half = count // 2
    dma = pltpu.SemaphoreType.DMA
    if count == 8:
        return [dma((7,)), dma((7,)), dma((6,)), dma((6,))]
    return [dma((half,)), dma((half,)), dma((half - 1,)), dma((half - 1,))]


def gather_begin(count, me, plane, own_ref, full_ref, send_sem, recv_sem):
    half = count // 2
    chip, core = me // 2, me % 2
    sibling = 2 * chip + (1 - core)
    if count == 8:
        beside, beyond, _ = square_of(me)
        cut = own_ref.shape[0] // 2
        sends = {}
        for n, target, begin in ((1, beside, 0), (3, beyond, 1), (2, beside, 1), (4, beyond, 0)):
            at = pl.ds(begin * cut, cut)
            sends[n] = send(
                own_ref.at[at],
                full_ref.at[me, at],
                send_sem.at[n],
                recv_sem.at[n],
                (target, plane),
            )
        sends[0] = send(
            own_ref, full_ref.at[me], send_sem.at[0], recv_sem.at[0], (sibling, plane)
        )
        return sends
    targets = [sibling] + [2 * ((chip + j) % half) + core for j in range(1, half)]
    return {
        j: send(own_ref, full_ref.at[me], send_sem.at[j], recv_sem.at[j], (target, plane))
        for j, target in enumerate(targets)
    }


def hand_on(me, plane, passes, block, pass_send, pass_recv):
    n = len(passes)
    sibling = 2 * (me // 2) + (1 - me % 2)
    passes.append(send(block, block, pass_send.at[n], pass_recv.at[n], (sibling, plane)))


def gather_middle(count, me, plane, full_ref, sends, send_sem, recv_sem, pass_send, pass_recv):
    passes = []
    if count == 8:
        beside, beyond, _ = square_of(me)
        cut = full_ref.shape[1] // 2
        for n, device, begin, target in ((1, beside, 0, beyond), (3, beyond, 1, beside)):
            sends[n].wait_recv()
            block = full_ref.at[device, pl.ds(begin * cut, cut)]
            far = 5 if n == 1 else 6
            sends[far] = send(block, block, send_sem.at[far], recv_sem.at[far], (target, plane))
            hand_on(me, plane, passes, block, pass_send, pass_recv)
    return passes


def gather_end(count, me, plane, full_ref, sends, passes, pass_send, pass_recv):
    half = count // 2
    chip, core = me // 2, me % 2
    if count == 8:
        beside, beyond, across = square_of(me)
        cut = full_ref.shape[1] // 2
        for n, device, begin in ((2, beside, 1), (4, beyond, 0), (5, across, 0), (6, across, 1)):
            sends[n].wait_recv()
            block = full_ref.at[device, pl.ds(begin * cut, cut)]
            hand_on(me, plane, passes, block, pass_send, pass_recv)
    else:
        for j in range(1, half):
            sends[j].wait_recv()
            block = full_ref.at[2 * ((chip + half - j) % half) + core]
            hand_on(me, plane, passes, block, pass_send, pass_recv)
    sends[0].wait_recv()
    for copy in passes:
        copy.wait_recv()
    return list(sends.values()) + passes


def plane_kernel(count, ring, reduce, mode, gather, kinds, *refs):
    refs = list(refs)
    half = count // 2
    partial_ref = refs.pop(0) if reduce else None
    base_ref = refs.pop(0) if mode != "none" else None
    gain_ref = refs.pop(0) if mode in ("norm", "back") else None
    shift_ref = refs.pop(0) if mode == "norm" else None
    saved_ref = refs.pop(0) if mode == "back" else None
    ride_refs = [refs.pop(0) for _ in kinds]
    full_ref = refs.pop(0) if gather else None
    new_ref = refs.pop(0) if reduce else None
    stat_ref = refs.pop(0) if mode == "back" else None
    ride_outs = [refs.pop(0) for _ in kinds]
    square, paired = count == 8, ring == 4
    if reduce:
        mine_ref, side_ref, out_ref, in_ref = (refs.pop(0) for _ in range(4))
        mine_sem, side_send, side_recv, far_send, far_recv = (refs.pop(0) for _ in range(5))
    if gather:
        own_ref, own_sem = refs.pop(0), refs.pop(0)
        gather_send, gather_recv, pass_send, pass_recv = (refs.pop(0) for _ in range(4))
    land_refs = [refs.pop(0) if kind in ("sum0", "sum1") else None for kind in kinds]
    if kinds:
        ride_send, ride_recv, ride_own = refs.pop(0), refs.pop(0), refs.pop(0)

    me = lax.axis_index("dp")
    plane = lax.axis_index("ctx")
    chip, core = me // 2, me % 2
    sibling = 2 * chip + (1 - core)
    if square:
        peers = list(square_of(me))
    else:
        peers = [2 * ((chip + j) % half) + core for j in range(1, half)]

    greet = []
    if "mix" in kinds:
        greet += [((me + k) % count, plane) for k in range(1, count)]
    elif reduce or gather:
        greet += [(sibling, plane)] + [(peer, plane) for peer in peers]
    mate, twin = 2 * (plane // 2) + (1 - plane % 2), (plane + 2) % ring
    if any(kind in ("get0", "get1", "hop") for kind in kinds) or (kinds and not paired):
        greet += [(me, (plane + j) % ring) for j in range(1, ring)]
    elif "sum0" in kinds or "sum1" in kinds:
        greet += [(me, mate), (me, twin)]
    partner, away = partner_of(me, plane, ring)
    if "swap" in kinds:
        greet_all(greet, partner, away)
    else:
        greet_all(greet)
    pending = []
    rides, stays, swaps, mixes = [], [], [], []

    def to_mate(i, n, t):
        return send(
            ride_refs[i].at[t] if kinds[i] == "sum0" else ride_refs[i].at[:, t],
            land_refs[i].at[n],
            ride_send.at[i, n],
            ride_recv.at[i, n],
            (me, mate),
        )

    for i, kind in enumerate(kinds):
        if kind == "swap":
            swaps.append(
                swap_begin(
                    ride_refs[i],
                    ride_outs[i],
                    ride_send.at[i, 0],
                    ride_recv.at[i, 0],
                    partner,
                    away,
                )
            )
        if kind in ("sum0", "sum1") and paired:
            rides.append(to_mate(i, 0, 2 * (1 - plane // 2) + (1 - plane % 2)))
            continue
        for j in range(1, ring) if kind not in ("mix", "swap") else ():
            there = (plane + j) % ring
            if kind == "sum0":
                source, target = ride_refs[i].at[there], land_refs[i].at[j - 1]
            elif kind == "sum1":
                source, target = ride_refs[i].at[:, there], land_refs[i].at[j - 1]
            elif kind == "get0":
                source, target = ride_refs[i], ride_outs[i].at[plane]
            elif kind == "hop":
                source, target = ride_refs[i].at[there], ride_outs[i].at[plane]
            else:
                source, target = ride_refs[i], ride_outs[i].at[:, plane]
            rides.append(
                send(source, target, ride_send.at[i, j - 1], ride_recv.at[i, j - 1], (me, there))
            )
        if kind not in ("sum0", "sum1", "swap"):
            if kind == "mix":
                source, target = ride_refs[i].at[me], ride_outs[i].at[me]
            elif kind == "hop":
                source, target = ride_refs[i].at[plane], ride_outs[i].at[plane]
            elif kind == "get0":
                source, target = ride_refs[i], ride_outs[i].at[plane]
            else:
                source, target = ride_refs[i], ride_outs[i].at[:, plane]
            stay = pltpu.make_async_copy(source, target, ride_own.at[i])
            stay.start()
            stays.append(stay)
    pending += rides

    def chunks_of(i):
        steps = ride_outs[i].shape[0]
        chunk = 1 if kinds[i] == "sum1" else min(steps, 32)
        return steps // chunk, chunk

    def own_part(i, at, t):
        return (ride_refs[i][t, at] if kinds[i] == "sum0" else ride_refs[i][at, t]).astype(F32)

    pairs = [i for i, kind in enumerate(kinds) if kind in ("sum0", "sum1") and paired]

    def add_pairs(most):
        for i in pairs[len(crossing) : len(crossing) + most]:
            rides[i].wait_recv()
            steps, chunk = chunks_of(i)

            def add(step, carry, i=i, chunk=chunk):
                at = pl.ds(pl.multiple_of(step * chunk, chunk), chunk)
                total = own_part(i, at, twin) + land_refs[i][0, at].astype(F32)
                land_refs[i][3, at] = total.astype(BF16)
                return carry

            lax.fori_loop(0, steps, add, 0)
            crossing.append(
                send(
                    land_refs[i].at[3],
                    land_refs[i].at[2],
                    ride_send.at[i, 2],
                    ride_recv.at[i, 2],
                    (me, twin),
                )
            )
        if len(crossing) == len(pairs) and not staying:
            staying.extend(to_mate(i, 1, mate) for i in pairs)

    def begin_mixes():
        for i, kind in enumerate(kinds):
            for k in range(1, count) if kind == "mix" else ():
                there = mate_of(count, me, k)
                mixes.append(
                    send(
                        ride_refs[i].at[there],
                        ride_outs[i].at[me],
                        ride_send.at[i, k - 1],
                        ride_recv.at[i, k - 1],
                        (there, plane),
                    )
                )

    staying = []
    crossing = []
    if reduce:
        if square:
            beside, beyond, across = peers
            order = [across // 2, beside // 2, beyond // 2, chip]
        else:
            order = [(chip + j + 1) % half for j in range(half)]
        side, mine = [], []
        for j, where in enumerate(order):
            side.append(
                send(
                    partial_ref.at[2 * where + (1 - core)],
                    side_ref.at[j],
                    side_send.at[j],
                    side_recv.at[j],
                    (sibling, plane),
                )
            )
            mine.append(
                pltpu.make_async_copy(
                    partial_ref.at[2 * where + core], mine_ref.at[j], mine_sem.at[j]
                )
            )
            mine[-1].start()

        def pair_sum(j):
            mine[j].wait()
            side[j].wait_recv()
            return mine_ref[j].astype(F32) + side_ref[j].astype(F32)

        far = []
        if square:
            cut = out_ref.shape[1] // 2
            upper, lower = pl.ds(0, cut), pl.ds(cut, cut)

            def give(source, slot, target):
                far.append(
                    send(
                        source,
                        in_ref.at[slot],
                        far_send.at[slot],
                        far_recv.at[slot],
                        (target, plane),
                    )
                )

            out_ref[0] = pair_sum(0).astype(BF16)
            give(out_ref.at[0, upper], 0, beside)
            give(out_ref.at[0, lower], 3, beyond)
            out_ref[1] = pair_sum(1).astype(BF16)
            give(out_ref.at[1, upper], 1, beside)
            out_ref[2] = pair_sum(2).astype(BF16)
            give(out_ref.at[2, lower], 4, beyond)
            total = pair_sum(3)
            add_pairs(1)
            far[0].wait_recv()
            out_ref[3, upper] = (out_ref[2, upper].astype(F32) + in_ref[0].astype(F32)).astype(BF16)
            give(out_ref.at[3, upper], 5, beyond)
            far[1].wait_recv()
            out_ref[3, lower] = (out_ref[1, lower].astype(F32) + in_ref[3].astype(F32)).astype(BF16)
            give(out_ref.at[3, lower], 2, beside)
            begin_mixes()
            add_pairs(1)
            far[2].wait_recv()
            far[3].wait_recv()
            far[4].wait_recv()
            far[5].wait_recv()
            total = total + jnp.concatenate(
                [
                    in_ref[1].astype(F32) + in_ref[5].astype(F32),
                    in_ref[4].astype(F32) + in_ref[2].astype(F32),
                ],
                axis=0,
            )
        else:
            for j in range(1, half):
                out_ref[j - 1] = pair_sum(j - 1).astype(BF16)
                far.append(
                    send(
                        out_ref.at[j - 1],
                        in_ref.at[j - 1],
                        far_send.at[j - 1],
                        far_recv.at[j - 1],
                        (peers[j - 1], plane),
                    )
                )
            total = pair_sum(half - 1)
            for j in range(1, half):
                far[j - 1].wait_recv()
                total = total + in_ref[j - 1].astype(F32)
        pending += side + far
    if mode == "norm":
        value = base_ref[...] + total
        new_ref[...] = value
        unit, _ = norm_parts(value)
        result = unit * gain_ref[...] + shift_ref[...]
    elif mode == "back":
        unit, inverse = norm_parts(saved_ref[...].astype(F32))
        stat_ref[0:1, :] = jnp.sum(total * unit, axis=0, keepdims=True)
        stat_ref[1:2, :] = jnp.sum(total, axis=0, keepdims=True)
        result = base_ref[...] + norm_backward(total, unit, inverse, gain_ref[...])
        new_ref[...] = result
    elif mode == "plain":
        result = base_ref[...]
        if reduce:
            result = result + total
            new_ref[...] = result

    if gather:
        own_ref[...] = result.astype(BF16)
        sends = gather_begin(count, me, plane, own_ref, full_ref, gather_send, gather_recv)
        stay = pltpu.make_async_copy(own_ref, full_ref.at[me], own_sem)
        stay.start()
        stays.append(stay)
    if not (reduce and square):
        begin_mixes()
    add_pairs(len(pairs))
    if gather:
        passes = gather_middle(
            count, me, plane, full_ref, sends, gather_send, gather_recv, pass_send, pass_recv
        )
        pending += gather_end(count, me, plane, full_ref, sends, passes, pass_send, pass_recv)
    n = len(pairs)
    for copy in rides[n:] + mixes + staying + crossing:
        copy.wait_recv()
    pending += mixes + staying + crossing
    for copy in stays:
        copy.wait()
    for swap in swaps:
        swap_end(swap)
    for i, kind in enumerate(kinds):
        if kind not in ("sum0", "sum1"):
            continue
        steps, chunk = chunks_of(i)

        def add(step, carry, i=i, chunk=chunk):
            at = pl.ds(pl.multiple_of(step * chunk, chunk), chunk)
            total = own_part(i, at, plane)
            for j in (1, 2) if paired else range(ring - 1):
                total = total + land_refs[i][j, at].astype(F32)
            ride_outs[i][at] = total.astype(ride_outs[i].dtype)
            return carry

        lax.fori_loop(0, steps, add, 0)
    for copy in pending:
        copy.wait_send()


def plane_exchange(
    count,
    ring,
    call_id,
    partial=None,
    base=None,
    gains=None,
    shifts=None,
    saved=None,
    gather=True,
    sums=(),
    gets=(),
    mixes=(),
    hops=(),
    swaps=(),
):
    reduce = partial is not None
    mode = "none" if base is None else "plain"
    if gains is not None:
        mode = "norm" if saved is None else "back"
    half = count // 2
    operands = [partial] if reduce else []
    if base is not None:
        operands.append(base)
        rows, width = base.shape
    if gains is not None:
        operands.append(gains.reshape(1, width))
    if mode == "norm":
        operands.append(shifts.reshape(1, width))
    if mode == "back":
        operands.append(saved)
    operands += sums
    specs = [pl.BlockSpec(memory_space=VMEM)] * len(operands)
    if reduce:
        specs[0] = pl.BlockSpec(memory_space=pltpu.HBM)
    operands += list(gets) + list(mixes) + list(hops) + list(swaps)
    specs += [pl.BlockSpec(memory_space=pltpu.HBM)] * (len(operands) - len(specs))
    kinds = tuple("sum" + str(x.ndim - 3) for x in sums)
    kinds += tuple("get" + str(x.ndim - 2) for x in gets)
    kinds += ("mix",) * len(mixes) + ("hop",) * len(hops) + ("swap",) * len(swaps)
    outs, scratch = [], []
    if gather:
        outs.append(jax.ShapeDtypeStruct((count, rows, width), BF16))
    if reduce:
        outs.append(jax.ShapeDtypeStruct((rows, width), F32))
    if mode == "back":
        outs.append(jax.ShapeDtypeStruct((8, width), F32))
    lands = [x.shape[1:] if x.ndim == 3 else x.shape[:1] + x.shape[2:] for x in sums]
    outs += [
        jax.ShapeDtypeStruct(land, F32 if x.ndim == 3 else BF16) for land, x in zip(lands, sums)
    ]
    out_specs = [pl.BlockSpec(memory_space=VMEM)] * len(outs)
    if gather:
        out_specs[0] = pl.BlockSpec(memory_space=pltpu.HBM)
    outs += [
        jax.ShapeDtypeStruct((ring,) + x.shape if x.ndim == 2 else (count, ring) + x.shape[1:], BF16)
        for x in gets
    ]
    outs += [jax.ShapeDtypeStruct(x.shape, x.dtype) for x in list(mixes) + list(hops) + list(swaps)]
    out_specs += [pl.BlockSpec(memory_space=pltpu.HBM)] * (len(outs) - len(out_specs))
    dma = pltpu.SemaphoreType.DMA
    if reduce:
        taken = (6, rows // 2, width) if count == 8 else (half - 1, rows, width)
        scratch += [
            VMEM((half, rows, width), BF16),
            VMEM((half, rows, width), BF16),
            VMEM((half, rows, width), BF16),
            VMEM(taken, BF16),
            dma((half,)),
            dma((half,)),
            dma((half,)),
            dma(taken[:1]),
            dma(taken[:1]),
        ]
    if gather:
        scratch += [VMEM((rows, width), BF16), dma] + gather_sems(count)
    scratch += [VMEM((4 if ring == 4 else ring - 1,) + land, BF16) for land in lands]
    if kinds:
        most = max(ring, count if mixes else 0) - 1
        scratch += [dma((len(kinds), most)), dma((len(kinds), most)), dma((len(kinds),))]
    return pl.pallas_call(
        functools.partial(plane_kernel, count, ring, reduce, mode, gather, kinds),
        out_shape=tuple(outs),
        in_specs=specs,
        out_specs=tuple(out_specs),
        scratch_shapes=scratch,
        compiler_params=pltpu.CompilerParams(
            collective_id=call_id, has_side_effects=True, vmem_limit_bytes=16 * 1024 * 1024
        ),
        cost_estimate=pl.CostEstimate(
            flops=0, bytes_accessed=(60 if reduce else 30) << 20, transcendentals=0
        ),
    )(*operands)


def relay(source, target, sems, where, begin):
    copy = pltpu.make_async_remote_copy(
        src_ref=source,
        dst_ref=target,
        send_sem=sems[0],
        recv_sem=sems[1],
        device_id=where,
        device_id_type=MESH,
    )
    if begin:
        copy.start()
    return copy


def relay_begin(ring, me, plane, own, place, send_sem, recv_sem):
    for side, shift in ((0, 1), (1, -1)):
        there = (me, (plane + ring + shift) % ring)
        sems = (send_sem.at[side, 0], recv_sem.at[side, 0])

        @pl.when(plane < ring - 1 if side == 0 else plane > 0)
        def _(there=there, sems=sems):
            relay(own, place(plane), sems, there, True)


def relay_step(ring, me, plane, step, place, send_sem, recv_sem):
    for side, shift in ((0, 1), (1, -1)):
        there = (me, (plane + ring + shift) % ring)
        origin = (plane + ring - shift * step) % ring
        came = plane >= step if side == 0 else plane < ring - step
        more = plane < ring - 1 if side == 0 else plane > 0

        @pl.when(came)
        def _(side=side, there=there, origin=origin):
            block = place(origin)
            sems = (send_sem.at[side, step - 1], recv_sem.at[side, step - 1])
            relay(block, block, sems, there, False).wait_recv()

        if step < ring - 1:

            @pl.when(jnp.logical_and(came, more))
            def _(side=side, there=there, origin=origin):
                block = place(origin)
                sems = (send_sem.at[side, step], recv_sem.at[side, step])
                relay(block, block, sems, there, True)


def relay_end(ring, me, plane, place, send_sem, recv_sem):
    for step in range(ring - 1):
        for side, shift in ((0, 1), (1, -1)):
            there = (me, (plane + ring + shift) % ring)
            came = plane >= step if side == 0 else plane < ring - step
            more = plane < ring - 1 if side == 0 else plane > 0

            @pl.when(jnp.logical_and(came, more))
            def _(side=side, there=there):
                block = place(plane)
                sems = (send_sem.at[side, step], recv_sem.at[side, step])
                relay(block, block, sems, there, False).wait_send()


def first_kernel(count, ring, layers, talls, picks, *refs):
    refs = list(refs)
    token_ref, asked_ref, note_ref, crowded_ref = (refs.pop(0) for _ in range(4))
    vector_refs = [refs.pop(0) for _ in range(6)]
    store_ref = refs.pop(0)
    column_refs = [refs.pop(0) for _ in range(2)]
    tall_refs = [refs.pop(0) for _ in range(talls)]
    full_ref, vector_ref, rows_ref, mine_ref, notes_ref, guest_ref = (refs.pop(0) for _ in range(6))
    wide_refs = [[refs.pop(0) for _ in range(layers)] for _ in range(2)]
    whole_refs = [refs.pop(0) for _ in picks]
    small_all, small_ref, wanted_ref = refs.pop(0), refs.pop(0), refs.pop(0)
    asked_in, asked_all, asked_rows = (refs.pop(0) for _ in range(3))
    column_all = [refs.pop(0) for _ in range(2)]
    own_sem, own_ref = refs.pop(0), refs.pop(0)
    held_ref, total_ref, served_ref, held_sem = (refs.pop(0) for _ in range(4))
    (
        gather_send,
        gather_recv,
        pass_send,
        pass_recv,
        small_send,
        small_recv,
        across_send,
        across_recv,
        column_send,
        column_recv,
        relay_send,
        relay_recv,
        flag_send,
        flag_recv,
        rows_send,
        rows_recv,
        swap_send,
        swap_recv,
        guest_send,
        guest_recv,
        mix_send,
        mix_recv,
        hop_send,
        hop_recv,
    ) = refs
    me = lax.axis_index("dp")
    plane = lax.axis_index("ctx")
    hold = pltpu.make_async_copy(store_ref, held_ref, held_sem)
    hold.start()
    mates = [mate_of(count, me, k) for k in range(1, count)]
    planes = [(plane + j) % ring for j in range(1, ring)]
    part = vector_refs[0].shape[1]
    spot = lax.broadcasted_iota(jnp.int32, (part, 128), 1)
    tile = (spot % part == lax.broadcasted_iota(jnp.int32, (part, 128), 0)).astype(F32).astype(BF16)
    lane = lax.broadcasted_iota(jnp.int32, (1, 128), 1)
    here = lane // part == (me * ring + plane) % (128 // part)
    at = 0
    for ref in vector_refs:
        size = ref.shape[0]
        small_ref[at : at + size, :] = jnp.where(here, dot(ref[...], tile), 0.0)
        at += size
    small_ref[at : at + 1, :] = jnp.broadcast_to(crowded_ref[...], (1, 128))
    small_ref[at + 1 :, :] = jnp.zeros((16 - at - 1, 128), F32)
    partner, away = partner_of(me, plane, ring)
    greet_all([(mate, plane) for mate in mates] + [(me, there) for there in planes], partner, away)
    asks = [
        send(asked_ref.at[mate], asked_in.at[me], mix_send.at[k], mix_recv.at[k], (mate, plane))
        for k, mate in enumerate(mates)
    ]
    swap = swap_begin(note_ref, mine_ref, swap_send, swap_recv, partner, away)
    guest = swap_begin(token_ref, guest_ref, guest_send, guest_recv, partner, away)
    asked_in[me] = asked_ref[me]

    stays = []

    def stay(source, target):
        copy = pltpu.make_async_copy(source, target, own_sem.at[len(stays)])
        copy.start()
        stays.append(copy)

    small_all[me, plane] = small_ref[...]
    smalls = [
        send(small_ref, small_all.at[me, plane], small_send.at[k], small_recv.at[k], (mate, plane))
        for k, mate in enumerate(mates)
    ]
    columns = []
    for i in range(2):
        pieces = 3 if i == 0 and len(column_refs[0].shape) == 3 else 1
        lanes = column_all[i].shape[-1] // pieces
        for n in range(pieces):

            def block(device, i=i, n=n, lanes=lanes, pieces=pieces):
                if len(column_refs[i].shape) == 4:
                    return column_refs[i].at[device]
                at = pl.multiple_of((n * count + device) * lanes, 128)
                return column_refs[i].at[:, :, pl.ds(at, lanes)]

            target = column_all[i].at[me]
            if pieces > 1:
                target = column_all[i].at[me, :, :, n * lanes : (n + 1) * lanes]
            stay(block(me), target)
            for k, mate in enumerate(mates):
                columns.append(
                    send(
                        block(mate),
                        target,
                        column_send.at[3 * i + n, k],
                        column_recv.at[3 * i + n, k],
                        (mate, plane),
                    )
                )
    column_stays = stays[:]
    for copy in asks:
        copy.wait_recv()
    hops = [
        send(
            asked_in.at[:, there],
            asked_all.at[plane],
            hop_send.at[j],
            hop_recv.at[j],
            (me, there),
        )
        for j, there in enumerate(planes)
    ]
    pending = smalls + columns + asks + hops
    for n in range(count):
        asked_all[plane, n] = asked_in[n, plane]
    late = []
    for copy in smalls:
        copy.wait_recv()
    across = [
        send(
            small_all.at[:, plane],
            small_all.at[:, plane],
            across_send.at[j],
            across_recv.at[j],
            (me, there),
        )
        for j, there in enumerate(planes)
    ]

    relays = []

    def spread(own, place):
        n = len(relays)
        relays.append((place, relay_send.at[n], relay_recv.at[n]))
        stay(own, place(plane))
        relay_begin(ring, me, plane, own, *relays[-1])

    def spread_tall(i):
        array, layer = picks[i]
        spread(tall_refs[array].at[layer], lambda p: whole_refs[i].at[p])

    for i in range(2):
        spread_tall(i)
    swap_end(swap)
    for j, there in enumerate(planes):
        late.append(
            send(
                mine_ref.at[there],
                notes_ref.at[plane],
                flag_send.at[j],
                flag_recv.at[j],
                (me, there),
            )
        )
    notes_ref[plane] = mine_ref[plane]
    hold.wait()
    size = served_ref.shape[1]
    entries = size // ring
    for copy in hops:
        copy.wait_recv()
    for p in range(ring):
        for n in range(count):
            asked_rows[p * count + n : p * count + n + 1, :] = asked_all[p, n, 0:1, :].astype(F32)
    wanted_ref[...] = jnp.transpose(asked_rows[...])[:entries, :]
    depth = min(1024, held_ref.shape[0])

    def rows_copy(k):
        mate = mate_of(count, me, k)
        return pltpu.make_async_remote_copy(
            src_ref=served_ref.at[mate],
            dst_ref=rows_ref.at[me],
            send_sem=rows_send.at[k - 1],
            recv_sem=rows_recv.at[k - 1],
            device_id=(mate, plane),
            device_id_type=MESH,
        )

    def pick(mate):
        first = (mate % ring) * count + (mate // ring) * ring
        spots = lax.broadcasted_iota(jnp.int32, wanted_ref.shape, 1)
        columns_of = [
            jnp.sum(jnp.where(spots == first + n, wanted_ref[...], 0.0), axis=1, keepdims=True)
            for n in range(ring)
        ]
        wanted = jnp.concatenate(columns_of, axis=0).astype(jnp.int32)
        total_ref[...] = jnp.zeros_like(total_ref)

        def look(n, carry):
            at = pl.ds(pl.multiple_of(n * depth, depth), depth)
            marks = wanted == n * depth + lax.broadcasted_iota(jnp.int32, (size, depth), 1)
            total_ref[...] += dot(marks.astype(F32).astype(BF16), held_ref[at, :])
            return carry

        lax.fori_loop(0, held_ref.shape[0] // depth, look, 0)
        served_ref[mate] = total_ref[...].astype(BF16)

    def serve(k, carry):
        pick(mate_of(count, me, k))
        rows_copy(k).start()
        return carry

    serve(1, 0)
    for copy in columns:
        copy.wait_recv()
    for copy in column_stays:
        copy.wait()
    for layer in range(layers):
        for i in range(2):
            spread(
                column_all[i].at[:, layer],
                lambda p, layer=layer, i=i: wide_refs[i][layer].at[:, p],
            )
    for i in range(2, len(picks)):
        spread_tall(i)
    for copy in across:
        copy.wait_recv()
    groups = vector_ref.shape[1] // 128
    members = count * ring // groups
    for group in range(groups):
        total = small_all[group * members // ring, group * members % ring]
        for n in range(group * members + 1, (group + 1) * members):
            total = total + small_all[n // ring, n % ring]
        vector_ref[:, group * 128 : (group + 1) * 128] = total
    swap_end(guest)
    unit, _ = norm_parts(guest_ref[...].astype(F32))
    shift = vector_refs[0].shape[0]
    own_ref[...] = (unit * vector_ref[0:1, :] + vector_ref[shift : shift + 1, :]).astype(BF16)
    stay(own_ref, full_ref.at[me])
    sends = gather_begin(count, me, plane, own_ref, full_ref, gather_send, gather_recv)
    serve(2, 0)
    passes = gather_middle(
        count, me, plane, full_ref, sends, gather_send, gather_recv, pass_send, pass_recv
    )
    lax.fori_loop(3, count // 2, serve, 0)
    for one in relays:
        relay_step(ring, me, plane, 1, *one)
    lax.fori_loop(count // 2, count - 1, serve, 0)
    for one in relays:
        relay_step(ring, me, plane, 2, *one)
    serve(count - 1, 0)
    pick(me)
    stay(served_ref.at[me], rows_ref.at[me])
    for step in range(3, ring):
        for one in relays:
            relay_step(ring, me, plane, step, *one)
    pending += gather_end(count, me, plane, full_ref, sends, passes, pass_send, pass_recv)
    for copy in late:
        copy.wait_recv()

    def rows_done(k, carry):
        rows_copy(k).wait()
        return carry

    lax.fori_loop(1, count, rows_done, 0)
    for copy in stays[len(column_stays) :]:
        copy.wait()
    for copy in pending + across + late:
        copy.wait_send()
    for one in relays:
        relay_end(ring, me, plane, *one)


def first_exchange(
    count, ring, call_id, tokens, asked, notes, crowded, vectors, store, joint, expand, talls, picks
):
    rows, width = tokens.shape
    layers, part = talls[0].shape[0], joint.shape[-2]
    size = ring * notes.shape[-1]
    spread = max(128, count * ring)
    columns = []
    for x in (joint, expand):
        columns.append((count, layers, part, x.shape[-1] if x.ndim == 4 else x.shape[-1] // count))
    dma = pltpu.SemaphoreType.DMA
    near, far = pl.BlockSpec(memory_space=VMEM), pl.BlockSpec(memory_space=pltpu.HBM)
    outs = [
        jax.ShapeDtypeStruct((count, rows, width), BF16),
        jax.ShapeDtypeStruct((16, width), F32),
        jax.ShapeDtypeStruct((count, size, width), BF16),
        jax.ShapeDtypeStruct(notes.shape, notes.dtype),
        jax.ShapeDtypeStruct(notes.shape, notes.dtype),
        jax.ShapeDtypeStruct(tokens.shape, BF16),
    ]
    for shape in columns:
        outs += [jax.ShapeDtypeStruct((count, ring) + shape[2:], BF16)] * layers
    outs += [jax.ShapeDtypeStruct((ring,) + talls[i].shape[1:], BF16) for i, _ in picks]

    def pair(*shape):
        return [dma(shape), dma(shape)]

    return pl.pallas_call(
        functools.partial(first_kernel, count, ring, layers, len(talls), picks),
        out_shape=tuple(outs),
        in_specs=[near] * (4 + len(vectors)) + [far] * (3 + len(talls)),
        out_specs=tuple([far, near, far, near, near, near] + [far] * (2 * layers + len(picks))),
        scratch_shapes=[
            VMEM((count, ring, 16, 128), F32),
            VMEM((16, 128), F32),
            VMEM((size // ring, spread), F32),
            VMEM(asked.shape, jnp.int32),
            VMEM((ring, count) + asked.shape[2:], jnp.int32),
            VMEM((spread, 128), F32),
            VMEM(columns[0], BF16),
            VMEM(columns[1], BF16),
            dma((6 + 2 * layers + len(picks),)),
            VMEM((rows, width), BF16),
            VMEM(store.shape, BF16),
            VMEM((size, width), F32),
            VMEM((count, size, width), BF16),
            dma,
        ]
        + gather_sems(count)
        + pair(count - 1)
        + pair(ring - 1)
        + pair(4, count - 1)
        + pair(2 * layers + len(picks), 2, ring - 1)
        + pair(ring - 1)
        + pair(count - 1)
        + [dma, dma, dma, dma]
        + pair(count - 1)
        + pair(ring - 1),
        compiler_params=pltpu.CompilerParams(
            collective_id=call_id, has_side_effects=True, vmem_limit_bytes=61 * 1024 * 1024
        ),
        cost_estimate=pl.CostEstimate(flops=0, bytes_accessed=200 << 20, transcendentals=0),
    )(tokens, asked, notes, crowded, *vectors, store, joint, expand, *talls)


def last_kernel(
    count,
    ring,
    layers,
    sums_ref,
    wide_ref,
    rows_ref,
    *refs,
):
    refs = list(refs)
    joint_refs = [refs.pop(0) for _ in range(layers - 1)]
    expand_refs = [refs.pop(0) for _ in range(layers)]
    total_ref, joint_grad_ref, expand_grad_ref, home_ref = (refs.pop(0) for _ in range(4))
    sums_in, across_ref, mixed_ref, rows_in = (refs.pop(0) for _ in range(4))
    (
        own_sem,
        swap_send,
        swap_recv,
        sums_send,
        sums_recv,
        wide_send,
        wide_recv,
        across_send,
        across_recv,
    ) = refs
    me = lax.axis_index("dp")
    plane = lax.axis_index("ctx")
    partner, away = partner_of(me, plane, ring)
    greet = [((me + k) % count, plane) for k in range(1, count)]
    greet += [(me, (plane + j) % ring) for j in range(1, ring)]
    greet_all(greet, partner, away)

    pending, sums = [], []
    for k in range(1, count):
        there = mate_of(count, me, k)
        sums.append(
            send(
                sums_ref.at[there],
                sums_in.at[me],
                sums_send.at[k - 1],
                sums_recv.at[k - 1],
                (there, plane),
            )
        )
    swap = swap_begin(rows_ref, rows_in, swap_send, swap_recv, partner, away)
    for k in range(1, count):
        there = mate_of(count, me, k)
        pending.append(
            send(
                wide_ref.at[there],
                mixed_ref.at[me],
                wide_send.at[k - 1],
                wide_recv.at[k - 1],
                (there, plane),
            )
        )
    sums_in[me] = sums_ref[me]
    stay = pltpu.make_async_copy(wide_ref.at[me], mixed_ref.at[me], own_sem)
    stay.start()
    for copy in sums:
        copy.wait_recv()
    total = sums_in[0]
    for k in range(1, count):
        total = total + sums_in[k]
    across_ref[plane] = total
    across = [
        send(
            across_ref.at[plane],
            across_ref.at[plane],
            across_send.at[j - 1],
            across_recv.at[j - 1],
            (me, (plane + j) % ring),
        )
        for j in range(1, ring)
    ]
    inner = expand_refs[0].shape[2]
    size = wide_ref.shape[2] // 3
    for layer in range(layers):
        for k in range(count):
            expand_grad_ref[layer, :, k * inner : (k + 1) * inner] = expand_refs[layer][k].astype(F32)

    def spread(layer, ref):
        for k in range(count):
            for i in range(3):
                at = (i * count + k) * size
                joint_grad_ref[layer, :, at : at + size] = ref[
                    k, :, i * size : (i + 1) * size
                ].astype(F32)

    for layer in range(1, layers):
        spread(layer, joint_refs[layer - 1])
    for copy in across:
        copy.wait_recv()
    total = across_ref[0]
    for j in range(1, ring):
        total = total + across_ref[j]
    total_ref[...] = total
    for copy in pending:
        copy.wait_recv()
    stay.wait()
    spread(0, mixed_ref)
    swap_end(swap)
    home_ref[...] = rows_in[...].astype(F32)
    for copy in pending + sums + across:
        copy.wait_send()


def last_exchange(count, ring, call_id, sums, wide, rows, joints, expands):
    dma = pltpu.SemaphoreType.DMA
    layers = len(expands)
    part = wide.shape[1]
    operands = (sums, wide, rows, *joints, *expands)
    outs = (
        jax.ShapeDtypeStruct(sums.shape[1:], F32),
        jax.ShapeDtypeStruct((layers, part, count * wide.shape[2]), F32),
        jax.ShapeDtypeStruct((layers, part, count * expands[0].shape[2]), F32),
        jax.ShapeDtypeStruct(rows.shape, F32),
    )
    spec = pl.BlockSpec(memory_space=VMEM)
    return pl.pallas_call(
        functools.partial(last_kernel, count, ring, layers),
        out_shape=outs,
        in_specs=[spec] * len(operands),
        out_specs=(spec,) * len(outs),
        scratch_shapes=[
            VMEM(sums.shape, F32),
            VMEM((ring,) + sums.shape[1:], F32),
            VMEM(wide.shape, BF16),
            VMEM(rows.shape, BF16),
            dma,
            dma,
            dma,
            dma((count - 1,)),
            dma((count - 1,)),
            dma((count - 1,)),
            dma((count - 1,)),
            dma((ring - 1,)),
            dma((ring - 1,)),
        ],
        compiler_params=pltpu.CompilerParams(
            collective_id=call_id, has_side_effects=True, vmem_limit_bytes=16 * 1024 * 1024
        ),
    )(*operands)


GATE_SCALE = math.sqrt(2.0 / math.pi)
GATE_CUBE = 0.044715


def after(*arrays):
    return lax.optimization_barrier(arrays)


def dot(left, right):
    return jnp.dot(left, right, preferred_element_type=F32)


def contract_rows(left, right):
    return lax.dot_general(left, right, (((0,), (0,)), ((), ())), preferred_element_type=F32)


def contract_cols(left, right):
    return lax.dot_general(left, right, (((1,), (1,)), ((), ())), preferred_element_type=F32)


def local_call(body, outs, operands, grid, in_specs, out_specs, scratch=(), flops=0, grant=32):
    moved = sum(math.prod(x.shape) * x.dtype.itemsize for x in list(operands) + list(outs))
    return pl.pallas_call(
        body,
        out_shape=tuple(outs),
        grid=grid,
        in_specs=in_specs,
        out_specs=tuple(out_specs),
        scratch_shapes=list(scratch),
        compiler_params=pltpu.CompilerParams(vmem_limit_bytes=grant * 1024 * 1024),
        cost_estimate=pl.CostEstimate(flops=flops, bytes_accessed=moved, transcendentals=0),
    )(*operands)


def whole(x):
    return pl.BlockSpec(x.shape, lambda *_, n=len(x.shape): (0,) * n)


def stripe(shape):
    return pl.BlockSpec(shape, lambda i: (i,) + (0,) * (len(shape) - 1))


def probabilities(queries, keys, begin):
    scores = contract_cols(queries, keys) * (queries.shape[-1] ** (-0.5))
    row = begin + lax.broadcasted_iota(jnp.int32, scores.shape, 0)
    allowed = row >= lax.broadcasted_iota(jnp.int32, scores.shape, 1)
    scores = jnp.where(allowed, scores, FLOOR)
    raised = jnp.exp(scores - jnp.max(scores, axis=-1, keepdims=True))
    return raised / jnp.sum(raised, axis=-1, keepdims=True)


def attend_kernel(heads, block, x_ref, joint_ref, project_ref, packed_ref, attended_ref, partial_ref):
    packed_ref[...] = dot(x_ref[...], joint_ref[...]).astype(BF16)
    length, width = attended_ref.shape
    size = width // heads
    for head in range(heads):
        at = head * size
        for begin in range(0, length, block):
            end = begin + block
            probs = probabilities(
                packed_ref[begin:end, at : at + size], packed_ref[:end, width + at : width + at + size], begin
            )
            values = packed_ref[:end, 2 * width + at : 2 * width + at + size]
            attended_ref[begin:end, at : at + size] = dot(probs.astype(BF16), values).astype(BF16)
    partial_ref[...] = dot(attended_ref[...], project_ref[...]).astype(BF16)


def attend(normed, joint, project, seqs, heads):
    rows, width = normed.shape
    length, inner = rows // seqs, project.shape[0]
    outs = [
        jax.ShapeDtypeStruct((rows, 3 * inner), BF16),
        jax.ShapeDtypeStruct((rows, inner), BF16),
        jax.ShapeDtypeStruct((rows, width), BF16),
    ]
    return local_call(
        functools.partial(attend_kernel, heads, min(256, length)),
        outs,
        (normed, joint, project),
        (seqs,),
        [stripe((length, width)), whole(joint), whole(project)],
        [stripe((length, 3 * inner)), stripe((length, inner)), stripe((length, width))],
        flops=8 * rows * width * inner,
    )


def attend_backward_kernel(
    heads,
    block,
    grad_ref,
    x_ref,
    packed_ref,
    attended_ref,
    joint_ref,
    project_ref,
    joint_grad_ref,
    project_grad_ref,
    partial_ref,
    joint_sum,
    project_sum,
    key_sum,
    value_sum,
    low_ref,
):
    step = pl.program_id(0)
    length, width = attended_ref.shape
    size = width // heads
    scale = size ** (-0.5)
    grad = contract_cols(grad_ref[...], project_ref[...]).astype(BF16)
    key_sum[...] = jnp.zeros_like(key_sum)
    value_sum[...] = jnp.zeros_like(value_sum)
    for head in range(heads):
        at = head * size
        for begin in range(0, length, block):
            end = begin + block
            queries = packed_ref[begin:end, at : at + size]
            keys = packed_ref[:end, width + at : width + at + size]
            values = packed_ref[:end, 2 * width + at : 2 * width + at + size]
            here = grad[begin:end, at : at + size]
            probs = probabilities(queries, keys, begin)
            grad_probs = contract_cols(here, values)
            delta = jnp.sum(probs * grad_probs, axis=-1, keepdims=True)
            grad_scores = (probs * (grad_probs - delta)).astype(BF16)
            low_ref[begin:end, at : at + size] = (dot(grad_scores, keys) * scale).astype(BF16)
            key_sum[:end, at : at + size] += contract_rows(grad_scores, queries) * scale
            value_sum[:end, at : at + size] += contract_rows(probs.astype(BF16), here)
    low_ref[:, width : 2 * width] = key_sum[...].astype(BF16)
    low_ref[:, 2 * width :] = value_sum[...].astype(BF16)
    partial_ref[...] = contract_cols(low_ref[...], joint_ref[...]).astype(BF16)
    joint_part = contract_rows(x_ref[...], low_ref[...])
    project_part = contract_rows(attended_ref[...], grad_ref[...])

    @pl.when(step == 0)
    def _():
        joint_sum[...] = joint_part
        project_sum[...] = project_part

    @pl.when(step > 0)
    def _():
        joint_sum[...] += joint_part
        project_sum[...] += project_part

    @pl.when(step == pl.num_programs(0) - 1)
    def _():
        joint_grad_ref[...] = joint_sum[...].astype(BF16)
        project_grad_ref[...] = project_sum[...].astype(BF16)


def attend_backward(grad_out, normed, packed, attended, joint, project, seqs, heads):
    rows, width = normed.shape
    length, inner = rows // seqs, project.shape[0]
    outs = [
        jax.ShapeDtypeStruct(joint.shape, BF16),
        jax.ShapeDtypeStruct(project.shape, BF16),
        jax.ShapeDtypeStruct((rows, width), BF16),
    ]
    return local_call(
        functools.partial(attend_backward_kernel, heads, min(256, length)),
        outs,
        (grad_out, normed, packed, attended, joint, project),
        (seqs,),
        [
            stripe((length, width)),
            stripe((length, width)),
            stripe((length, 3 * inner)),
            stripe((length, inner)),
            whole(joint),
            whole(project),
        ],
        [whole(outs[0]), whole(outs[1]), stripe((length, width))],
        [
            VMEM(joint.shape, F32),
            VMEM(project.shape, F32),
            VMEM((length, inner), F32),
            VMEM((length, inner), F32),
            VMEM((length, 3 * inner), BF16),
        ],
        flops=16 * rows * width * inner,
    )


def forward_kernel(x_ref, expand_ref, shrink_ref, inner_ref, partial_ref):
    inner = dot(x_ref[...], expand_ref[...])
    inner_ref[...] = inner
    turn = jnp.tanh(GATE_SCALE * (inner + GATE_CUBE * (inner * inner * inner)))
    active = (0.5 * inner * (1.0 + turn)).astype(BF16)
    partial_ref[...] = dot(active, shrink_ref[...]).astype(BF16)


def forward(normed, expand, shrink):
    rows, width = normed.shape
    inner, block = expand.shape[1], 256
    outs = [jax.ShapeDtypeStruct((rows, inner), F32), jax.ShapeDtypeStruct((rows, width), BF16)]
    return local_call(
        forward_kernel,
        outs,
        (normed, expand, shrink),
        (rows // block,),
        [stripe((block, width)), whole(expand), whole(shrink)],
        [stripe((block, inner)), stripe((block, width))],
        flops=4 * rows * width * inner,
    )


def backward_kernel(
    branch_ref,
    x_ref,
    inner_ref,
    expand_ref,
    shrink_ref,
    expand_grad_ref,
    shrink_grad_ref,
    partial_ref,
    expand_sum,
    shrink_sum,
):
    step = pl.program_id(0)
    branch, inner = branch_ref[...], inner_ref[...]
    square = inner * inner
    turn = jnp.tanh(GATE_SCALE * (inner + GATE_CUBE * (square * inner)))
    active = (0.5 * inner * (1.0 + turn)).astype(BF16)
    slope = GATE_SCALE * (1.0 + (3.0 * GATE_CUBE) * square)
    slope = 0.5 * (1.0 + turn) + 0.5 * inner * (1.0 - turn * turn) * slope
    grad_inner = (contract_cols(branch, shrink_ref[...]) * slope).astype(BF16)
    partial_ref[...] = contract_cols(grad_inner, expand_ref[...]).astype(BF16)
    expand_part = contract_rows(x_ref[...], grad_inner)
    shrink_part = contract_rows(active, branch)

    @pl.when(step == 0)
    def _():
        expand_sum[...] = expand_part
        shrink_sum[...] = shrink_part

    @pl.when(step > 0)
    def _():
        expand_sum[...] += expand_part
        shrink_sum[...] += shrink_part

    @pl.when(step == pl.num_programs(0) - 1)
    def _():
        expand_grad_ref[...] = expand_sum[...].astype(BF16)
        shrink_grad_ref[...] = shrink_sum[...].astype(BF16)


def backward(branch, normed, inner, expand, shrink):
    rows, width = normed.shape
    block = 256
    outs = [
        jax.ShapeDtypeStruct(expand.shape, BF16),
        jax.ShapeDtypeStruct(shrink.shape, BF16),
        jax.ShapeDtypeStruct((rows, width), BF16),
    ]
    return local_call(
        backward_kernel,
        outs,
        (branch, normed, inner, expand, shrink),
        (rows // block,),
        [
            stripe((block, width)),
            stripe((block, width)),
            stripe((block, inner.shape[1])),
            whole(expand),
            whole(shrink),
        ],
        [whole(outs[0]), whole(outs[1]), stripe((block, width))],
        [VMEM(expand.shape, F32), VMEM(shrink.shape, F32)],
        flops=8 * rows * width * inner.shape[1],
    )


def ranks_of(flags):
    planes, groups, rows = flags.shape
    upto = jnp.arange(rows)[:, None] <= jnp.arange(rows)[None, :]
    inside = dot(flags.astype(BF16), upto.astype(BF16))
    before = jnp.where(
        jnp.arange(groups)[None, :, None] < jnp.arange(groups)[None, None, :],
        inside[:, :, -1:],
        0.0,
    )
    rank = inside + jnp.sum(before, axis=1)[:, :, None]
    return rank.reshape(planes, groups * rows), rank[:, -1, -1]


def pack_kernel(note_ref, rows_ref, out_ref, rank_ref):
    _, groups, size = note_ref.shape
    room, width = out_ref.shape[1:]
    marks = (note_ref[0] >= 0).astype(F32)
    upto = lax.broadcasted_iota(jnp.int32, (size, size), 0) <= lax.broadcasted_iota(
        jnp.int32, (size, size), 1
    )
    inside = dot(marks.astype(BF16), upto.astype(F32).astype(BF16))
    before = jnp.zeros((1, 1), F32)
    for n in range(groups):
        mine = inside[n : n + 1, :]
        rank_ref[0:1, n * size : (n + 1) * size] = jnp.where(
            marks[n : n + 1, :] > 0, mine + before, 0.0
        )
        before = before + mine[:, size - 1 : size]
    place = lax.broadcasted_iota(jnp.int32, (room, groups * size), 0) + 1
    chosen = (rank_ref[0:1, :].astype(jnp.int32) == place).astype(F32).astype(BF16)
    out_ref[0] = dot(chosen, rows_ref[...].reshape(groups * size, width)).astype(BF16)


def pack(notes, rows, room):
    planes, groups, size = notes.shape
    width = rows.shape[-1]
    outs = [jax.ShapeDtypeStruct((planes, room, width), BF16)]
    (packed,) = local_call(
        pack_kernel,
        outs,
        (notes, rows),
        (planes,),
        [
            stripe((1, groups, size)),
            pl.BlockSpec((groups, None, size, width), lambda i: (0, i, 0, 0)),
        ],
        [stripe((1, room, width))],
        [VMEM((8, groups * size), F32)],
        flops=2 * planes * room * groups * size * width,
        grant=61,
    )
    return packed


def pieces_of(values, terms):
    pieces = []
    for _ in range(terms):
        pieces.append(values.astype(BF16))
        values = values - pieces[-1].astype(F32)
    return jnp.concatenate(pieces, axis=0)


def recall_kernel(
    tile,
    hidden_ref,
    vector_ref,
    cotangent_ref,
    token_ref,
    stored_ref,
    mixed_ref,
    grad_ref,
    sums_ref,
    scaled_ref,
    pull_ref,
):
    rows, width = hidden_ref.shape
    tiles = stored_ref.shape[0] // tile
    unit, inverse = norm_parts(hidden_ref[...])
    gains = vector_ref[8:9, :]
    query = unit * gains + vector_ref[9:10, :]
    scale = DISTANCE_SCALE * math.sqrt(width)
    terms = jnp.concatenate([pieces_of(query, 3), cotangent_ref[...]], axis=0)
    ones = jnp.ones((8, width), BF16)

    def look(n, carry):
        at = pl.ds(pl.multiple_of(n * tile, tile), tile)
        stored = stored_ref[at, :]
        near = contract_cols(terms, stored)
        squares = jnp.square(stored.astype(F32))
        high = squares.astype(BF16)
        low = (squares - high.astype(F32)).astype(BF16)
        lengths = (contract_cols(ones, high) + contract_cols(ones, low))[0:1, :]
        scaled_ref[:, at] = (
            2.0 * (near[:rows] + (near[rows : 2 * rows] + near[2 * rows : 3 * rows])) - lengths
        ) / scale
        pull_ref[:, at] = RECALL_SHARE * near[3 * rows :]
        return carry

    lax.fori_loop(0, tiles, look, 0)
    usable = token_ref[...] == lax.broadcasted_iota(jnp.int32, scaled_ref.shape, 0)
    scaled = jnp.where(usable, scaled_ref[...], FLOOR)
    raised = jnp.where(usable, jnp.exp(scaled - jnp.max(scaled, axis=1, keepdims=True)), 0.0)
    weights = raised / jnp.sum(raised, axis=1, keepdims=True)
    pull = pull_ref[...]
    grad_scaled = weights * (pull - jnp.sum(weights * pull, axis=1, keepdims=True))
    scaled_ref[...] = weights
    pull_ref[...] = grad_scaled
    rest = jnp.sum(grad_scaled, axis=1, keepdims=True)

    def gather(n, total):
        at = pl.ds(pl.multiple_of(n * tile, tile), tile)
        both = jnp.concatenate(
            [pieces_of(scaled_ref[:, at], 2), pieces_of(pull_ref[:, at], 2)], axis=0
        )
        return total + dot(both, stored_ref[at, :])

    total = lax.fori_loop(0, tiles, gather, jnp.zeros((4 * rows, width), F32))
    recalled = total[:rows] + total[rows : 2 * rows]
    moved = total[2 * rows : 3 * rows] + total[3 * rows :] - rest * query
    mixed_ref[...] = (1.0 - RECALL_SHARE) * query + RECALL_SHARE * recalled
    grad_query = (1.0 - RECALL_SHARE) * cotangent_ref[...].astype(F32) + moved * (2.0 / scale)
    sums_ref[0:1, :] = jnp.sum(grad_query * unit, axis=0, keepdims=True)
    sums_ref[1:2, :] = jnp.sum(grad_query, axis=0, keepdims=True)
    grad_ref[...] = norm_backward(grad_query, unit, inverse, gains)


def recall_padded(hidden, vectors, stored, usable, cotangent):
    unit, inverse = norm_parts(hidden)
    query = unit * vectors[8] + vectors[9]
    scale = DISTANCE_SCALE * math.sqrt(query.shape[-1])
    stored, cotangent = stored.astype(F32), cotangent.astype(F32)
    distance = jnp.sum(jnp.square(query[None] - stored), axis=-1)
    pull = RECALL_SHARE * jnp.sum(cotangent[None] * stored, axis=-1)
    scaled = jnp.where(usable, -distance / scale, FLOOR)
    raised = jnp.where(usable, jnp.exp(scaled - jnp.max(scaled, axis=0, keepdims=True)), 0.0)
    weights = raised / jnp.sum(raised, axis=0, keepdims=True)
    grad_scaled = weights * (pull - jnp.sum(weights * pull, axis=0, keepdims=True))
    recalled = jnp.sum(weights[..., None] * stored, axis=0)
    moved = jnp.sum(grad_scaled[..., None] * stored, axis=0)
    moved = moved - jnp.sum(grad_scaled, axis=0)[:, None] * query
    mixed = (1.0 - RECALL_SHARE) * query + RECALL_SHARE * recalled
    grad_query = (1.0 - RECALL_SHARE) * cotangent + moved * (2.0 / scale)
    sums = jnp.stack([jnp.sum(grad_query * unit, axis=0), jnp.sum(grad_query, axis=0)])
    grad = norm_backward(grad_query, unit, inverse, vectors[8])
    return mixed, grad, jnp.pad(sums, ((0, 6), (0, 0)))


def recall(hidden, vectors, stored, token_of, cotangent):
    rows, width = hidden.shape
    entries = stored.shape[0]
    operands = (hidden, vectors, cotangent, token_of.reshape(1, entries), stored)
    outs = [
        jax.ShapeDtypeStruct((rows, width), F32),
        jax.ShapeDtypeStruct((rows, width), F32),
        jax.ShapeDtypeStruct((8, width), F32),
    ]
    return local_call(
        functools.partial(recall_kernel, min(512, entries)),
        outs,
        operands,
        (1,),
        [whole(x) for x in operands],
        [whole(x) for x in outs],
        [VMEM((rows, entries), F32), VMEM((rows, entries), F32)],
        flops=16 * rows * width * entries,
    )


def shards(
    tokens,
    ln1_gain,
    ln1_bias,
    qkv_weight,
    out_weight,
    ln2_gain,
    ln2_bias,
    in_weight,
    fc_weight,
    final_gain,
    final_bias,
    datastore,
    neighbour_owner,
    neighbour_row,
    neighbour_count,
    cotangent,
):
    local_seqs, local_rows, width = tokens.shape
    rows = local_seqs * local_rows
    count, ring = lax.axis_size("dp"), lax.axis_size("ctx")
    devices = count * ring
    both = ("dp", "ctx")
    seqs = count * local_seqs // ring
    heads = HEADS // count
    slots = neighbour_owner.shape[2]
    part = width // devices
    head_width = width // count
    inner_width = in_weight.shape[2] // count

    forth = []
    for s in range(count):
        for p in range(ring):
            forth.append((s * ring + p, ((s // ring) * ring + p) * ring + s % ring))

    pair_room = -(-(3 * rows * slots) // (2 * devices * 16)) * 16
    room = rows * slots // ring
    owners = neighbour_owner.reshape(rows, slots)
    live = neighbour_count.reshape(rows, 1)
    hits = (owners[:, :, None] == jnp.arange(devices)[None, None, :]) & (
        jnp.arange(slots)[None, :, None] < live[:, :, None]
    )
    asked_all = jnp.sum(jnp.where(hits, neighbour_row.reshape(rows, slots, 1), 0), axis=1).T
    usable_all = jnp.any(hits, axis=1).T
    upto = jnp.arange(rows)[:, None] <= jnp.arange(rows)[None, :]
    order = dot(usable_all.astype(BF16), upto.astype(BF16))
    taken = usable_all[:, None, :] & (
        order[:, None, :] == jnp.arange(1, pair_room + 1, dtype=F32)[None, :, None]
    )
    asked = jnp.sum(jnp.where(taken, asked_all[:, None, :], 0), axis=-1)
    asked = asked.reshape(count, ring, 1, pair_room)
    asked = jnp.pad(asked, ((0, 0), (0, 0), (0, 7), (0, 128 - pair_room)))

    def by_plane(x):
        return x.reshape((count, ring) + x.shape[1:]).swapaxes(0, 1)

    token_at = by_plane(jnp.sum(jnp.where(taken, jnp.arange(rows)[None, None, :], 0), axis=-1))
    amounts = order[:, -1]
    usable = by_plane(jnp.arange(pair_room, dtype=F32)[None, :] < amounts[:, None])
    crowded = (jnp.max(amounts) > pair_room) | (jnp.max(jnp.sum(by_plane(amounts), axis=1)) > room)

    joint_own, expand_own = qkv_weight, in_weight
    if head_width % 128:
        joint_own = qkv_weight.reshape(LAYERS, part, 3, count, head_width).transpose(3, 0, 1, 2, 4)
        joint_own = joint_own.reshape(count, LAYERS, part, 3 * head_width)
        expand_own = in_weight.reshape(LAYERS, part, count, inner_width).transpose(2, 0, 1, 3)

    notes = jnp.where(usable, token_at, -1)
    last_all = lax.all_gather(fc_weight[1], "ctx", axis=0, tiled=False)
    exchange = functools.partial(plane_exchange, count, ring)
    first = first_exchange(
        count,
        ring,
        0,
        tokens.reshape(rows, width),
        asked,
        notes,
        crowded.astype(F32).reshape(1, 1),
        (
            ln1_gain,
            ln1_bias,
            ln2_gain,
            ln2_bias,
            final_gain.reshape(1, part),
            final_bias.reshape(1, part),
        ),
        datastore,
        joint_own,
        expand_own,
        (out_weight, fc_weight),
        ((0, 0), (1, 0), (0, 1)),
    )
    normed, vectors, served, notes, asked_notes, my_tokens = first[:6]
    joint, expand = list(first[6 : 6 + LAYERS]), list(first[6 + LAYERS : 6 + 2 * LAYERS])
    project, shrink = [first[-3], first[-1]], [first[-2], None]
    gain_one, shift_one = vectors[:LAYERS], vectors[LAYERS : 2 * LAYERS]
    gain_two, shift_two = vectors[2 * LAYERS : 3 * LAYERS], vectors[3 * LAYERS : 4 * LAYERS]
    crowded = jnp.max(vectors[4 * LAYERS + 2]) > 0.5
    stored = pack(asked_notes, served.reshape(count, ring, pair_room, width), room)
    stored = lax.all_to_all(stored, "ctx", split_axis=0, concat_axis=0, tiled=True)

    hidden = my_tokens.astype(F32)
    saved = []
    for layer in range(LAYERS):
        normed = normed.reshape(count * rows, width)
        joint[layer] = joint[layer].reshape(width, 3 * head_width)
        project[layer] = project[layer].reshape(-1, width)
        packed, attended, partial = attend(normed, joint[layer], project[layer], seqs, heads)
        partial = partial.reshape(count, rows, width)
        normed_two, middle = exchange(2, partial, hidden, gain_two[layer], shift_two[layer])
        if layer + 1 == LAYERS:
            shrink[layer], middle = after(last_all, middle)
        normed_two = normed_two.reshape(count * rows, width)
        expand[layer] = expand[layer].reshape(width, inner_width)
        shrink[layer] = shrink[layer].reshape(-1, width)
        inner, partial = forward(normed_two, expand[layer], shrink[layer])
        partial = partial.reshape(count, rows, width)
        saved.append((hidden, normed, packed, attended, middle, normed_two, inner))
        if layer + 1 < LAYERS:
            normed, hidden = exchange(
                2, partial, middle, gain_one[layer + 1], shift_one[layer + 1]
            )
        else:
            hidden, my_cotangent = exchange(
                5, partial, middle, gather=False, swaps=(cotangent.reshape(rows, width),)
            )

    def few():
        rank, _ = ranks_of(notes >= 0)
        chosen = (notes.reshape(ring, 1, -1) >= 0) & (
            rank[:, None, :] == jnp.arange(1, room + 1, dtype=F32)[None, :, None]
        )
        token_of = jnp.sum(jnp.where(chosen, notes.reshape(ring, 1, -1) + 1, 0), axis=-1) - 1
        entries = stored.reshape(ring * room, width)
        return recall(hidden, vectors, entries, token_of.reshape(-1), my_cotangent)

    def many():
        asked = lax.all_to_all(asked_all, both, split_axis=0, concat_axis=0, tiled=True)
        padded = datastore.at[asked.reshape(-1)].get(mode="promise_in_bounds")
        padded = padded.reshape(devices, rows, width)
        padded = lax.all_to_all(padded, both, split_axis=0, concat_axis=0, tiled=True)
        padded = lax.ppermute(padded, both, forth)
        marks = lax.ppermute(usable_all.astype(jnp.int32), both, forth)
        return recall_padded(hidden, vectors, padded, marks > 0, my_cotangent)

    mixed, grad_hidden, head_sums = lax.cond(crowded, many, few)
    branch, mixed = exchange(6, base=grad_hidden, swaps=(mixed.astype(BF16),))
    sums_one, sums_two = [None] * LAYERS, [None] * LAYERS
    joint_sums, expand_sums = [None] * LAYERS, [None] * LAYERS
    grad_tall = [None] * LAYERS
    for layer in reversed(range(LAYERS)):
        start, normed, packed, attended, middle, normed_two, inner = saved[layer]
        grad_expand, grad_shrink, partial = backward(
            branch.reshape(count * rows, width), normed_two, inner, expand[layer], shrink[layer]
        )
        grad_expand = grad_expand.reshape(count, ring, part, inner_width)
        grad_shrink = grad_shrink.reshape(ring, -1, width)
        cut = grad_shrink.shape[1] // 2
        grad_out, grad_middle, sums_two[layer], upper_sum, expand_sum = exchange(
            7,
            partial.reshape(count, rows, width),
            grad_hidden,
            gain_two[layer],
            saved=middle,
            sums=(grad_shrink[:, :cut], grad_expand),
        )
        expand_sums[layer] = expand_sum
        grad_joint, grad_project, partial = attend_backward(
            grad_out.reshape(count * rows, width),
            normed,
            packed,
            attended,
            joint[layer],
            project[layer],
            seqs,
            heads,
        )
        rides = (
            grad_project.reshape(ring, part, width),
            grad_shrink[:, cut:],
            grad_joint.reshape(count, ring, part, 3 * head_width),
        )
        partial = partial.reshape(count, rows, width)
        if layer > 0:
            branch, grad_hidden, sums_one[layer], project_sum, lower_sum, joint_sum = exchange(
                8, partial, grad_middle, gain_one[layer], saved=start, sums=rides
            )
        else:
            grad_hidden, sums_one[layer], project_sum, lower_sum, joint_sum, *mixes = exchange(
                9,
                partial,
                grad_middle,
                gain_one[layer],
                saved=start,
                gather=False,
                sums=rides,
                mixes=tuple(joint_sums[1:]) + tuple(expand_sums),
            )
        shrink_sum = jnp.concatenate([upper_sum, lower_sum], axis=0)
        joint_sums[layer] = joint_sum
        grad_tall[layer] = (project_sum, shrink_sum)

    sums = jnp.concatenate(
        [one[n : n + 1] for every in (sums_one, sums_two) for n in (0, 1) for one in every]
        + [head_sums[:2]]
    )
    sums = jnp.pad(sums, ((0, 6), (0, 0))).reshape(16, count, head_width).transpose(1, 0, 2)
    sums, qkv_grad, in_grad, tokens_grad = last_exchange(
        count,
        ring,
        10,
        sums,
        joint_sums[0],
        grad_hidden.astype(BF16),
        mixes[: LAYERS - 1],
        mixes[LAYERS - 1 :],
    )
    sums = lax.dynamic_slice_in_dim(sums, lax.axis_index("ctx") * part, part, axis=1)

    return (
        mixed.astype(F32).reshape(local_seqs, local_rows, width),
        tokens_grad.reshape(local_seqs, local_rows, width),
        sums[0:LAYERS],
        sums[LAYERS : 2 * LAYERS],
        qkv_grad,
        jnp.stack([pair[0] for pair in grad_tall]),
        sums[2 * LAYERS : 3 * LAYERS],
        sums[3 * LAYERS : 4 * LAYERS],
        in_grad,
        jnp.stack([pair[1] for pair in grad_tall]),
        sums[4 * LAYERS],
        sums[4 * LAYERS + 1],
    )


def solution(mesh):
    both = ("dp", "ctx")
    return jax.shard_map(
        shards,
        mesh=mesh,
        in_specs=(
            P("dp", "ctx", None),
            P(None, both),
            P(None, both),
            P(None, both, None),
            P(None, both, None),
            P(None, both),
            P(None, both),
            P(None, both, None),
            P(None, both, None),
            P(both),
            P(both),
            P(both, None),
            P("dp", "ctx", None),
            P("dp", "ctx", None),
            P("dp", "ctx"),
            P("dp", "ctx", None),
        ),
        out_specs=(
            P("dp", "ctx", None),
            P("dp", "ctx", None),
            P(None, both),
            P(None, both),
            P(None, both, None),
            P(None, both, None),
            P(None, both),
            P(None, both),
            P(None, both, None),
            P(None, both, None),
            P(both),
            P(both),
        ),
        check_vma=False,
    )
```

```python
import functools
import math

import jax
import jax.numpy as jnp
from jax import lax
from jax.experimental import pallas as pl
from jax.experimental.pallas import tpu as pltpu
from jax.sharding import PartitionSpec as P

HEADS = 16
LAYERS = 2

EPSILON = 1e-05
FLOOR = -1e30
RECALL_SHARE = 0.25
DISTANCE_SCALE = 1.5

MESH = pl.DeviceIdType.MESH
VMEM = pltpu.VMEM
BF16 = jnp.bfloat16
F32 = jnp.float32


def norm_parts(values):
    average = jnp.mean(values, axis=-1, keepdims=True)
    centered = values - average
    variance = jnp.mean(centered * centered, axis=-1, keepdims=True)
    inverse = lax.rsqrt(variance + EPSILON)
    return centered * inverse, inverse


def norm_backward(grad, unit, inverse, gains):
    scaled = grad * gains
    return inverse * (
        scaled
        - jnp.mean(scaled, axis=-1, keepdims=True)
        - unit * jnp.mean(scaled * unit, axis=-1, keepdims=True)
    )


def send(source, target, send_sem, recv_sem, where):
    copy = pltpu.make_async_remote_copy(
        src_ref=source,
        dst_ref=target,
        send_sem=send_sem,
        recv_sem=recv_sem,
        device_id=where,
        device_id_type=MESH,
    )
    copy.start()
    return copy


def partner_of(me, plane, ring):
    return ((me // ring) * ring + plane, me % ring), me % ring != plane


def greet_all(targets, partner=None, away=None):
    barrier = pltpu.get_barrier_semaphore()
    for target in targets:
        pl.semaphore_signal(barrier, inc=1, device_id=target, device_id_type=MESH)
    if partner is None:
        pl.semaphore_wait(barrier, len(targets))
        return

    @pl.when(away)
    def _():
        pl.semaphore_signal(barrier, inc=1, device_id=partner, device_id_type=MESH)

    pl.semaphore_wait(barrier, len(targets) + away.astype(jnp.int32))


def swap_begin(source, target, send_sem, recv_sem, partner, away):
    copy = pltpu.make_async_remote_copy(
        src_ref=source,
        dst_ref=target,
        send_sem=send_sem,
        recv_sem=recv_sem,
        device_id=partner,
        device_id_type=MESH,
    )
    stay = pltpu.make_async_copy(source, target, recv_sem)

    @pl.when(away)
    def _():
        copy.start()

    @pl.when(jnp.logical_not(away))
    def _():
        stay.start()

    return copy, stay, away


def swap_end(swap):
    copy, stay, away = swap

    @pl.when(away)
    def _():
        copy.wait()

    @pl.when(jnp.logical_not(away))
    def _():
        stay.wait()


def mate_of(count, me, k):
    if count != 8:
        return (me + k) % count
    step = (2 * k - 1) % 7 + 1
    core, x, y = (me + step) % 2, (me // 2 + step // 2) % 2, (me // 4 + step // 4) % 2
    return 4 * y + 2 * x + core


def square_of(me):
    core, x, y = me % 2, (me // 2) % 2, me // 4
    return (
        4 * y + 2 * (1 - x) + core,
        4 * (1 - y) + 2 * x + core,
        4 * (1 - y) + 2 * (1 - x) + core,
    )


def gather_sems(count):
    half = count // 2
    dma = pltpu.SemaphoreType.DMA
    if count == 8:
        return [dma((7,)), dma((7,)), dma((6,)), dma((6,))]
    return [dma((half,)), dma((half,)), dma((half - 1,)), dma((half - 1,))]


def gather_begin(count, me, plane, own_ref, full_ref, send_sem, recv_sem):
    half = count // 2
    chip, core = me // 2, me % 2
    sibling = 2 * chip + (1 - core)
    if count == 8:
        beside, beyond, _ = square_of(me)
        cut = own_ref.shape[0] // 2
        sends = {}
        for n, target, begin in ((1, beside, 0), (3, beyond, 1), (2, beside, 1), (4, beyond, 0)):
            at = pl.ds(begin * cut, cut)
            sends[n] = send(
                own_ref.at[at],
                full_ref.at[me, at],
                send_sem.at[n],
                recv_sem.at[n],
                (target, plane),
            )
        sends[0] = send(
            own_ref, full_ref.at[me], send_sem.at[0], recv_sem.at[0], (sibling, plane)
        )
        return sends
    targets = [sibling] + [2 * ((chip + j) % half) + core for j in range(1, half)]
    return {
        j: send(own_ref, full_ref.at[me], send_sem.at[j], recv_sem.at[j], (target, plane))
        for j, target in enumerate(targets)
    }


def hand_on(me, plane, passes, block, pass_send, pass_recv):
    n = len(passes)
    sibling = 2 * (me // 2) + (1 - me % 2)
    passes.append(send(block, block, pass_send.at[n], pass_recv.at[n], (sibling, plane)))


def gather_middle(count, me, plane, full_ref, sends, send_sem, recv_sem, pass_send, pass_recv):
    passes = []
    if count == 8:
        beside, beyond, _ = square_of(me)
        cut = full_ref.shape[1] // 2
        for n, device, begin, target in ((1, beside, 0, beyond), (3, beyond, 1, beside)):
            sends[n].wait_recv()
            block = full_ref.at[device, pl.ds(begin * cut, cut)]
            far = 5 if n == 1 else 6
            sends[far] = send(block, block, send_sem.at[far], recv_sem.at[far], (target, plane))
            hand_on(me, plane, passes, block, pass_send, pass_recv)
    return passes


def gather_end(count, me, plane, full_ref, sends, passes, pass_send, pass_recv):
    half = count // 2
    chip, core = me // 2, me % 2
    if count == 8:
        beside, beyond, across = square_of(me)
        cut = full_ref.shape[1] // 2
        for n, device, begin in ((2, beside, 1), (4, beyond, 0), (5, across, 0), (6, across, 1)):
            sends[n].wait_recv()
            block = full_ref.at[device, pl.ds(begin * cut, cut)]
            hand_on(me, plane, passes, block, pass_send, pass_recv)
    else:
        for j in range(1, half):
            sends[j].wait_recv()
            block = full_ref.at[2 * ((chip + half - j) % half) + core]
            hand_on(me, plane, passes, block, pass_send, pass_recv)
    sends[0].wait_recv()
    for copy in passes:
        copy.wait_recv()
    return list(sends.values()) + passes


def plane_kernel(count, ring, reduce, mode, gather, kinds, *refs):
    refs = list(refs)
    half = count // 2
    partial_ref = refs.pop(0) if reduce else None
    base_ref = refs.pop(0) if mode != "none" else None
    gain_ref = refs.pop(0) if mode in ("norm", "back") else None
    shift_ref = refs.pop(0) if mode == "norm" else None
    saved_ref = refs.pop(0) if mode == "back" else None
    ride_refs = [refs.pop(0) for _ in kinds]
    full_ref = refs.pop(0) if gather else None
    new_ref = refs.pop(0) if reduce else None
    stat_ref = refs.pop(0) if mode == "back" else None
    ride_outs = [refs.pop(0) for _ in kinds]
    square, paired = count == 8, ring == 4
    if reduce:
        mine_ref, side_ref, out_ref, in_ref = (refs.pop(0) for _ in range(4))
        mine_sem, side_send, side_recv, far_send, far_recv = (refs.pop(0) for _ in range(5))
    if gather:
        own_ref, own_sem = refs.pop(0), refs.pop(0)
        gather_send, gather_recv, pass_send, pass_recv = (refs.pop(0) for _ in range(4))
    land_refs = [refs.pop(0) if kind in ("sum0", "sum1") else None for kind in kinds]
    if kinds:
        ride_send, ride_recv, ride_own = refs.pop(0), refs.pop(0), refs.pop(0)

    me = lax.axis_index("dp")
    plane = lax.axis_index("ctx")
    chip, core = me // 2, me % 2
    sibling = 2 * chip + (1 - core)
    if square:
        peers = list(square_of(me))
    else:
        peers = [2 * ((chip + j) % half) + core for j in range(1, half)]

    greet = []
    if "mix" in kinds:
        greet += [((me + k) % count, plane) for k in range(1, count)]
    elif reduce or gather:
        greet += [(sibling, plane)] + [(peer, plane) for peer in peers]
    mate, twin = 2 * (plane // 2) + (1 - plane % 2), (plane + 2) % ring
    if any(kind in ("get0", "get1", "hop") for kind in kinds) or (kinds and not paired):
        greet += [(me, (plane + j) % ring) for j in range(1, ring)]
    elif "sum0" in kinds or "sum1" in kinds:
        greet += [(me, mate), (me, twin)]
    partner, away = partner_of(me, plane, ring)
    if "swap" in kinds:
        greet_all(greet, partner, away)
    else:
        greet_all(greet)
    pending = []
    rides, stays, swaps, mixes = [], [], [], []

    def to_mate(i, n, t):
        return send(
            ride_refs[i].at[t] if kinds[i] == "sum0" else ride_refs[i].at[:, t],
            land_refs[i].at[n],
            ride_send.at[i, n],
            ride_recv.at[i, n],
            (me, mate),
        )

    for i, kind in enumerate(kinds):
        if kind == "swap":
            swaps.append(
                swap_begin(
                    ride_refs[i],
                    ride_outs[i],
                    ride_send.at[i, 0],
                    ride_recv.at[i, 0],
                    partner,
                    away,
                )
            )
        if kind in ("sum0", "sum1") and paired:
            rides.append(to_mate(i, 0, 2 * (1 - plane // 2) + (1 - plane % 2)))
            continue
        for j in range(1, ring) if kind not in ("mix", "swap") else ():
            there = (plane + j) % ring
            if kind == "sum0":
                source, target = ride_refs[i].at[there], land_refs[i].at[j - 1]
            elif kind == "sum1":
                source, target = ride_refs[i].at[:, there], land_refs[i].at[j - 1]
            elif kind == "get0":
                source, target = ride_refs[i], ride_outs[i].at[plane]
            elif kind == "hop":
                source, target = ride_refs[i].at[there], ride_outs[i].at[plane]
            else:
                source, target = ride_refs[i], ride_outs[i].at[:, plane]
            rides.append(
                send(source, target, ride_send.at[i, j - 1], ride_recv.at[i, j - 1], (me, there))
            )
        if kind not in ("sum0", "sum1", "swap"):
            if kind == "mix":
                source, target = ride_refs[i].at[me], ride_outs[i].at[me]
            elif kind == "hop":
                source, target = ride_refs[i].at[plane], ride_outs[i].at[plane]
            elif kind == "get0":
                source, target = ride_refs[i], ride_outs[i].at[plane]
            else:
                source, target = ride_refs[i], ride_outs[i].at[:, plane]
            stay = pltpu.make_async_copy(source, target, ride_own.at[i])
            stay.start()
            stays.append(stay)
    pending += rides

    def chunks_of(i):
        steps = ride_outs[i].shape[0]
        chunk = 1 if kinds[i] == "sum1" else min(steps, 32)
        return steps // chunk, chunk

    def own_part(i, at, t):
        return (ride_refs[i][t, at] if kinds[i] == "sum0" else ride_refs[i][at, t]).astype(F32)

    pairs = [i for i, kind in enumerate(kinds) if kind in ("sum0", "sum1") and paired]

    def add_pairs(most):
        for i in pairs[len(crossing) : len(crossing) + most]:
            rides[i].wait_recv()
            steps, chunk = chunks_of(i)

            def add(step, carry, i=i, chunk=chunk):
                at = pl.ds(pl.multiple_of(step * chunk, chunk), chunk)
                total = own_part(i, at, twin) + land_refs[i][0, at].astype(F32)
                land_refs[i][3, at] = total.astype(BF16)
                return carry

            lax.fori_loop(0, steps, add, 0)
            crossing.append(
                send(
                    land_refs[i].at[3],
                    land_refs[i].at[2],
                    ride_send.at[i, 2],
                    ride_recv.at[i, 2],
                    (me, twin),
                )
            )
        if len(crossing) == len(pairs) and not staying:
            staying.extend(to_mate(i, 1, mate) for i in pairs)

    def begin_mixes():
        for i, kind in enumerate(kinds):
            for k in range(1, count) if kind == "mix" else ():
                there = mate_of(count, me, k)
                mixes.append(
                    send(
                        ride_refs[i].at[there],
                        ride_outs[i].at[me],
                        ride_send.at[i, k - 1],
                        ride_recv.at[i, k - 1],
                        (there, plane),
                    )
                )

    staying = []
    crossing = []
    if reduce:
        if square:
            beside, beyond, across = peers
            order = [across // 2, beside // 2, beyond // 2, chip]
        else:
            order = [(chip + j + 1) % half for j in range(half)]
        side, mine = [], []
        for j, where in enumerate(order):
            side.append(
                send(
                    partial_ref.at[2 * where + (1 - core)],
                    side_ref.at[j],
                    side_send.at[j],
                    side_recv.at[j],
                    (sibling, plane),
                )
            )
            mine.append(
                pltpu.make_async_copy(
                    partial_ref.at[2 * where + core], mine_ref.at[j], mine_sem.at[j]
                )
            )
            mine[-1].start()

        def pair_sum(j):
            mine[j].wait()
            side[j].wait_recv()
            return mine_ref[j].astype(F32) + side_ref[j].astype(F32)

        far = []
        if square:
            cut = out_ref.shape[1] // 2
            upper, lower = pl.ds(0, cut), pl.ds(cut, cut)

            def give(source, slot, target):
                far.append(
                    send(
                        source,
                        in_ref.at[slot],
                        far_send.at[slot],
                        far_recv.at[slot],
                        (target, plane),
                    )
                )

            out_ref[0] = pair_sum(0).astype(BF16)
            give(out_ref.at[0, upper], 0, beside)
            give(out_ref.at[0, lower], 3, beyond)
            out_ref[1] = pair_sum(1).astype(BF16)
            give(out_ref.at[1, upper], 1, beside)
            out_ref[2] = pair_sum(2).astype(BF16)
            give(out_ref.at[2, lower], 4, beyond)
            total = pair_sum(3)
            add_pairs(1)
            far[0].wait_recv()
            out_ref[3, upper] = (out_ref[2, upper].astype(F32) + in_ref[0].astype(F32)).astype(BF16)
            give(out_ref.at[3, upper], 5, beyond)
            far[1].wait_recv()
            out_ref[3, lower] = (out_ref[1, lower].astype(F32) + in_ref[3].astype(F32)).astype(BF16)
            give(out_ref.at[3, lower], 2, beside)
            begin_mixes()
            add_pairs(1)
            far[2].wait_recv()
            far[3].wait_recv()
            far[4].wait_recv()
            far[5].wait_recv()
            total = total + jnp.concatenate(
                [
                    in_ref[1].astype(F32) + in_ref[5].astype(F32),
                    in_ref[4].astype(F32) + in_ref[2].astype(F32),
                ],
                axis=0,
            )
        else:
            for j in range(1, half):
                out_ref[j - 1] = pair_sum(j - 1).astype(BF16)
                far.append(
                    send(
                        out_ref.at[j - 1],
                        in_ref.at[j - 1],
                        far_send.at[j - 1],
                        far_recv.at[j - 1],
                        (peers[j - 1], plane),
                    )
                )
            total = pair_sum(half - 1)
            for j in range(1, half):
                far[j - 1].wait_recv()
                total = total + in_ref[j - 1].astype(F32)
        pending += side + far
    if mode == "norm":
        value = base_ref[...] + total
        new_ref[...] = value
        unit, _ = norm_parts(value)
        result = unit * gain_ref[...] + shift_ref[...]
    elif mode == "back":
        unit, inverse = norm_parts(saved_ref[...].astype(F32))
        stat_ref[0:1, :] = jnp.sum(total * unit, axis=0, keepdims=True)
        stat_ref[1:2, :] = jnp.sum(total, axis=0, keepdims=True)
        result = base_ref[...] + norm_backward(total, unit, inverse, gain_ref[...])
        new_ref[...] = result
    elif mode == "plain":
        result = base_ref[...]
        if reduce:
            result = result + total
            new_ref[...] = result

    if gather:
        own_ref[...] = result.astype(BF16)
        sends = gather_begin(count, me, plane, own_ref, full_ref, gather_send, gather_recv)
        stay = pltpu.make_async_copy(own_ref, full_ref.at[me], own_sem)
        stay.start()
        stays.append(stay)
    if not (reduce and square):
        begin_mixes()
    add_pairs(len(pairs))
    if gather:
        passes = gather_middle(
            count, me, plane, full_ref, sends, gather_send, gather_recv, pass_send, pass_recv
        )
        pending += gather_end(count, me, plane, full_ref, sends, passes, pass_send, pass_recv)
    n = len(pairs)
    for copy in rides[n:] + mixes + staying + crossing:
        copy.wait_recv()
    pending += mixes + staying + crossing
    for copy in stays:
        copy.wait()
    for swap in swaps:
        swap_end(swap)
    for i, kind in enumerate(kinds):
        if kind not in ("sum0", "sum1"):
            continue
        steps, chunk = chunks_of(i)

        def add(step, carry, i=i, chunk=chunk):
            at = pl.ds(pl.multiple_of(step * chunk, chunk), chunk)
            total = own_part(i, at, plane)
            for j in (1, 2) if paired else range(ring - 1):
                total = total + land_refs[i][j, at].astype(F32)
            ride_outs[i][at] = total.astype(ride_outs[i].dtype)
            return carry

        lax.fori_loop(0, steps, add, 0)
    for copy in pending:
        copy.wait_send()


def plane_exchange(
    count,
    ring,
    call_id,
    partial=None,
    base=None,
    gains=None,
    shifts=None,
    saved=None,
    gather=True,
    sums=(),
    gets=(),
    mixes=(),
    hops=(),
    swaps=(),
):
    reduce = partial is not None
    mode = "none" if base is None else "plain"
    if gains is not None:
        mode = "norm" if saved is None else "back"
    half = count // 2
    operands = [partial] if reduce else []
    if base is not None:
        operands.append(base)
        rows, width = base.shape
    if gains is not None:
        operands.append(gains.reshape(1, width))
    if mode == "norm":
        operands.append(shifts.reshape(1, width))
    if mode == "back":
        operands.append(saved)
    operands += sums
    specs = [pl.BlockSpec(memory_space=VMEM)] * len(operands)
    if reduce:
        specs[0] = pl.BlockSpec(memory_space=pltpu.HBM)
    operands += list(gets) + list(mixes) + list(hops) + list(swaps)
    specs += [pl.BlockSpec(memory_space=pltpu.HBM)] * (len(operands) - len(specs))
    kinds = tuple("sum" + str(x.ndim - 3) for x in sums)
    kinds += tuple("get" + str(x.ndim - 2) for x in gets)
    kinds += ("mix",) * len(mixes) + ("hop",) * len(hops) + ("swap",) * len(swaps)
    outs, scratch = [], []
    if gather:
        outs.append(jax.ShapeDtypeStruct((count, rows, width), BF16))
    if reduce:
        outs.append(jax.ShapeDtypeStruct((rows, width), F32))
    if mode == "back":
        outs.append(jax.ShapeDtypeStruct((8, width), F32))
    lands = [x.shape[1:] if x.ndim == 3 else x.shape[:1] + x.shape[2:] for x in sums]
    outs += [
        jax.ShapeDtypeStruct(land, F32 if x.ndim == 3 else BF16) for land, x in zip(lands, sums)
    ]
    out_specs = [pl.BlockSpec(memory_space=VMEM)] * len(outs)
    if gather:
        out_specs[0] = pl.BlockSpec(memory_space=pltpu.HBM)
    outs += [
        jax.ShapeDtypeStruct((ring,) + x.shape if x.ndim == 2 else (count, ring) + x.shape[1:], BF16)
        for x in gets
    ]
    outs += [jax.ShapeDtypeStruct(x.shape, x.dtype) for x in list(mixes) + list(hops) + list(swaps)]
    out_specs += [pl.BlockSpec(memory_space=pltpu.HBM)] * (len(outs) - len(out_specs))
    dma = pltpu.SemaphoreType.DMA
    if reduce:
        taken = (6, rows // 2, width) if count == 8 else (half - 1, rows, width)
        scratch += [
            VMEM((half, rows, width), BF16),
            VMEM((half, rows, width), BF16),
            VMEM((half, rows, width), BF16),
            VMEM(taken, BF16),
            dma((half,)),
            dma((half,)),
            dma((half,)),
            dma(taken[:1]),
            dma(taken[:1]),
        ]
    if gather:
        scratch += [VMEM((rows, width), BF16), dma] + gather_sems(count)
    scratch += [VMEM((4 if ring == 4 else ring - 1,) + land, BF16) for land in lands]
    if kinds:
        most = max(ring, count if mixes else 0) - 1
        scratch += [dma((len(kinds), most)), dma((len(kinds), most)), dma((len(kinds),))]
    return pl.pallas_call(
        functools.partial(plane_kernel, count, ring, reduce, mode, gather, kinds),
        out_shape=tuple(outs),
        in_specs=specs,
        out_specs=tuple(out_specs),
        scratch_shapes=scratch,
        compiler_params=pltpu.CompilerParams(
            collective_id=call_id, has_side_effects=True, vmem_limit_bytes=16 * 1024 * 1024
        ),
        cost_estimate=pl.CostEstimate(
            flops=0, bytes_accessed=(60 if reduce else 30) << 20, transcendentals=0
        ),
    )(*operands)


def relay(source, target, sems, where, begin):
    copy = pltpu.make_async_remote_copy(
        src_ref=source,
        dst_ref=target,
        send_sem=sems[0],
        recv_sem=sems[1],
        device_id=where,
        device_id_type=MESH,
    )
    if begin:
        copy.start()
    return copy


def relay_begin(ring, me, plane, own, place, send_sem, recv_sem):
    for side, shift in ((0, 1), (1, -1)):
        there = (me, (plane + ring + shift) % ring)
        sems = (send_sem.at[side, 0], recv_sem.at[side, 0])

        @pl.when(plane < ring - 1 if side == 0 else plane > 0)
        def _(there=there, sems=sems):
            relay(own, place(plane), sems, there, True)


def relay_step(ring, me, plane, step, place, send_sem, recv_sem):
    for side, shift in ((0, 1), (1, -1)):
        there = (me, (plane + ring + shift) % ring)
        origin = (plane + ring - shift * step) % ring
        came = plane >= step if side == 0 else plane < ring - step
        more = plane < ring - 1 if side == 0 else plane > 0

        @pl.when(came)
        def _(side=side, there=there, origin=origin):
            block = place(origin)
            sems = (send_sem.at[side, step - 1], recv_sem.at[side, step - 1])
            relay(block, block, sems, there, False).wait_recv()

        if step < ring - 1:

            @pl.when(jnp.logical_and(came, more))
            def _(side=side, there=there, origin=origin):
                block = place(origin)
                sems = (send_sem.at[side, step], recv_sem.at[side, step])
                relay(block, block, sems, there, True)


def relay_end(ring, me, plane, place, send_sem, recv_sem):
    for step in range(ring - 1):
        for side, shift in ((0, 1), (1, -1)):
            there = (me, (plane + ring + shift) % ring)
            came = plane >= step if side == 0 else plane < ring - step
            more = plane < ring - 1 if side == 0 else plane > 0

            @pl.when(jnp.logical_and(came, more))
            def _(side=side, there=there):
                block = place(plane)
                sems = (send_sem.at[side, step], recv_sem.at[side, step])
                relay(block, block, sems, there, False).wait_send()


def first_kernel(count, ring, layers, talls, picks, *refs):
    refs = list(refs)
    token_ref, asked_ref, note_ref, crowded_ref = (refs.pop(0) for _ in range(4))
    vector_refs = [refs.pop(0) for _ in range(6)]
    store_ref = refs.pop(0)
    column_refs = [refs.pop(0) for _ in range(2)]
    tall_refs = [refs.pop(0) for _ in range(talls)]
    full_ref, vector_ref, rows_ref, mine_ref, notes_ref, guest_ref = (refs.pop(0) for _ in range(6))
    wide_refs = [[refs.pop(0) for _ in range(layers)] for _ in range(2)]
    whole_refs = [refs.pop(0) for _ in picks]
    small_all, small_ref, wanted_ref = refs.pop(0), refs.pop(0), refs.pop(0)
    asked_in, asked_all, asked_rows = (refs.pop(0) for _ in range(3))
    column_all = [refs.pop(0) for _ in range(2)]
    own_sem, own_ref = refs.pop(0), refs.pop(0)
    held_ref, total_ref, served_ref, held_sem = (refs.pop(0) for _ in range(4))
    (
        gather_send,
        gather_recv,
        pass_send,
        pass_recv,
        small_send,
        small_recv,
        across_send,
        across_recv,
        column_send,
        column_recv,
        relay_send,
        relay_recv,
        flag_send,
        flag_recv,
        rows_send,
        rows_recv,
        swap_send,
        swap_recv,
        guest_send,
        guest_recv,
        mix_send,
        mix_recv,
        hop_send,
        hop_recv,
    ) = refs
    me = lax.axis_index("dp")
    plane = lax.axis_index("ctx")
    hold = pltpu.make_async_copy(store_ref, held_ref, held_sem)
    hold.start()
    mates = [mate_of(count, me, k) for k in range(1, count)]
    planes = [(plane + j) % ring for j in range(1, ring)]
    part = vector_refs[0].shape[1]
    spot = lax.broadcasted_iota(jnp.int32, (part, 128), 1)
    tile = (spot % part == lax.broadcasted_iota(jnp.int32, (part, 128), 0)).astype(F32).astype(BF16)
    lane = lax.broadcasted_iota(jnp.int32, (1, 128), 1)
    here = lane // part == (me * ring + plane) % (128 // part)
    at = 0
    for ref in vector_refs:
        size = ref.shape[0]
        small_ref[at : at + size, :] = jnp.where(here, dot(ref[...], tile), 0.0)
        at += size
    small_ref[at : at + 1, :] = jnp.broadcast_to(crowded_ref[...], (1, 128))
    small_ref[at + 1 :, :] = jnp.zeros((16 - at - 1, 128), F32)
    partner, away = partner_of(me, plane, ring)
    greet_all([(mate, plane) for mate in mates] + [(me, there) for there in planes], partner, away)
    asks = [
        send(asked_ref.at[mate], asked_in.at[me], mix_send.at[k], mix_recv.at[k], (mate, plane))
        for k, mate in enumerate(mates)
    ]
    swap = swap_begin(note_ref, mine_ref, swap_send, swap_recv, partner, away)
    guest = swap_begin(token_ref, guest_ref, guest_send, guest_recv, partner, away)
    asked_in[me] = asked_ref[me]

    stays = []

    def stay(source, target):
        copy = pltpu.make_async_copy(source, target, own_sem.at[len(stays)])
        copy.start()
        stays.append(copy)

    small_all[me, plane] = small_ref[...]
    smalls = [
        send(small_ref, small_all.at[me, plane], small_send.at[k], small_recv.at[k], (mate, plane))
        for k, mate in enumerate(mates)
    ]
    columns = []
    for i in range(2):
        pieces = 3 if i == 0 and len(column_refs[0].shape) == 3 else 1
        lanes = column_all[i].shape[-1] // pieces
        for n in range(pieces):

            def block(device, i=i, n=n, lanes=lanes, pieces=pieces):
                if len(column_refs[i].shape) == 4:
                    return column_refs[i].at[device]
                at = pl.multiple_of((n * count + device) * lanes, 128)
                return column_refs[i].at[:, :, pl.ds(at, lanes)]

            target = column_all[i].at[me]
            if pieces > 1:
                target = column_all[i].at[me, :, :, n * lanes : (n + 1) * lanes]
            stay(block(me), target)
            for k, mate in enumerate(mates):
                columns.append(
                    send(
                        block(mate),
                        target,
                        column_send.at[3 * i + n, k],
                        column_recv.at[3 * i + n, k],
                        (mate, plane),
                    )
                )
    column_stays = stays[:]
    for copy in asks:
        copy.wait_recv()
    hops = [
        send(
            asked_in.at[:, there],
            asked_all.at[plane],
            hop_send.at[j],
            hop_recv.at[j],
            (me, there),
        )
        for j, there in enumerate(planes)
    ]
    pending = smalls + columns + asks + hops
    for n in range(count):
        asked_all[plane, n] = asked_in[n, plane]
    late = []
    for copy in smalls:
        copy.wait_recv()
    across = [
        send(
            small_all.at[:, plane],
            small_all.at[:, plane],
            across_send.at[j],
            across_recv.at[j],
            (me, there),
        )
        for j, there in enumerate(planes)
    ]

    relays = []

    def spread(own, place):
        n = len(relays)
        relays.append((place, relay_send.at[n], relay_recv.at[n]))
        stay(own, place(plane))
        relay_begin(ring, me, plane, own, *relays[-1])

    def spread_tall(i):
        array, layer = picks[i]
        spread(tall_refs[array].at[layer], lambda p: whole_refs[i].at[p])

    for i in range(2):
        spread_tall(i)
    swap_end(swap)
    for j, there in enumerate(planes):
        late.append(
            send(
                mine_ref.at[there],
                notes_ref.at[plane],
                flag_send.at[j],
                flag_recv.at[j],
                (me, there),
            )
        )
    notes_ref[plane] = mine_ref[plane]
    hold.wait()
    size = served_ref.shape[1]
    entries = size // ring
    for copy in hops:
        copy.wait_recv()
    for p in range(ring):
        for n in range(count):
            asked_rows[p * count + n : p * count + n + 1, :] = asked_all[p, n, 0:1, :].astype(F32)
    wanted_ref[...] = jnp.transpose(asked_rows[...])[:entries, :]
    depth = min(1024, held_ref.shape[0])

    def rows_copy(k):
        mate = mate_of(count, me, k)
        return pltpu.make_async_remote_copy(
            src_ref=served_ref.at[mate],
            dst_ref=rows_ref.at[me],
            send_sem=rows_send.at[k - 1],
            recv_sem=rows_recv.at[k - 1],
            device_id=(mate, plane),
            device_id_type=MESH,
        )

    def pick(mate):
        first = (mate % ring) * count + (mate // ring) * ring
        spots = lax.broadcasted_iota(jnp.int32, wanted_ref.shape, 1)
        columns_of = [
            jnp.sum(jnp.where(spots == first + n, wanted_ref[...], 0.0), axis=1, keepdims=True)
            for n in range(ring)
        ]
        wanted = jnp.concatenate(columns_of, axis=0).astype(jnp.int32)
        total_ref[...] = jnp.zeros_like(total_ref)

        def look(n, carry):
            at = pl.ds(pl.multiple_of(n * depth, depth), depth)
            marks = wanted == n * depth + lax.broadcasted_iota(jnp.int32, (size, depth), 1)
            total_ref[...] += dot(marks.astype(F32).astype(BF16), held_ref[at, :])
            return carry

        lax.fori_loop(0, held_ref.shape[0] // depth, look, 0)
        served_ref[mate] = total_ref[...].astype(BF16)

    def serve(k, carry):
        pick(mate_of(count, me, k))
        rows_copy(k).start()
        return carry

    serve(1, 0)
    for copy in columns:
        copy.wait_recv()
    for copy in column_stays:
        copy.wait()
    for layer in range(layers):
        for i in range(2):
            spread(
                column_all[i].at[:, layer],
                lambda p, layer=layer, i=i: wide_refs[i][layer].at[:, p],
            )
    for i in range(2, len(picks)):
        spread_tall(i)
    for copy in across:
        copy.wait_recv()
    groups = vector_ref.shape[1] // 128
    members = count * ring // groups
    for group in range(groups):
        total = small_all[group * members // ring, group * members % ring]
        for n in range(group * members + 1, (group + 1) * members):
            total = total + small_all[n // ring, n % ring]
        vector_ref[:, group * 128 : (group + 1) * 128] = total
    swap_end(guest)
    unit, _ = norm_parts(guest_ref[...].astype(F32))
    shift = vector_refs[0].shape[0]
    own_ref[...] = (unit * vector_ref[0:1, :] + vector_ref[shift : shift + 1, :]).astype(BF16)
    stay(own_ref, full_ref.at[me])
    sends = gather_begin(count, me, plane, own_ref, full_ref, gather_send, gather_recv)
    serve(2, 0)
    passes = gather_middle(
        count, me, plane, full_ref, sends, gather_send, gather_recv, pass_send, pass_recv
    )
    lax.fori_loop(3, count // 2, serve, 0)
    for one in relays:
        relay_step(ring, me, plane, 1, *one)
    lax.fori_loop(count // 2, count - 1, serve, 0)
    for one in relays:
        relay_step(ring, me, plane, 2, *one)
    serve(count - 1, 0)
    pick(me)
    stay(served_ref.at[me], rows_ref.at[me])
    for step in range(3, ring):
        for one in relays:
            relay_step(ring, me, plane, step, *one)
    pending += gather_end(count, me, plane, full_ref, sends, passes, pass_send, pass_recv)
    for copy in late:
        copy.wait_recv()

    def rows_done(k, carry):
        rows_copy(k).wait()
        return carry

    lax.fori_loop(1, count, rows_done, 0)
    for copy in stays[len(column_stays) :]:
        copy.wait()
    for copy in pending + across + late:
        copy.wait_send()
    for one in relays:
        relay_end(ring, me, plane, *one)


def first_exchange(
    count, ring, call_id, tokens, asked, notes, crowded, vectors, store, joint, expand, talls, picks
):
    rows, width = tokens.shape
    layers, part = talls[0].shape[0], joint.shape[-2]
    size = ring * notes.shape[-1]
    spread = max(128, count * ring)
    columns = []
    for x in (joint, expand):
        columns.append((count, layers, part, x.shape[-1] if x.ndim == 4 else x.shape[-1] // count))
    dma = pltpu.SemaphoreType.DMA
    near, far = pl.BlockSpec(memory_space=VMEM), pl.BlockSpec(memory_space=pltpu.HBM)
    outs = [
        jax.ShapeDtypeStruct((count, rows, width), BF16),
        jax.ShapeDtypeStruct((16, width), F32),
        jax.ShapeDtypeStruct((count, size, width), BF16),
        jax.ShapeDtypeStruct(notes.shape, notes.dtype),
        jax.ShapeDtypeStruct(notes.shape, notes.dtype),
        jax.ShapeDtypeStruct(tokens.shape, BF16),
    ]
    for shape in columns:
        outs += [jax.ShapeDtypeStruct((count, ring) + shape[2:], BF16)] * layers
    outs += [jax.ShapeDtypeStruct((ring,) + talls[i].shape[1:], BF16) for i, _ in picks]

    def pair(*shape):
        return [dma(shape), dma(shape)]

    return pl.pallas_call(
        functools.partial(first_kernel, count, ring, layers, len(talls), picks),
        out_shape=tuple(outs),
        in_specs=[near] * (4 + len(vectors)) + [far] * (3 + len(talls)),
        out_specs=tuple([far, near, far, near, near, near] + [far] * (2 * layers + len(picks))),
        scratch_shapes=[
            VMEM((count, ring, 16, 128), F32),
            VMEM((16, 128), F32),
            VMEM((size // ring, spread), F32),
            VMEM(asked.shape, jnp.int32),
            VMEM((ring, count) + asked.shape[2:], jnp.int32),
            VMEM((spread, 128), F32),
            VMEM(columns[0], BF16),
            VMEM(columns[1], BF16),
            dma((6 + 2 * layers + len(picks),)),
            VMEM((rows, width), BF16),
            VMEM(store.shape, BF16),
            VMEM((size, width), F32),
            VMEM((count, size, width), BF16),
            dma,
        ]
        + gather_sems(count)
        + pair(count - 1)
        + pair(ring - 1)
        + pair(4, count - 1)
        + pair(2 * layers + len(picks), 2, ring - 1)
        + pair(ring - 1)
        + pair(count - 1)
        + [dma, dma, dma, dma]
        + pair(count - 1)
        + pair(ring - 1),
        compiler_params=pltpu.CompilerParams(
            collective_id=call_id, has_side_effects=True, vmem_limit_bytes=61 * 1024 * 1024
        ),
        cost_estimate=pl.CostEstimate(flops=0, bytes_accessed=200 << 20, transcendentals=0),
    )(tokens, asked, notes, crowded, *vectors, store, joint, expand, *talls)


def last_kernel(
    count,
    ring,
    layers,
    sums_ref,
    wide_ref,
    rows_ref,
    *refs,
):
    refs = list(refs)
    joint_refs = [refs.pop(0) for _ in range(layers - 1)]
    expand_refs = [refs.pop(0) for _ in range(layers)]
    total_ref, joint_grad_ref, expand_grad_ref, home_ref = (refs.pop(0) for _ in range(4))
    sums_in, across_ref, mixed_ref, rows_in = (refs.pop(0) for _ in range(4))
    (
        own_sem,
        swap_send,
        swap_recv,
        sums_send,
        sums_recv,
        wide_send,
        wide_recv,
        across_send,
        across_recv,
    ) = refs
    me = lax.axis_index("dp")
    plane = lax.axis_index("ctx")
    partner, away = partner_of(me, plane, ring)
    greet = [((me + k) % count, plane) for k in range(1, count)]
    greet += [(me, (plane + j) % ring) for j in range(1, ring)]
    greet_all(greet, partner, away)

    pending, sums = [], []
    for k in range(1, count):
        there = mate_of(count, me, k)
        sums.append(
            send(
                sums_ref.at[there],
                sums_in.at[me],
                sums_send.at[k - 1],
                sums_recv.at[k - 1],
                (there, plane),
            )
        )
    swap = swap_begin(rows_ref, rows_in, swap_send, swap_recv, partner, away)
    for k in range(1, count):
        there = mate_of(count, me, k)
        pending.append(
            send(
                wide_ref.at[there],
                mixed_ref.at[me],
                wide_send.at[k - 1],
                wide_recv.at[k - 1],
                (there, plane),
            )
        )
    sums_in[me] = sums_ref[me]
    stay = pltpu.make_async_copy(wide_ref.at[me], mixed_ref.at[me], own_sem)
    stay.start()
    for copy in sums:
        copy.wait_recv()
    total = sums_in[0]
    for k in range(1, count):
        total = total + sums_in[k]
    across_ref[plane] = total
    across = [
        send(
            across_ref.at[plane],
            across_ref.at[plane],
            across_send.at[j - 1],
            across_recv.at[j - 1],
            (me, (plane + j) % ring),
        )
        for j in range(1, ring)
    ]
    inner = expand_refs[0].shape[2]
    size = wide_ref.shape[2] // 3
    for layer in range(layers):
        for k in range(count):
            expand_grad_ref[layer, :, k * inner : (k + 1) * inner] = expand_refs[layer][k].astype(F32)

    def spread(layer, ref):
        for k in range(count):
            for i in range(3):
                at = (i * count + k) * size
                joint_grad_ref[layer, :, at : at + size] = ref[
                    k, :, i * size : (i + 1) * size
                ].astype(F32)

    for layer in range(1, layers):
        spread(layer, joint_refs[layer - 1])
    for copy in across:
        copy.wait_recv()
    total = across_ref[0]
    for j in range(1, ring):
        total = total + across_ref[j]
    total_ref[...] = total
    for copy in pending:
        copy.wait_recv()
    stay.wait()
    spread(0, mixed_ref)
    swap_end(swap)
    home_ref[...] = rows_in[...].astype(F32)
    for copy in pending + sums + across:
        copy.wait_send()


def last_exchange(count, ring, call_id, sums, wide, rows, joints, expands):
    dma = pltpu.SemaphoreType.DMA
    layers = len(expands)
    part = wide.shape[1]
    operands = (sums, wide, rows, *joints, *expands)
    outs = (
        jax.ShapeDtypeStruct(sums.shape[1:], F32),
        jax.ShapeDtypeStruct((layers, part, count * wide.shape[2]), F32),
        jax.ShapeDtypeStruct((layers, part, count * expands[0].shape[2]), F32),
        jax.ShapeDtypeStruct(rows.shape, F32),
    )
    spec = pl.BlockSpec(memory_space=VMEM)
    return pl.pallas_call(
        functools.partial(last_kernel, count, ring, layers),
        out_shape=outs,
        in_specs=[spec] * len(operands),
        out_specs=(spec,) * len(outs),
        scratch_shapes=[
            VMEM(sums.shape, F32),
            VMEM((ring,) + sums.shape[1:], F32),
            VMEM(wide.shape, BF16),
            VMEM(rows.shape, BF16),
            dma,
            dma,
            dma,
            dma((count - 1,)),
            dma((count - 1,)),
            dma((count - 1,)),
            dma((count - 1,)),
            dma((ring - 1,)),
            dma((ring - 1,)),
        ],
        compiler_params=pltpu.CompilerParams(
            collective_id=call_id, has_side_effects=True, vmem_limit_bytes=16 * 1024 * 1024
        ),
    )(*operands)


GATE_SCALE = math.sqrt(2.0 / math.pi)
GATE_CUBE = 0.044715


def after(*arrays):
    return lax.optimization_barrier(arrays)


def dot(left, right):
    return jnp.dot(left, right, preferred_element_type=F32)


def contract_rows(left, right):
    return lax.dot_general(left, right, (((0,), (0,)), ((), ())), preferred_element_type=F32)


def contract_cols(left, right):
    return lax.dot_general(left, right, (((1,), (1,)), ((), ())), preferred_element_type=F32)


def local_call(body, outs, operands, grid, in_specs, out_specs, scratch=(), flops=0, grant=32):
    moved = sum(math.prod(x.shape) * x.dtype.itemsize for x in list(operands) + list(outs))
    return pl.pallas_call(
        body,
        out_shape=tuple(outs),
        grid=grid,
        in_specs=in_specs,
        out_specs=tuple(out_specs),
        scratch_shapes=list(scratch),
        compiler_params=pltpu.CompilerParams(vmem_limit_bytes=grant * 1024 * 1024),
        cost_estimate=pl.CostEstimate(flops=flops, bytes_accessed=moved, transcendentals=0),
    )(*operands)


def whole(x):
    return pl.BlockSpec(x.shape, lambda *_, n=len(x.shape): (0,) * n)


def stripe(shape):
    return pl.BlockSpec(shape, lambda i: (i,) + (0,) * (len(shape) - 1))


def probabilities(queries, keys, begin):
    scores = contract_cols(queries, keys) * (queries.shape[-1] ** (-0.5))
    row = begin + lax.broadcasted_iota(jnp.int32, scores.shape, 0)
    allowed = row >= lax.broadcasted_iota(jnp.int32, scores.shape, 1)
    scores = jnp.where(allowed, scores, FLOOR)
    raised = jnp.exp(scores - jnp.max(scores, axis=-1, keepdims=True))
    return raised / jnp.sum(raised, axis=-1, keepdims=True)


def attend_kernel(heads, block, x_ref, joint_ref, project_ref, packed_ref, attended_ref, partial_ref):
    packed_ref[...] = dot(x_ref[...], joint_ref[...]).astype(BF16)
    length, width = attended_ref.shape
    size = width // heads
    for head in range(heads):
        at = head * size
        for begin in range(0, length, block):
            end = begin + block
            probs = probabilities(
                packed_ref[begin:end, at : at + size], packed_ref[:end, width + at : width + at + size], begin
            )
            values = packed_ref[:end, 2 * width + at : 2 * width + at + size]
            attended_ref[begin:end, at : at + size] = dot(probs.astype(BF16), values).astype(BF16)
    partial_ref[...] = dot(attended_ref[...], project_ref[...]).astype(BF16)


def attend(normed, joint, project, seqs, heads, grant):
    rows, width = normed.shape
    length, inner = rows // seqs, project.shape[0]
    outs = [
        jax.ShapeDtypeStruct((rows, 3 * inner), BF16),
        jax.ShapeDtypeStruct((rows, inner), BF16),
        jax.ShapeDtypeStruct((rows, width), BF16),
    ]
    return local_call(
        functools.partial(attend_kernel, heads, min(256, length)),
        outs,
        (normed, joint, project),
        (seqs,),
        [stripe((length, width)), whole(joint), whole(project)],
        [stripe((length, 3 * inner)), stripe((length, inner)), stripe((length, width))],
        flops=8 * rows * width * inner,
        grant=grant,
    )


def attend_backward_kernel(
    heads,
    block,
    grad_ref,
    x_ref,
    packed_ref,
    attended_ref,
    joint_ref,
    project_ref,
    joint_grad_ref,
    project_grad_ref,
    partial_ref,
    joint_sum,
    project_sum,
    key_sum,
    value_sum,
    low_ref,
):
    step = pl.program_id(0)
    length, width = attended_ref.shape
    size = width // heads
    scale = size ** (-0.5)
    grad = contract_cols(grad_ref[...], project_ref[...]).astype(BF16)
    key_sum[...] = jnp.zeros_like(key_sum)
    value_sum[...] = jnp.zeros_like(value_sum)
    for head in range(heads):
        at = head * size
        for begin in range(0, length, block):
            end = begin + block
            queries = packed_ref[begin:end, at : at + size]
            keys = packed_ref[:end, width + at : width + at + size]
            values = packed_ref[:end, 2 * width + at : 2 * width + at + size]
            here = grad[begin:end, at : at + size]
            probs = probabilities(queries, keys, begin)
            grad_probs = contract_cols(here, values)
            delta = jnp.sum(probs * grad_probs, axis=-1, keepdims=True)
            grad_scores = (probs * (grad_probs - delta)).astype(BF16)
            low_ref[begin:end, at : at + size] = (dot(grad_scores, keys) * scale).astype(BF16)
            key_sum[:end, at : at + size] += contract_rows(grad_scores, queries) * scale
            value_sum[:end, at : at + size] += contract_rows(probs.astype(BF16), here)
    low_ref[:, width : 2 * width] = key_sum[...].astype(BF16)
    low_ref[:, 2 * width :] = value_sum[...].astype(BF16)
    partial_ref[...] = contract_cols(low_ref[...], joint_ref[...]).astype(BF16)
    joint_part = contract_rows(x_ref[...], low_ref[...])
    project_part = contract_rows(attended_ref[...], grad_ref[...])

    @pl.when(step == 0)
    def _():
        joint_sum[...] = joint_part
        project_sum[...] = project_part

    @pl.when(step > 0)
    def _():
        joint_sum[...] += joint_part
        project_sum[...] += project_part

    @pl.when(step == pl.num_programs(0) - 1)
    def _():
        joint_grad_ref[...] = joint_sum[...].astype(BF16)
        project_grad_ref[...] = project_sum[...].astype(BF16)


def attend_backward(grad_out, normed, packed, attended, joint, project, seqs, heads):
    rows, width = normed.shape
    length, inner = rows // seqs, project.shape[0]
    outs = [
        jax.ShapeDtypeStruct(joint.shape, BF16),
        jax.ShapeDtypeStruct(project.shape, BF16),
        jax.ShapeDtypeStruct((rows, width), BF16),
    ]
    return local_call(
        functools.partial(attend_backward_kernel, heads, min(256, length)),
        outs,
        (grad_out, normed, packed, attended, joint, project),
        (seqs,),
        [
            stripe((length, width)),
            stripe((length, width)),
            stripe((length, 3 * inner)),
            stripe((length, inner)),
            whole(joint),
            whole(project),
        ],
        [whole(outs[0]), whole(outs[1]), stripe((length, width))],
        [
            VMEM(joint.shape, F32),
            VMEM(project.shape, F32),
            VMEM((length, inner), F32),
            VMEM((length, inner), F32),
            VMEM((length, 3 * inner), BF16),
        ],
        flops=16 * rows * width * inner,
    )


def forward_kernel(x_ref, expand_ref, shrink_ref, inner_ref, partial_ref):
    inner = dot(x_ref[...], expand_ref[...])
    inner_ref[...] = inner
    turn = jnp.tanh(GATE_SCALE * (inner + GATE_CUBE * (inner * inner * inner)))
    active = (0.5 * inner * (1.0 + turn)).astype(BF16)
    partial_ref[...] = dot(active, shrink_ref[...]).astype(BF16)


def forward(normed, expand, shrink):
    rows, width = normed.shape
    inner, block = expand.shape[1], 256
    outs = [jax.ShapeDtypeStruct((rows, inner), F32), jax.ShapeDtypeStruct((rows, width), BF16)]
    return local_call(
        forward_kernel,
        outs,
        (normed, expand, shrink),
        (rows // block,),
        [stripe((block, width)), whole(expand), whole(shrink)],
        [stripe((block, inner)), stripe((block, width))],
        flops=4 * rows * width * inner,
    )


def backward_kernel(
    branch_ref,
    x_ref,
    inner_ref,
    expand_ref,
    shrink_ref,
    expand_grad_ref,
    shrink_grad_ref,
    partial_ref,
    expand_sum,
    shrink_sum,
):
    step = pl.program_id(0)
    branch, inner = branch_ref[...], inner_ref[...]
    square = inner * inner
    turn = jnp.tanh(GATE_SCALE * (inner + GATE_CUBE * (square * inner)))
    active = (0.5 * inner * (1.0 + turn)).astype(BF16)
    slope = GATE_SCALE * (1.0 + (3.0 * GATE_CUBE) * square)
    slope = 0.5 * (1.0 + turn) + 0.5 * inner * (1.0 - turn * turn) * slope
    grad_inner = (contract_cols(branch, shrink_ref[...]) * slope).astype(BF16)
    partial_ref[...] = contract_cols(grad_inner, expand_ref[...]).astype(BF16)
    expand_part = contract_rows(x_ref[...], grad_inner)
    shrink_part = contract_rows(active, branch)

    @pl.when(step == 0)
    def _():
        expand_sum[...] = expand_part
        shrink_sum[...] = shrink_part

    @pl.when(step > 0)
    def _():
        expand_sum[...] += expand_part
        shrink_sum[...] += shrink_part

    @pl.when(step == pl.num_programs(0) - 1)
    def _():
        expand_grad_ref[...] = expand_sum[...].astype(BF16)
        shrink_grad_ref[...] = shrink_sum[...].astype(BF16)


def backward(branch, normed, inner, expand, shrink):
    rows, width = normed.shape
    block = 256
    outs = [
        jax.ShapeDtypeStruct(expand.shape, BF16),
        jax.ShapeDtypeStruct(shrink.shape, BF16),
        jax.ShapeDtypeStruct((rows, width), BF16),
    ]
    return local_call(
        backward_kernel,
        outs,
        (branch, normed, inner, expand, shrink),
        (rows // block,),
        [
            stripe((block, width)),
            stripe((block, width)),
            stripe((block, inner.shape[1])),
            whole(expand),
            whole(shrink),
        ],
        [whole(outs[0]), whole(outs[1]), stripe((block, width))],
        [VMEM(expand.shape, F32), VMEM(shrink.shape, F32)],
        flops=8 * rows * width * inner.shape[1],
    )


def ranks_of(flags):
    planes, groups, rows = flags.shape
    upto = jnp.arange(rows)[:, None] <= jnp.arange(rows)[None, :]
    inside = dot(flags.astype(BF16), upto.astype(BF16))
    before = jnp.where(
        jnp.arange(groups)[None, :, None] < jnp.arange(groups)[None, None, :],
        inside[:, :, -1:],
        0.0,
    )
    rank = inside + jnp.sum(before, axis=1)[:, :, None]
    return rank.reshape(planes, groups * rows), rank[:, -1, -1]


def pack_kernel(note_ref, rows_ref, out_ref, rank_ref):
    _, groups, size = note_ref.shape
    room, width = out_ref.shape[1:]
    marks = (note_ref[0] >= 0).astype(F32)
    upto = lax.broadcasted_iota(jnp.int32, (size, size), 0) <= lax.broadcasted_iota(
        jnp.int32, (size, size), 1
    )
    inside = dot(marks.astype(BF16), upto.astype(F32).astype(BF16))
    before = jnp.zeros((1, 1), F32)
    for n in range(groups):
        mine = inside[n : n + 1, :]
        rank_ref[0:1, n * size : (n + 1) * size] = jnp.where(
            marks[n : n + 1, :] > 0, mine + before, 0.0
        )
        before = before + mine[:, size - 1 : size]
    place = lax.broadcasted_iota(jnp.int32, (room, groups * size), 0) + 1
    chosen = (rank_ref[0:1, :].astype(jnp.int32) == place).astype(F32).astype(BF16)
    out_ref[0] = dot(chosen, rows_ref[...].reshape(groups * size, width)).astype(BF16)


def pack(notes, rows, room):
    planes, groups, size = notes.shape
    width = rows.shape[-1]
    outs = [jax.ShapeDtypeStruct((planes, room, width), BF16)]
    (packed,) = local_call(
        pack_kernel,
        outs,
        (notes, rows),
        (planes,),
        [
            stripe((1, groups, size)),
            pl.BlockSpec((groups, None, size, width), lambda i: (0, i, 0, 0)),
        ],
        [stripe((1, room, width))],
        [VMEM((8, groups * size), F32)],
        flops=2 * planes * room * groups * size * width,
        grant=61,
    )
    return packed


def pieces_of(values, terms):
    pieces = []
    for _ in range(terms):
        pieces.append(values.astype(BF16))
        values = values - pieces[-1].astype(F32)
    return jnp.concatenate(pieces, axis=0)


def recall_kernel(
    tile,
    hidden_ref,
    vector_ref,
    cotangent_ref,
    token_ref,
    stored_ref,
    mixed_ref,
    grad_ref,
    sums_ref,
    scaled_ref,
    pull_ref,
):
    rows, width = hidden_ref.shape
    tiles = stored_ref.shape[0] // tile
    unit, inverse = norm_parts(hidden_ref[...])
    gains = vector_ref[8:9, :]
    query = unit * gains + vector_ref[9:10, :]
    scale = DISTANCE_SCALE * math.sqrt(width)
    terms = jnp.concatenate([pieces_of(query, 3), cotangent_ref[...]], axis=0)
    ones = jnp.ones((8, width), BF16)

    def look(n, carry):
        at = pl.ds(pl.multiple_of(n * tile, tile), tile)
        stored = stored_ref[at, :]
        near = contract_cols(terms, stored)
        squares = jnp.square(stored.astype(F32))
        high = squares.astype(BF16)
        low = (squares - high.astype(F32)).astype(BF16)
        lengths = (contract_cols(ones, high) + contract_cols(ones, low))[0:1, :]
        scaled_ref[:, at] = (
            2.0 * (near[:rows] + (near[rows : 2 * rows] + near[2 * rows : 3 * rows])) - lengths
        ) / scale
        pull_ref[:, at] = RECALL_SHARE * near[3 * rows :]
        return carry

    lax.fori_loop(0, tiles, look, 0)
    usable = token_ref[...] == lax.broadcasted_iota(jnp.int32, scaled_ref.shape, 0)
    scaled = jnp.where(usable, scaled_ref[...], FLOOR)
    raised = jnp.where(usable, jnp.exp(scaled - jnp.max(scaled, axis=1, keepdims=True)), 0.0)
    weights = raised / jnp.sum(raised, axis=1, keepdims=True)
    pull = pull_ref[...]
    grad_scaled = weights * (pull - jnp.sum(weights * pull, axis=1, keepdims=True))
    scaled_ref[...] = weights
    pull_ref[...] = grad_scaled
    rest = jnp.sum(grad_scaled, axis=1, keepdims=True)

    def gather(n, total):
        at = pl.ds(pl.multiple_of(n * tile, tile), tile)
        both = jnp.concatenate(
            [pieces_of(scaled_ref[:, at], 2), pieces_of(pull_ref[:, at], 2)], axis=0
        )
        return total + dot(both, stored_ref[at, :])

    total = lax.fori_loop(0, tiles, gather, jnp.zeros((4 * rows, width), F32))
    recalled = total[:rows] + total[rows : 2 * rows]
    moved = total[2 * rows : 3 * rows] + total[3 * rows :] - rest * query
    mixed_ref[...] = (1.0 - RECALL_SHARE) * query + RECALL_SHARE * recalled
    grad_query = (1.0 - RECALL_SHARE) * cotangent_ref[...].astype(F32) + moved * (2.0 / scale)
    sums_ref[0:1, :] = jnp.sum(grad_query * unit, axis=0, keepdims=True)
    sums_ref[1:2, :] = jnp.sum(grad_query, axis=0, keepdims=True)
    grad_ref[...] = norm_backward(grad_query, unit, inverse, gains)


def recall_padded(hidden, vectors, stored, usable, cotangent):
    unit, inverse = norm_parts(hidden)
    query = unit * vectors[8] + vectors[9]
    scale = DISTANCE_SCALE * math.sqrt(query.shape[-1])
    stored, cotangent = stored.astype(F32), cotangent.astype(F32)
    distance = jnp.sum(jnp.square(query[None] - stored), axis=-1)
    pull = RECALL_SHARE * jnp.sum(cotangent[None] * stored, axis=-1)
    scaled = jnp.where(usable, -distance / scale, FLOOR)
    raised = jnp.where(usable, jnp.exp(scaled - jnp.max(scaled, axis=0, keepdims=True)), 0.0)
    weights = raised / jnp.sum(raised, axis=0, keepdims=True)
    grad_scaled = weights * (pull - jnp.sum(weights * pull, axis=0, keepdims=True))
    recalled = jnp.sum(weights[..., None] * stored, axis=0)
    moved = jnp.sum(grad_scaled[..., None] * stored, axis=0)
    moved = moved - jnp.sum(grad_scaled, axis=0)[:, None] * query
    mixed = (1.0 - RECALL_SHARE) * query + RECALL_SHARE * recalled
    grad_query = (1.0 - RECALL_SHARE) * cotangent + moved * (2.0 / scale)
    sums = jnp.stack([jnp.sum(grad_query * unit, axis=0), jnp.sum(grad_query, axis=0)])
    grad = norm_backward(grad_query, unit, inverse, vectors[8])
    return mixed, grad, jnp.pad(sums, ((0, 6), (0, 0)))


def recall(hidden, vectors, stored, token_of, cotangent):
    rows, width = hidden.shape
    entries = stored.shape[0]
    operands = (hidden, vectors, cotangent, token_of.reshape(1, entries), stored)
    outs = [
        jax.ShapeDtypeStruct((rows, width), F32),
        jax.ShapeDtypeStruct((rows, width), F32),
        jax.ShapeDtypeStruct((8, width), F32),
    ]
    return local_call(
        functools.partial(recall_kernel, min(512, entries)),
        outs,
        operands,
        (1,),
        [whole(x) for x in operands],
        [whole(x) for x in outs],
        [VMEM((rows, entries), F32), VMEM((rows, entries), F32)],
        flops=16 * rows * width * entries,
    )


def shards(
    tokens,
    ln1_gain,
    ln1_bias,
    qkv_weight,
    out_weight,
    ln2_gain,
    ln2_bias,
    in_weight,
    fc_weight,
    final_gain,
    final_bias,
    datastore,
    neighbour_owner,
    neighbour_row,
    neighbour_count,
    cotangent,
):
    local_seqs, local_rows, width = tokens.shape
    rows = local_seqs * local_rows
    count, ring = lax.axis_size("dp"), lax.axis_size("ctx")
    devices = count * ring
    both = ("dp", "ctx")
    seqs = count * local_seqs // ring
    heads = HEADS // count
    slots = neighbour_owner.shape[2]
    part = width // devices
    head_width = width // count
    inner_width = in_weight.shape[2] // count

    forth = []
    for s in range(count):
        for p in range(ring):
            forth.append((s * ring + p, ((s // ring) * ring + p) * ring + s % ring))

    pair_room = -(-(3 * rows * slots) // (2 * devices * 16)) * 16
    room = rows * slots // ring
    owners = neighbour_owner.reshape(rows, slots)
    live = neighbour_count.reshape(rows, 1)
    hits = (owners[:, :, None] == jnp.arange(devices)[None, None, :]) & (
        jnp.arange(slots)[None, :, None] < live[:, :, None]
    )
    asked_all = jnp.sum(jnp.where(hits, neighbour_row.reshape(rows, slots, 1), 0), axis=1).T
    usable_all = jnp.any(hits, axis=1).T
    upto = jnp.arange(rows)[:, None] <= jnp.arange(rows)[None, :]
    order = dot(usable_all.astype(BF16), upto.astype(BF16))
    taken = usable_all[:, None, :] & (
        order[:, None, :] == jnp.arange(1, pair_room + 1, dtype=F32)[None, :, None]
    )
    asked = jnp.sum(jnp.where(taken, asked_all[:, None, :], 0), axis=-1)
    asked = asked.reshape(count, ring, 1, pair_room)
    asked = jnp.pad(asked, ((0, 0), (0, 0), (0, 7), (0, 128 - pair_room)))

    def by_plane(x):
        return x.reshape((count, ring) + x.shape[1:]).swapaxes(0, 1)

    token_at = by_plane(jnp.sum(jnp.where(taken, jnp.arange(rows)[None, None, :], 0), axis=-1))
    amounts = order[:, -1]
    usable = by_plane(jnp.arange(pair_room, dtype=F32)[None, :] < amounts[:, None])
    crowded = (jnp.max(amounts) > pair_room) | (jnp.max(jnp.sum(by_plane(amounts), axis=1)) > room)

    joint_own, expand_own = qkv_weight, in_weight
    if head_width % 128:
        joint_own = qkv_weight.reshape(LAYERS, part, 3, count, head_width).transpose(3, 0, 1, 2, 4)
        joint_own = joint_own.reshape(count, LAYERS, part, 3 * head_width)
        expand_own = in_weight.reshape(LAYERS, part, count, inner_width).transpose(2, 0, 1, 3)

    notes = jnp.where(usable, token_at, -1)
    last_all = lax.all_gather(fc_weight[1], "ctx", axis=0, tiled=False)
    exchange = functools.partial(plane_exchange, count, ring)
    first = first_exchange(
        count,
        ring,
        0,
        tokens.reshape(rows, width),
        asked,
        notes,
        crowded.astype(F32).reshape(1, 1),
        (
            ln1_gain,
            ln1_bias,
            ln2_gain,
            ln2_bias,
            final_gain.reshape(1, part),
            final_bias.reshape(1, part),
        ),
        datastore,
        joint_own,
        expand_own,
        (out_weight, fc_weight),
        ((0, 0), (1, 0), (0, 1)),
    )
    normed, vectors, served, notes, asked_notes, my_tokens = first[:6]
    joint, expand = list(first[6 : 6 + LAYERS]), list(first[6 + LAYERS : 6 + 2 * LAYERS])
    project, shrink = [first[-3], first[-1]], [first[-2], None]
    gain_one, shift_one = vectors[:LAYERS], vectors[LAYERS : 2 * LAYERS]
    gain_two, shift_two = vectors[2 * LAYERS : 3 * LAYERS], vectors[3 * LAYERS : 4 * LAYERS]
    crowded = jnp.max(vectors[4 * LAYERS + 2]) > 0.5
    stored = pack(asked_notes, served.reshape(count, ring, pair_room, width), room)
    stored = lax.all_to_all(stored, "ctx", split_axis=0, concat_axis=0, tiled=True)

    hidden = my_tokens.astype(F32)
    saved = []
    for layer in range(LAYERS):
        normed = normed.reshape(count * rows, width)
        joint[layer] = joint[layer].reshape(width, 3 * head_width)
        project[layer] = project[layer].reshape(-1, width)
        packed, attended, partial = attend(
            normed, joint[layer], project[layer], seqs, heads, 61 if layer == 0 else 32
        )
        partial = partial.reshape(count, rows, width)
        normed_two, middle = exchange(2, partial, hidden, gain_two[layer], shift_two[layer])
        if layer + 1 == LAYERS:
            shrink[layer], middle = after(last_all, middle)
        normed_two = normed_two.reshape(count * rows, width)
        expand[layer] = expand[layer].reshape(width, inner_width)
        shrink[layer] = shrink[layer].reshape(-1, width)
        inner, partial = forward(normed_two, expand[layer], shrink[layer])
        partial = partial.reshape(count, rows, width)
        saved.append((hidden, normed, packed, attended, middle, normed_two, inner))
        if layer + 1 < LAYERS:
            normed, hidden = exchange(
                2, partial, middle, gain_one[layer + 1], shift_one[layer + 1]
            )
        else:
            hidden, my_cotangent = exchange(
                5, partial, middle, gather=False, swaps=(cotangent.reshape(rows, width),)
            )

    def few():
        rank, _ = ranks_of(notes >= 0)
        chosen = (notes.reshape(ring, 1, -1) >= 0) & (
            rank[:, None, :] == jnp.arange(1, room + 1, dtype=F32)[None, :, None]
        )
        token_of = jnp.sum(jnp.where(chosen, notes.reshape(ring, 1, -1) + 1, 0), axis=-1) - 1
        entries = stored.reshape(ring * room, width)
        return recall(hidden, vectors, entries, token_of.reshape(-1), my_cotangent)

    def many():
        asked = lax.all_to_all(asked_all, both, split_axis=0, concat_axis=0, tiled=True)
        padded = datastore.at[asked.reshape(-1)].get(mode="promise_in_bounds")
        padded = padded.reshape(devices, rows, width)
        padded = lax.all_to_all(padded, both, split_axis=0, concat_axis=0, tiled=True)
        padded = lax.ppermute(padded, both, forth)
        marks = lax.ppermute(usable_all.astype(jnp.int32), both, forth)
        return recall_padded(hidden, vectors, padded, marks > 0, my_cotangent)

    mixed, grad_hidden, head_sums = lax.cond(crowded, many, few)
    branch, mixed = exchange(6, base=grad_hidden, swaps=(mixed.astype(BF16),))
    sums_one, sums_two = [None] * LAYERS, [None] * LAYERS
    joint_sums, expand_sums = [None] * LAYERS, [None] * LAYERS
    grad_tall = [None] * LAYERS
    for layer in reversed(range(LAYERS)):
        start, normed, packed, attended, middle, normed_two, inner = saved[layer]
        grad_expand, grad_shrink, partial = backward(
            branch.reshape(count * rows, width), normed_two, inner, expand[layer], shrink[layer]
        )
        grad_expand = grad_expand.reshape(count, ring, part, inner_width)
        grad_shrink = grad_shrink.reshape(ring, -1, width)
        cut = grad_shrink.shape[1] // 2
        grad_out, grad_middle, sums_two[layer], upper_sum, expand_sum = exchange(
            7,
            partial.reshape(count, rows, width),
            grad_hidden,
            gain_two[layer],
            saved=middle,
            sums=(grad_shrink[:, :cut], grad_expand),
        )
        expand_sums[layer] = expand_sum
        grad_joint, grad_project, partial = attend_backward(
            grad_out.reshape(count * rows, width),
            normed,
            packed,
            attended,
            joint[layer],
            project[layer],
            seqs,
            heads,
        )
        rides = (
            grad_project.reshape(ring, part, width),
            grad_shrink[:, cut:],
            grad_joint.reshape(count, ring, part, 3 * head_width),
        )
        partial = partial.reshape(count, rows, width)
        if layer > 0:
            branch, grad_hidden, sums_one[layer], project_sum, lower_sum, joint_sum = exchange(
                8, partial, grad_middle, gain_one[layer], saved=start, sums=rides
            )
        else:
            grad_hidden, sums_one[layer], project_sum, lower_sum, joint_sum, *mixes = exchange(
                9,
                partial,
                grad_middle,
                gain_one[layer],
                saved=start,
                gather=False,
                sums=rides,
                mixes=tuple(joint_sums[1:]) + tuple(expand_sums),
            )
        shrink_sum = jnp.concatenate([upper_sum, lower_sum], axis=0)
        joint_sums[layer] = joint_sum
        grad_tall[layer] = (project_sum, shrink_sum)

    sums = jnp.concatenate(
        [one[n : n + 1] for every in (sums_one, sums_two) for n in (0, 1) for one in every]
        + [head_sums[:2]]
    )
    sums = jnp.pad(sums, ((0, 6), (0, 0))).reshape(16, count, head_width).transpose(1, 0, 2)
    sums, qkv_grad, in_grad, tokens_grad = last_exchange(
        count,
        ring,
        10,
        sums,
        joint_sums[0],
        grad_hidden.astype(BF16),
        mixes[: LAYERS - 1],
        mixes[LAYERS - 1 :],
    )
    sums = lax.dynamic_slice_in_dim(sums, lax.axis_index("ctx") * part, part, axis=1)

    return (
        mixed.astype(F32).reshape(local_seqs, local_rows, width),
        tokens_grad.reshape(local_seqs, local_rows, width),
        sums[0:LAYERS],
        sums[LAYERS : 2 * LAYERS],
        qkv_grad,
        jnp.stack([pair[0] for pair in grad_tall]),
        sums[2 * LAYERS : 3 * LAYERS],
        sums[3 * LAYERS : 4 * LAYERS],
        in_grad,
        jnp.stack([pair[1] for pair in grad_tall]),
        sums[4 * LAYERS],
        sums[4 * LAYERS + 1],
    )


def solution(mesh):
    both = ("dp", "ctx")
    return jax.shard_map(
        shards,
        mesh=mesh,
        in_specs=(
            P("dp", "ctx", None),
            P(None, both),
            P(None, both),
            P(None, both, None),
            P(None, both, None),
            P(None, both),
            P(None, both),
            P(None, both, None),
            P(None, both, None),
            P(both),
            P(both),
            P(both, None),
            P("dp", "ctx", None),
            P("dp", "ctx", None),
            P("dp", "ctx"),
            P("dp", "ctx", None),
        ),
        out_specs=(
            P("dp", "ctx", None),
            P("dp", "ctx", None),
            P(None, both),
            P(None, both),
            P(None, both, None),
            P(None, both, None),
            P(None, both),
            P(None, both),
            P(None, both, None),
            P(None, both, None),
            P(both),
            P(both),
        ),
        check_vma=False,
    )
```
